128 devices in a mesh: row: 16 (over y, x_hi, core), col: 8 (over z, x_lo).
Axes of the slice: x: 4 (x_hi: 2, x_lo: 2; x = x_hi * 2 + x_lo), y: 4, z: 4, core: 2. Of those that a mesh axis runs over, the one named last changes fastest.
Arguments:
- estimate: bfloat16 [2, 2048, 2048], P(None, 'row', 'col'), may hold values from -6 to 6
- dirty_image: bfloat16 [2, 2048, 2048], P(None, 'row', 'col'), may hold values from -6 to 6
- psf_spectra: float32 [3, 2048, 16, 128], P(None, ('row', 'col')), may hold values from -1 to 1
- w_first: bfloat16 [32, 4, 3, 3], replicated, may hold values from -1 to 1
- b_first: float32 [32], replicated, may hold values from -1 to 1
- w_second: bfloat16 [2, 32, 3, 3], replicated, may hold values from -0.375 to 0.375
- cotangent: bfloat16 [2, 2048, 2048], P(None, 'row', 'col'), may hold values from -36 to 36
Outputs:
- grad_image: float32 [2, 2048, 2048], P(None, 'row', 'col')
- grad_first: float32 [32, 4, 3, 3], replicated
- grad_first_bias: float32 [32], replicated
- grad_second: float32 [2, 32, 3, 3], replicated
- grad_second_bias: float32 [2], replicated
The draws below stay inside these ranges and needn't reach their ends.
All inputs are finite; a program needn't handle non-finite values.
Results may differ from the reference program's by a relative error of at most 0.01.
Values may be sent and summed in bfloat16 or wider, within the bound.
No kernel may reach another device: no remote copies, remote signals or barrier semaphores. Data moves between devices by JAX's collectives and lax.ppermute only.
A program may use at most 192 MiB of HBM per device.

```python
import jax
import jax.numpy as jnp
from jax import lax

IMAGE = 2048
TERMS = 2
CHANNELS = 32
LOW = 16
N_ROW = 16
N_COL = 8


def draw_cotangent(key, part):
    key = jax.random.fold_in(key, 11)
    ramp = jnp.arange(IMAGE, dtype=jnp.float32) / IMAGE
    growth = jnp.exp(jnp.log(3.0) * (ramp[:, None] + ramp[None, :]))
    base_values = jax.random.truncated_normal(key, -4.0, 4.0, (TERMS, IMAGE, IMAGE), jnp.float32)
    return (base_values * growth).astype(jnp.bfloat16)


def block_levels(stream_key, shape, pieces, least, largest):
    def one(position, shards_of):
        heights = jax.random.uniform(jax.random.fold_in(jax.random.fold_in(stream_key, 6), position), (shards_of,), jnp.float32, least / len(pieces), largest / len(pieces))
        return jnp.repeat(jnp.exp(heights), shape[position] // shards_of).reshape((-1,) + (1,) * (len(shape) - position - 1))

    gain = one(*pieces[0])
    for cut in pieces[1:]:
        gain = gain * one(*cut)
    return gain


def noise(rng, extent, scale, limit, cuts=(), held_as=jnp.bfloat16):
    drawn = scale * jax.random.normal(rng, extent, jnp.float32)
    if cuts:
        drawn = drawn * block_levels(rng, extent, cuts, -0.22, 0.18)
    return jnp.clip(drawn, -limit, limit).astype(held_as)


def setup_inputs(seed: int = 0) -> dict:
    key_of = jax.random.split(jax.random.key(seed), 8)
    return {
        "estimate": noise(key_of[0], (TERMS, IMAGE, IMAGE), 1.0, 6.0, ((1, 16), (2, 8))),
        "dirty_image": noise(key_of[1], (TERMS, IMAGE, IMAGE), 1.0, 6.0, ((1, 16), (2, 8))),
        "psf_spectra": jnp.clip(jax.random.uniform(key_of[2], (2 * TERMS - 1, IMAGE, LOW, N_ROW * N_COL), jnp.float32, -1.0, 1.0) * block_levels(key_of[2], (2 * TERMS - 1, IMAGE, LOW, N_ROW * N_COL), ((1, 128),), -0.4, 0.0), -1.0, 1.0),
        "w_first": noise(key_of[3], (CHANNELS, 2 * TERMS, 3, 3), (18 * TERMS) ** -0.5, 1.0),
        "b_first": jnp.clip(jax.random.uniform(key_of[4], (CHANNELS,), jnp.float32, -1.0, 1.0), -1.0, 1.0),
        "w_second": noise(key_of[5], (TERMS, CHANNELS, 3, 3), (9 * CHANNELS) ** -0.5, 0.375),
        "cotangent": draw_cotangent(jax.random.fold_in(key_of[7], 71), 0),
    }


def rounded(values):
    return lax.optimization_barrier(values.astype(jnp.bfloat16)).astype(jnp.float32)

def blur(tile_data, spectra):
    columns = jnp.fft.fft(tile_data.astype(jnp.float32), axis=2)
    columns = rounded(jnp.real(columns)) + 1j * rounded(jnp.imag(columns))
    spectrum = jnp.fft.fft(columns, axis=1)
    term_count = tile_data.shape[0]
    mixed = []
    for target in range(term_count):
        total = spectra[target] * spectrum[0]
        for source in range(1, term_count):
            total = total + spectra[target + source] * spectrum[source]
        mixed.append(total)
    back_rows = jnp.fft.ifft(jnp.stack(mixed), axis=1)
    back_rows = rounded(jnp.real(back_rows)) + 1j * rounded(jnp.imag(back_rows))
    return jnp.real(jnp.fft.ifft(back_rows, axis=2)).astype(jnp.bfloat16)

def conv_valid(inputs, kernel):
    return lax.conv_general_dilated(inputs[None].astype(jnp.float32), kernel.astype(jnp.float32), (1, 1), 'VALID', dimension_numbers=('NCHW', 'OIHW', 'NCHW'))[0]

def kernel_grad(inputs, cot_part):
    return lax.conv_general_dilated(inputs[:, None].astype(jnp.float32), cot_part[:, None].astype(jnp.float32), (1, 1), 'VALID', dimension_numbers=('NCHW', 'OIHW', 'NCHW'))

def activation_slope(preact):
    gate_value = jax.nn.sigmoid(preact)
    return gate_value * (1.0 + preact * (1.0 - gate_value))

def network(features, cotangent, w_first, b_first, w_second):
    channels = features.shape[0]
    size_rows = features.shape[1]
    hidden_count = w_first.shape[0]
    term_count = cotangent.shape[0]
    padded = jnp.pad(jnp.concatenate([features, cotangent], 0), ((0, 0), (2, 2), (2, 2)))
    flip_first = jnp.flip(w_first, (2, 3)).transpose(1, 0, 2, 3)
    flip_second = jnp.flip(w_second, (2, 3)).transpose(1, 0, 2, 3)
    band_rows = min(512, size_rows)
    band_count = size_rows // band_rows
    col_pos = jnp.arange(size_rows + 2, dtype=jnp.int32) - 1
    col_inside = (col_pos >= 0) & (col_pos < size_rows)

    def band_pass(band_index, state_pair):
        totals, result = state_pair
        offset = (band_index * band_rows).astype(jnp.int32)
        window_rows = lax.dynamic_slice_in_dim(padded, offset, band_rows + 4, 1)
        preact = conv_valid(window_rows[:channels], w_first) + b_first[:, None, None]
        row_pos = offset - 1 + jnp.arange(band_rows + 2, dtype=jnp.int32)
        inside = ((row_pos >= 0) & (row_pos < size_rows))[:, None] & col_inside[None, :]
        grad_pre = jnp.where(inside, conv_valid(window_rows[channels:], flip_second) * activation_slope(preact), 0.0).astype(jnp.bfloat16)
        result = lax.dynamic_update_slice_in_dim(result, conv_valid(grad_pre, flip_first), offset, 1)
        inner_pre = preact[:, 1:-1, 1:-1]
        inner_grad = grad_pre[:, 1:-1, 1:-1]
        hidden = jax.nn.silu(inner_pre).astype(jnp.bfloat16)
        totals = (totals[0] + kernel_grad(window_rows[:channels, 1:-1, 1:-1], inner_grad).transpose(1, 0, 2, 3), totals[1] + lax.optimization_barrier(jnp.sum(inner_grad.astype(jnp.float32), axis=(1, 2))), totals[2] + jnp.flip(kernel_grad(window_rows[channels:, 1:-1, 1:-1], hidden), (2, 3)))
        return (totals, result)
    start_totals = (jnp.zeros((hidden_count, channels, 3, 3), jnp.float32), jnp.zeros((hidden_count,), jnp.float32), jnp.zeros((term_count, hidden_count, 3, 3), jnp.float32))
    start_grad = jnp.zeros((channels, size_rows, size_rows), jnp.float32)
    totals, feature_grad = lax.fori_loop(0, band_count, band_pass, (start_totals, start_grad))
    return (feature_grad, totals)

def reference(estimate, dirty_image, psf_spectra, w_first, b_first, w_second, cotangent):
    spectra = psf_spectra.transpose(0, 3, 2, 1).reshape(2 * TERMS - 1, IMAGE, IMAGE)
    model_blur = blur(estimate, spectra)
    residual = (dirty_image.astype(jnp.float32) - model_blur.astype(jnp.float32)).astype(jnp.bfloat16)
    features = jnp.concatenate([estimate, residual], 0)
    feature_grad, totals = network(features, cotangent, w_first, b_first, w_second)
    residual_grad = feature_grad[TERMS:].astype(jnp.bfloat16)
    blurred_grad = blur(residual_grad, spectra)
    grad_image = cotangent.astype(jnp.float32) + feature_grad[:TERMS] - blurred_grad.astype(jnp.float32)
    scaling = 1.0 / IMAGE
    cot_sum = lax.optimization_barrier(jnp.sum(cotangent.astype(jnp.float32), axis=(1, 2)))
    return (grad_image, totals[0] * scaling, totals[1] * scaling, totals[2] * scaling, cot_sum * scaling)
```

```python
import functools

import jax
import jax.numpy as jnp
import numpy as np
from jax import lax
from jax.experimental import pallas as pl
from jax.experimental.pallas import tpu as pltpu
from jax.sharding import PartitionSpec as P

IMAGE = 2048
DEVS = 128
STRIP = 16
REACH = 20
HOLD = 24
GRAD_ROWS = 18
HIDDEN = 32
RC = ("row", "col")
F32 = jnp.float32
BF16 = jnp.bfloat16
NT = (((1,), (1,)), ((), ()))
TN = (((0,), (0,)), ((), ()))


def turn(product, period):
    angle = 2.0 * np.pi * (product % period) / period
    return np.cos(angle), np.sin(angle)


def bf16_table(values):
    return np.asarray(values, np.float32).astype(jnp.bfloat16)


@functools.lru_cache(None)
def column_twiddle():
    cos, sin = turn(np.arange(8)[:, None] * np.arange(256)[None, :], 2048)
    return np.concatenate([cos, sin]).astype(np.float32)


@functools.lru_cache(None)
def column_forward_table(per):
    freq = 2 * np.arange(128)[:, None] + np.arange(2)[None, :]
    cos, sin = turn(freq[:, :, None] * np.arange(256), 256)
    table = np.zeros((128, 2, 2, 2, 2, 2, 256))
    for jhi in range(2):
        table[:, 0, :, jhi, jhi, 0] = cos
        table[:, 0, :, jhi, jhi, 1] = sin
        table[:, 1, :, jhi, jhi, 0] = -sin
        table[:, 1, :, jhi, jhi, 1] = cos
    full = np.zeros((128, per, 1024))
    full[:, :8] = table.reshape(128, 8, 1024)
    return bf16_table(full.reshape(128 * per, 1024))


@functools.lru_cache(None)
def column_inverse_table(per):
    freq = 2 * np.arange(128)[:, None] + np.arange(2)[None, :]
    cos, sin = turn(freq[:, :, None] * np.arange(256), 256)
    table = np.zeros((128, 2, 2, 2, 2, 2, 256))
    for jhi in range(2):
        table[:, 0, :, jhi, 0, jhi] = cos
        table[:, 1, :, jhi, 0, jhi] = -sin
        table[:, 0, :, jhi, 1, jhi] = sin
        table[:, 1, :, jhi, 1, jhi] = cos
    full = np.zeros((128, per, 1024))
    full[:, :8] = table.reshape(128, 8, 1024)
    return bf16_table(full.reshape(128 * per, 1024))


@functools.lru_cache(None)
def row_block_tables(per):
    cos, sin = turn(np.arange(16)[:, None] * np.arange(16), 16)
    ahead = np.zeros((2, 4, 8, 16, 16, 8, 2, 4))
    for kj in range(4):
        for c in range(8):
            ahead[0, kj, c, :, :, c, 0, kj] = cos
            ahead[0, kj, c, :, :, c, 1, kj] = sin
            ahead[1, kj, c, :, :, c, 0, kj] = -sin
            ahead[1, kj, c, :, :, c, 1, kj] = cos
    back = np.conj(ahead).transpose(4, 5, 6, 7, 0, 1, 2, 3).reshape(128, 8, 1024)
    full_ahead = np.zeros((1024, 128, per))
    full_ahead[:, :, :8] = ahead.reshape(1024, 128, 8)
    full_back = np.zeros((128, per, 1024))
    full_back[:, :8] = back
    return (
        bf16_table(full_ahead.reshape(1024, 128 * per)),
        bf16_table(full_back.reshape(128 * per, 1024) / IMAGE),
    )


@functools.lru_cache(None)
def row_forward_tables():
    pos = np.arange(128)
    cos, sin = turn(np.arange(16)[:, None] * pos, 2048)
    twiddle = np.concatenate([cos, sin]).astype(np.float32)
    cos, sin = turn(pos[:, None] * np.arange(128), 128)
    return twiddle, bf16_table(np.concatenate([cos, sin], 1))


@functools.lru_cache(None)
def row_inverse_tables(window, lead):
    pos = (16 * np.arange(8)[:, None] + np.arange(window)[None, :] - lead).reshape(-1)
    cos, sin = turn(np.arange(16)[:, None] * pos, 2048)
    twiddle = np.concatenate([cos, sin]).astype(np.float32)
    cos, sin = turn(np.arange(128)[:, None] * pos, 128)
    return twiddle, bf16_table(np.concatenate([cos, sin], 1))


@functools.lru_cache(None)
def sum_tables():
    spread = np.zeros((128, 10, 64))
    share = np.zeros((128, 10, 32))
    gather = np.zeros((16, 128, 10))
    collect = np.zeros((32, 128, 10))
    for d in range(128):
        spread[d, 8, d % 32] = 1.0
        spread[d, 9, 32 + d % 32] = 1.0
    share[:, 8, 0] = 1.0
    share[:, 9, 16] = 1.0
    gather[:, :, 8:] = 1.0
    for c in range(32):
        collect[c, c, 8:] = 1.0
    return (
        bf16_table(spread.reshape(1280, 64)),
        bf16_table(gather.reshape(16, 1280)),
        bf16_table(share.reshape(1280, 32)),
        bf16_table(collect.reshape(32, 1280)),
    )


@functools.lru_cache(None)
def weight_tables():
    first = np.zeros((3, 36, 256))
    second = np.zeros((2, 3, 9, 128))
    back = np.zeros((3, 36, 192))
    rows = np.full((8, 256), 99)
    for i in range(4):
        for q in range(3):
            at = 128 * (i // 2) + 20 * (3 * (i % 2) + q)
            rows[:, at : at + 20] = np.arange(20)
            for p in range(3):
                first[p, i * 9 + p * 3 + q, at : at + 20] = 1.0
                back[p, i * 9 + p * 3 + q, q * 64 + i * 16 : q * 64 + i * 16 + 16] = 1.0
    rows[:, 120] = -1
    for o in range(2):
        for q in range(3):
            at = 20 * (3 * o + q)
            for e in range(3):
                second[o, e, (2 - e) * 3 + 2 - q, at : at + 20] = 1.0
    fold = np.zeros((3, 384, 128), np.float32)
    for p in range(3):
        for i in range(4):
            for q in range(3):
                at = 128 * (i // 2) + 20 * (3 * (i % 2) + q)
                fold[p, at : at + 20, p * 12 + i * 3 + q] = 1.0
        for o in range(2):
            for q in range(3):
                at = 256 + 20 * (3 * o + q)
                fold[p, at : at + 20, 36 + p * 6 + o * 3 + q] = 1.0
    fold[0, 120, 54] = 1.0
    return (
        bf16_table(first),
        bf16_table(second),
        bf16_table(back),
        rows.astype(np.int32),
        fold,
    )


def columns_ahead(z, twiddle_ref):
    root = float(np.sqrt(0.5))
    s04, d04 = z[0] + z[4], z[0] - z[4]
    s26, d26 = z[2] + z[6], z[2] - z[6]
    s15, d15 = z[1] + z[5], z[1] - z[5]
    s37, d37 = z[3] + z[7], z[3] - z[7]
    low, high = root * (d15 - d37), root * (d15 + d37)
    real = [None] * 8
    imag = [None] * 8
    even, odd = s04 + s26, s15 + s37
    real[0], real[4] = even + odd, even - odd
    real[2], imag[2] = s04 - s26, s37 - s15
    real[1], imag[1] = d04 + low, -d26 - high
    real[3], imag[3] = d04 - low, d26 - high
    for j in (1, 2, 3):
        real[8 - j], imag[8 - j] = real[j], -imag[j]
    groups = []
    for jlo in range(4):
        pieces = []
        for jhi in range(2):
            j = 4 * jhi + jlo
            cos, sin = twiddle_ref[j : j + 1, :], twiddle_ref[8 + j : 9 + j, :]
            if imag[j] is None:
                pieces += [real[j] * cos, -real[j] * sin]
            else:
                pieces += [real[j] * cos + imag[j] * sin, imag[j] * cos - real[j] * sin]
        groups.append(jnp.concatenate(pieces, axis=1).astype(BF16))
    return jnp.concatenate(groups, axis=0)


def columns_back(rows_of, twiddle_ref):
    real = [None] * 8
    imag = [None] * 8
    for jlo in range(4):
        rows = rows_of(jlo)
        for jhi in range(2):
            j = 4 * jhi + jlo
            re = rows[:, jhi * 256 : jhi * 256 + 256]
            im = rows[:, 512 + jhi * 256 : 768 + jhi * 256]
            cos, sin = twiddle_ref[j : j + 1, :], twiddle_ref[8 + j : 9 + j, :]
            real[j] = re * cos - im * sin
            imag[j] = re * sin + im * cos
    fold_re = [real[0]] + [real[j] + real[8 - j] for j in (1, 2, 3)] + [real[4]]
    fold_im = [None] + [imag[j] - imag[8 - j] for j in (1, 2, 3)]
    scale = 1.0 / IMAGE
    root = float(np.sqrt(0.5)) * scale
    base_even = (fold_re[0] + fold_re[4]) * scale
    base_odd = (fold_re[0] - fold_re[4]) * scale
    re2, im2 = fold_re[2] * scale, fold_im[2] * scale
    sum_re, dif_re = fold_re[1] + fold_re[3], fold_re[1] - fold_re[3]
    sum_im, dif_im = fold_im[1] + fold_im[3], fold_im[1] - fold_im[3]
    cross = root * (dif_re - sum_im), root * (dif_re + sum_im)
    return [
        base_even + re2 + sum_re * scale,
        base_odd - im2 + cross[0],
        base_even - re2 - dif_im * scale,
        base_odd + im2 - cross[1],
        base_even + re2 - sum_re * scale,
        base_odd - im2 - cross[0],
        base_even - re2 + dif_im * scale,
        base_odd + im2 + cross[1],
    ]


def swap_blocks(arrays, size):
    arrays = list(arrays)
    count = 128 // size
    lane = lax.broadcasted_iota(jnp.int32, arrays[0].shape, 1)
    step = count // 2
    while step:
        low = (lane & (step * size)) == 0
        for i in range(count):
            if not i & step:
                one, two = arrays[i], arrays[i + step]
                arrays[i] = jnp.where(low, one, pltpu.roll(two, step * size, 1))
                arrays[i + step] = jnp.where(low, pltpu.roll(one, 128 - step * size, 1), two)
        step //= 2
    return arrays


def halves(values):
    high = values.astype(BF16)
    return high, (values - high.astype(F32)).astype(BF16)


def ahead_body(strip_ref, twiddle_ref, table_ref, out_ref):
    z = [strip_ref[c, 0:2].astype(F32).reshape(32, 256) for c in range(8)]
    values = columns_ahead(z, twiddle_ref)
    out_ref[...] = lax.dot_general(
        table_ref[...], values, NT, preferred_element_type=F32
    ).astype(BF16)


def middle_body(window, summing, *refs):
    in_ref, spectra_ref, ahead_ref, back_ref, row_ref, back_row_ref, tw_ref, back_tw_ref = refs[:8]
    out_ref = refs[-1]
    chunks = in_ref[...]
    first = jnp.dot(ahead_ref[...], chunks, preferred_element_type=F32).reshape(8, 8, 16, 128)
    per_m = swap_blocks([first[:, c].reshape(128, 128) for c in range(8)], 16)
    cos, sin = tw_ref[0:16, :], tw_ref[16:32, :]
    rows = []
    for m in range(8):
        real = per_m[m][:64].reshape(4, 16, 128)
        imag = per_m[m][64:].reshape(4, 16, 128)
        rows.append((real * cos + imag * sin).astype(BF16).reshape(64, 128))
        rows.append((imag * cos - real * sin).astype(BF16).reshape(64, 128))
    second = jnp.dot(jnp.concatenate(rows, 0), row_ref[...], preferred_element_type=F32)
    rows = []
    for jlo in range(4):
        full_re, full_im = [], []
        for plane in range(2):
            m = 2 * jlo + plane
            part = second[128 * m : 128 * m + 128]
            full_re.append(part[:64, :128] + part[64:, 128:])
            full_im.append(part[64:, :128] - part[:64, 128:])
        weights = [
            spectra_ref[t].reshape(4, 4, 16, 128)[:, jlo].reshape(64, 128) for t in range(3)
        ]
        for plane in range(2):
            for part in (full_re, full_im):
                mixed = weights[plane] * part[0] + weights[plane + 1] * part[1]
                rows.append(mixed.astype(BF16))
    third = jnp.dot(jnp.concatenate(rows, 0), back_row_ref[...], preferred_element_type=F32)
    half = 8 * window
    cos, sin = back_tw_ref[0:16, :], back_tw_ref[16:32, :]
    per_m = []
    for m in range(8):
        part = third[128 * m : 128 * m + 128]
        real = (part[:64, :half] - part[64:, half:]).reshape(4, 16, half)
        imag = (part[64:, :half] + part[:64, half:]).reshape(4, 16, half)
        per_m.append(
            jnp.concatenate(
                [
                    (real * cos - imag * sin).reshape(64, half),
                    (real * sin + imag * cos).reshape(64, half),
                ],
                0,
            )
        )
    count = 128 // window
    tiles = 8 // count
    per_c = [[None] * tiles for _ in range(8)]
    for m_hi in range(tiles):
        for c_hi in range(tiles):
            cols = slice(128 * c_hi, 128 * c_hi + 128)
            group = [per_m[m_hi * count + i][:, cols] for i in range(count)]
            for i, value in enumerate(swap_blocks(group, window)):
                per_c[c_hi * count + i][m_hi] = value
    blocks = [
        (v[0] if tiles == 1 else jnp.concatenate(v, 1)).astype(BF16).reshape(8, 1, 16, half)
        for v in per_c
    ]
    rows = jnp.concatenate(blocks, 1).reshape(1024, half)
    out = jnp.dot(back_ref[...], rows, preferred_element_type=F32)
    if summing:
        gather_ref, share_ref = refs[8:10]
        total = jnp.dot(gather_ref[...], chunks, preferred_element_type=F32)
        out = out + jnp.dot(
            share_ref[...], jnp.concatenate(halves(total), 0), preferred_element_type=F32
        )
    out_ref[...] = out.astype(BF16)


def shifted(value, q):
    if q == 1:
        return value
    lane = lax.broadcasted_iota(jnp.int32, value.shape, 1)
    if q == 0:
        return jnp.where(lane == 0, 0.0, pltpu.roll(value, 1, 1))
    return jnp.where(lane == IMAGE - 1, 0.0, pltpu.roll(value, IMAGE - 1, 1))


def banded(weights, first_row, lowest):
    rows = []
    for r in range(GRAD_ROWS):
        total = jnp.zeros(weights[0].shape, F32)
        for p in range(3):
            total = total + jnp.where(first_row == r + p + lowest, weights[p], 0.0)
        rows.append(total)
    return jnp.concatenate(rows, 0)


def prepare_body(
    strip_ref,
    above_ref,
    below_ref,
    w_first_ref,
    w_second_ref,
    bias_ref,
    first_table_ref,
    second_table_ref,
    back_table_ref,
    rows_ref,
    estimate_ref,
    cot_ref,
    dirty_ref,
    first_ref,
    second_ref,
    back_ref,
    tall_ref,
    stack_ref,
):
    row = lax.broadcasted_iota(jnp.int32, (128, IMAGE), 0)
    tall_ref[...] = jnp.zeros_like(tall_ref)
    for i in range(6):
        for c in range(8):
            cols = slice(256 * c, 256 * c + 256)
            tall_ref[0:2, cols] = above_ref[c, i].astype(F32)
            tall_ref[2:18, cols] = strip_ref[c, i].astype(F32)
            tall_ref[18:20, cols] = below_ref[c, i].astype(F32)
        value = tall_ref[...]
        if i in (2, 3):
            dirty_ref[i - 2] = value
        else:
            for q in range(3):
                at = 20 * (3 * (i % 2) + q)
                stack_ref[at : at + 20, :] = shifted(value, q)[0:20]
            if i == 1:
                out = jnp.where(row < 120, stack_ref[...], jnp.where(row < 123, 1.0, 0.0))
                estimate_ref[...] = out.astype(BF16)
            if i == 5:
                cot_ref[...] = jnp.where(row < 120, stack_ref[...], 0.0).astype(BF16)
    w_first = w_first_ref[...]
    rows = rows_ref[0:1, :]
    parts = [jnp.dot(w_first, first_table_ref[p], preferred_element_type=F32) for p in range(3)]
    lanes = lax.broadcasted_iota(jnp.int32, (HIDDEN, 256), 1)
    bias = bias_ref[...]
    high = bias.astype(BF16).astype(F32)
    middle = (bias - high).astype(BF16).astype(F32)
    low = bias - high - middle
    offset = jnp.where(
        lanes == 120, high, jnp.where(lanes == 121, middle, jnp.where(lanes == 122, low, 0.0))
    )
    first = banded(parts, rows, 0) + jnp.concatenate([offset] * GRAD_ROWS, 0)
    first_ref[...] = first.astype(BF16)
    parts = [
        jnp.dot(w_second_ref[0], second_table_ref[0, e], preferred_element_type=F32)
        + jnp.dot(w_second_ref[1], second_table_ref[1, e], preferred_element_type=F32)
        for e in range(3)
    ]
    second_ref[...] = banded(parts, rows[:, :128], 0).astype(BF16)
    parts = [jnp.dot(w_first, back_table_ref[p], preferred_element_type=F32) for p in range(3)]
    rows = lax.broadcasted_iota(jnp.int32, (1, 192), 1) & 15
    parts = [parts[2 - p] for p in range(3)]
    back = banded_back(parts, rows)
    back_ref[...] = back.T.astype(BF16)


def banded_back(parts, rows):
    blocks = []
    for r in range(GRAD_ROWS):
        total = jnp.zeros(parts[0].shape, F32)
        for k in range(3):
            total = total + jnp.where(rows == r - k, parts[k], 0.0)
        blocks.append(total)
    return jnp.concatenate(blocks, 0)


def network_body(
    place_ref,
    in_ref,
    strip_ref,
    dirty_ref,
    estimate_ref,
    cot_ref,
    first_ref,
    second_ref,
    back_ref,
    twiddle_ref,
    inverse_ref,
    forward_ref,
    spread_ref,
    rows_ref,
    fold_ref,
    base_ref,
    out_ref,
    stack_ref,
    features_ref,
    spread_grad_ref,
    acc_first_ref,
    acc_second_ref,
):
    place = place_ref[0]
    values = lax.dot_general(in_ref[...], inverse_ref[...], TN, preferred_element_type=F32)
    row = lax.broadcasted_iota(jnp.int32, (HOLD, IMAGE), 0)
    inside = ((row >= 2) | (place > 0)) & ((row < 18) | (place < DEVS - 1))
    for plane in range(2):
        blocks = columns_back(
            lambda jlo: values[64 * jlo + 32 * plane : 64 * jlo + 32 * plane + HOLD], twiddle_ref
        )
        blurred = jnp.concatenate(blocks, 1).astype(BF16).astype(F32)
        residual = dirty_ref[plane] - jnp.where(inside, blurred, 0.0)
        residual = residual.astype(BF16).astype(F32)
        for q in range(3):
            at = 20 * (3 * plane + q)
            stack_ref[at : at + 20, :] = shifted(residual, q)[0:20]
    stack_ref[120:128, :] = jnp.zeros((8, IMAGE), F32)
    features_ref[0:128, :] = estimate_ref[...]
    features_ref[128:256, :] = stack_ref[...].astype(BF16)
    acc_first_ref[...] = jnp.zeros_like(acc_first_ref)
    acc_second_ref[...] = jnp.zeros_like(acc_second_ref)
    top = jnp.where(place > 0, 1.0, 0.0)
    bottom = jnp.where(place < DEVS - 1, 1.0, 0.0)

    def block(step, carry):
        cols = pl.ds(pl.multiple_of(step * 256, 256), 256)
        features = features_ref[:, cols]
        cots = cot_ref[:, cols]
        preact = jnp.dot(first_ref[...], features, preferred_element_type=F32)
        back = jnp.dot(second_ref[...], cots, preferred_element_type=F32)
        gate = 0.5 * jnp.tanh(0.5 * preact) + 0.5
        hidden = preact * gate
        grad_pre = back * (gate + hidden * (1.0 - gate))
        grad_pre = jnp.concatenate(
            [grad_pre[0:32] * top, grad_pre[32:544], grad_pre[544:576] * bottom], 0
        ).astype(BF16)
        spread_grad_ref[:, cols] = jnp.dot(back_ref[...], grad_pre, preferred_element_type=F32)
        acc_first_ref[...] += lax.dot_general(grad_pre, features, NT, preferred_element_type=F32)
        acc_second_ref[...] += lax.dot_general(
            hidden.astype(BF16), cots, NT, preferred_element_type=F32
        )
        return carry

    lax.fori_loop(0, 8, block, 0)

    cot_sums = []
    z = [[None, None] for _ in range(8)]
    for i in range(4):
        rows = [spread_grad_ref[64 * q + 16 * i : 64 * q + 16 * i + 16, :] for q in range(3)]
        total = shifted(rows[0], 2) + rows[1] + shifted(rows[2], 0)
        for c in range(8):
            part = total[:, 256 * c : 256 * c + 256]
            if i < 2:
                base_ref[c, i] = part + strip_ref[c, 4 + i].astype(F32)
            else:
                z[c][i - 2] = part.astype(BF16).astype(F32)
    for i in range(2):
        total = strip_ref[0, 4 + i].astype(F32)
        for c in range(1, 8):
            total = total + strip_ref[c, 4 + i].astype(F32)
        cot_sums.append(total.sum(axis=0, keepdims=True).sum(axis=1, keepdims=True))

    rows = rows_ref[0:1, :]
    parts = [jnp.zeros((HIDDEN, 384), F32) for _ in range(3)]
    for r in range(1, 17):
        of_first = acc_first_ref[32 * r : 32 * r + 32, :]
        of_second = acc_second_ref[32 * r : 32 * r + 32, :]
        for p in range(3):
            keep = (rows == r + p) | (rows == -1)
            parts[p] = parts[p] + jnp.concatenate(
                [
                    jnp.where(keep, of_first, 0.0),
                    jnp.where(rows[:, :128] == r + p, of_second, 0.0),
                ],
                1,
            )
    sums = jnp.zeros((HIDDEN, 128), F32)
    for p in range(3):
        sums = sums + jnp.dot(
            parts[p], fold_ref[p], precision=lax.Precision.HIGHEST, preferred_element_type=F32
        )
    at = lax.broadcasted_iota(jnp.int32, (HIDDEN, 128), 1)
    of = lax.broadcasted_iota(jnp.int32, (HIDDEN, 128), 0)
    for i in range(2):
        sums = jnp.where((at == 55) & (of == i), cot_sums[i], sums)

    values = columns_ahead([jnp.concatenate(v, 0) for v in z], twiddle_ref)
    out = lax.dot_general(forward_ref[...], values, NT, preferred_element_type=F32)
    out = out + jnp.dot(
        spread_ref[...], jnp.concatenate(halves(sums), 0), preferred_element_type=F32
    )
    out_ref[...] = out.astype(BF16)


def finish_body(in_ref, base_ref, twiddle_ref, inverse_ref, collect_ref, out_ref, sums_ref):
    chunks = in_ref[...]
    sums_ref[...] = jnp.dot(collect_ref[...], chunks, preferred_element_type=F32) * (1.0 / IMAGE)
    values = lax.dot_general(chunks, inverse_ref[...], TN, preferred_element_type=F32)
    blocks = columns_back(lambda jlo: values[32 * jlo : 32 * jlo + 32], twiddle_ref)
    for c in range(8):
        blurred = blocks[c].astype(BF16).astype(F32).reshape(2, STRIP, 256)
        out_ref[c] = base_ref[c] - blurred


def call(body, outs, *args, scratch=(), scalars=0, vmem=56):
    whole = pl.BlockSpec(memory_space=pltpu.VMEM)
    return pl.pallas_call(
        body,
        out_shape=outs,
        in_specs=[pl.BlockSpec(memory_space=pltpu.SMEM)] * scalars
        + [whole] * (len(args) - scalars),
        out_specs=jax.tree.map(lambda _: whole, outs),
        scratch_shapes=list(scratch),
        compiler_params=pltpu.CompilerParams(vmem_limit_bytes=vmem * 1024 * 1024),
    )(*args)


def like(*shape, dtype=BF16):
    return jax.ShapeDtypeStruct(shape, dtype)


def exchange(chunks, per):
    width = chunks.shape[-1]
    rows = 8 if per == 8 else 2
    moved = lax.all_to_all(chunks.reshape(DEVS * per // rows, rows, width), RC, 0, 0, tiled=True)
    return moved.reshape(DEVS * per, width)


def middle(chunks, spectra, window, lead, per):
    ahead, back = row_block_tables(per)
    twiddle, row_table = row_forward_tables()
    back_twiddle, back_row = row_inverse_tables(window, lead)
    extra = sum_tables()[1:3] if per == 10 else ()
    return call(
        functools.partial(middle_body, window, per == 10),
        like(DEVS * per, 8 * window),
        chunks,
        spectra,
        ahead,
        back,
        row_table,
        back_row,
        twiddle,
        back_twiddle,
        *extra,
    )


def shards(estimate, dirty_image, psf_spectra, w_first, b_first, w_second, cotangent):
    cells = jnp.stack([v.reshape(2, 8, STRIP, 256) for v in (estimate, dirty_image, cotangent)])
    cells = cells.transpose(2, 0, 1, 3, 4).reshape(8, 6, STRIP, 256)
    strip = lax.all_to_all(cells, "col", 0, 0, tiled=True)
    spec = call(
        ahead_body, like(1024, 128), strip, column_twiddle(), column_forward_table(8)
    )
    spec = exchange(spec, 8)
    above = lax.ppermute(strip[:, :, -2:], RC, [(d, d + 1) for d in range(DEVS - 1)])
    below = lax.ppermute(strip[:, :, :2], RC, [(d + 1, d) for d in range(DEVS - 1)])
    first_table, second_table, back_table, row_of, fold = weight_tables()
    im_estimate, im_cot, dirty, first, second, back = call(
        prepare_body,
        (
            like(128, IMAGE),
            like(128, IMAGE),
            like(2, HOLD, IMAGE, dtype=F32),
            like(576, 256),
            like(576, 128),
            like(192, 576),
        ),
        strip,
        above,
        below,
        w_first.reshape(32, 36),
        w_second.reshape(2, 32, 9),
        b_first.reshape(32, 1),
        first_table,
        second_table,
        back_table,
        row_of,
        scratch=[pltpu.VMEM((HOLD, IMAGE), F32), pltpu.VMEM((128, IMAGE), F32)],
    )
    mixed = exchange(middle(spec, psf_spectra, 32, 2, 8), 8)
    place = (lax.axis_index("row") * 8 + lax.axis_index("col")).astype(jnp.int32).reshape(1)
    base, spec = call(
        network_body,
        (like(8, 2, STRIP, 256, dtype=F32), like(1280, 128)),
        place,
        mixed,
        strip,
        dirty,
        im_estimate,
        im_cot,
        first,
        second,
        back,
        column_twiddle(),
        column_inverse_table(8),
        column_forward_table(10),
        sum_tables()[0],
        row_of,
        fold,
        scratch=[
            pltpu.VMEM((128, IMAGE), F32),
            pltpu.VMEM((256, IMAGE), BF16),
            pltpu.VMEM((192, IMAGE), F32),
            pltpu.VMEM((576, 256), F32),
            pltpu.VMEM((576, 128), F32),
        ],
        scalars=1,
    )
    mixed = exchange(middle(exchange(spec, 10), psf_spectra, 16, 0, 10), 10)
    image, sums = call(
        finish_body,
        (like(8, 2, STRIP, 256, dtype=F32), like(32, 128, dtype=F32)),
        mixed,
        base,
        column_twiddle(),
        column_inverse_table(10),
        sum_tables()[3],
    )
    image = lax.all_to_all(image, "col", 0, 0, tiled=True)
    grad_image = image.transpose(1, 0, 2, 3).reshape(2, 128, 256)
    grad_first = sums[:, :36].reshape(32, 3, 4, 3).transpose(0, 2, 1, 3)
    grad_second = jnp.flip(sums[:, 36:54].reshape(32, 3, 2, 3), (1, 3)).transpose(2, 0, 1, 3)
    return grad_image, grad_first, sums[:, 54], grad_second, sums[:2, 55]


def solution(mesh):
    return jax.shard_map(
        shards,
        mesh=mesh,
        in_specs=(
            P(None, "row", "col"),
            P(None, "row", "col"),
            P(None, ("row", "col"), None, None),
            P(),
            P(),
            P(),
            P(None, "row", "col"),
        ),
        out_specs=(P(None, "row", "col"), P(), P(), P(), P()),
        check_vma=False,
    )
```

```python
import functools

import jax
import jax.numpy as jnp
import numpy as np
from jax import lax
from jax.experimental import pallas as pl
from jax.experimental.pallas import tpu as pltpu
from jax.sharding import PartitionSpec as P

IMAGE = 2048
DEVS = 128
STRIP = 16
REACH = 20
HOLD = 24
GRAD_ROWS = 18
HIDDEN = 32
RC = ("row", "col")
F32 = jnp.float32
BF16 = jnp.bfloat16
NT = (((1,), (1,)), ((), ()))
TN = (((0,), (0,)), ((), ()))


def turn(product, period):
    angle = 2.0 * np.pi * (product % period) / period
    return np.cos(angle), np.sin(angle)


def bf16_table(values):
    return np.asarray(values, np.float32).astype(jnp.bfloat16)


@functools.lru_cache(None)
def column_twiddle():
    cos, sin = turn(np.arange(8)[:, None] * np.arange(256)[None, :], 2048)
    return np.concatenate([cos, sin]).astype(np.float32)


@functools.lru_cache(None)
def column_tables():
    freq = 2 * np.arange(128)[:, None] + np.arange(2)[None, :]
    cos, sin = turn(freq[:, :, None] * np.arange(256), 256)
    ahead = np.zeros((128, 2, 2, 2, 256))
    ahead[:, 0, :, 0] = cos
    ahead[:, 0, :, 1] = sin
    ahead[:, 1, :, 0] = -sin
    ahead[:, 1, :, 1] = cos
    back = np.zeros((128, 2, 2, 2, 256))
    back[:, 0, :, 0] = cos
    back[:, 1, :, 0] = -sin
    back[:, 0, :, 1] = sin
    back[:, 1, :, 1] = cos
    return bf16_table(ahead.reshape(512, 512)), bf16_table(back.reshape(512, 512))


@functools.lru_cache(None)
def row_block_tables():
    cos, sin = turn(np.arange(16)[:, None] * np.arange(16), 16)
    ahead = np.zeros((2, 2, 2, 16, 16, 2, 2, 2))
    for kappa in range(2):
        for jhi in range(2):
            ahead[0, kappa, jhi, :, :, jhi, 0, kappa] = cos
            ahead[0, kappa, jhi, :, :, jhi, 1, kappa] = sin
            ahead[1, kappa, jhi, :, :, jhi, 0, kappa] = -sin
            ahead[1, kappa, jhi, :, :, jhi, 1, kappa] = cos
    ahead = ahead.reshape(128, 128)
    return bf16_table(ahead), bf16_table(ahead.T / IMAGE)


@functools.lru_cache(None)
def row_forward_tables():
    pos = np.arange(128)
    cos, sin = turn(np.arange(16)[:, None] * pos, 2048)
    twiddle = np.concatenate([cos, sin]).astype(np.float32)
    cos, sin = turn(pos[:, None] * np.arange(128), 128)
    return twiddle, bf16_table(np.concatenate([cos, sin], 1))


@functools.lru_cache(None)
def row_inverse_tables(window, lead):
    pos = (16 * np.arange(8)[:, None] + np.arange(window)[None, :] - lead).reshape(-1)
    cos, sin = turn(np.arange(16)[:, None] * pos, 2048)
    twiddle = np.concatenate([cos, sin]).astype(np.float32)
    cos, sin = turn(np.arange(128)[:, None] * pos, 128)
    return twiddle, bf16_table(np.concatenate([cos, sin], 1))


@functools.lru_cache(None)
def sum_tables():
    spread = np.zeros((128, 10, 64))
    share = np.zeros((128, 10, 32))
    gather = np.zeros((16, 128, 10))
    collect = np.zeros((32, 128, 10))
    for d in range(128):
        spread[d, 8, d % 32] = 1.0
        spread[d, 9, 32 + d % 32] = 1.0
    share[:, 8, 0] = 1.0
    share[:, 9, 16] = 1.0
    gather[:, :, 8:] = 1.0
    for c in range(32):
        collect[c, c, 8:] = 1.0
    return (
        bf16_table(spread.reshape(1280, 64)),
        bf16_table(gather.reshape(16, 1280)),
        bf16_table(share.reshape(1280, 32)),
        bf16_table(collect.reshape(32, 1280)),
    )


@functools.lru_cache(None)
def weight_tables():
    first = np.zeros((3, 36, 256))
    second = np.zeros((2, 3, 9, 128))
    back = np.zeros((3, 36, 192))
    rows = np.full((8, 256), 99)
    for i in range(4):
        for q in range(3):
            at = 128 * (i // 2) + 20 * (3 * (i % 2) + q)
            rows[:, at : at + 20] = np.arange(20)
            for p in range(3):
                first[p, i * 9 + p * 3 + q, at : at + 20] = 1.0
                back[p, i * 9 + p * 3 + q, q * 64 + i * 16 : q * 64 + i * 16 + 16] = 1.0
    rows[:, 120] = -1
    for o in range(2):
        for q in range(3):
            at = 20 * (3 * o + q)
            for e in range(3):
                second[o, e, (2 - e) * 3 + 2 - q, at : at + 20] = 1.0
    fold = np.zeros((3, 384, 128), np.float32)
    for p in range(3):
        for i in range(4):
            for q in range(3):
                at = 128 * (i // 2) + 20 * (3 * (i % 2) + q)
                fold[p, at : at + 20, p * 12 + i * 3 + q] = 1.0
        for o in range(2):
            for q in range(3):
                at = 256 + 20 * (3 * o + q)
                fold[p, at : at + 20, 36 + p * 6 + o * 3 + q] = 1.0
    fold[0, 120, 54] = 1.0
    return (
        bf16_table(first),
        bf16_table(second),
        bf16_table(back),
        rows.astype(np.int32),
        bf16_table(fold),
    )


def columns_ahead(z, twiddle_ref, table_ref):
    root = float(np.sqrt(0.5))
    s04, d04 = z[0] + z[4], z[0] - z[4]
    s26, d26 = z[2] + z[6], z[2] - z[6]
    s15, d15 = z[1] + z[5], z[1] - z[5]
    s37, d37 = z[3] + z[7], z[3] - z[7]
    low, high = root * (d15 - d37), root * (d15 + d37)
    real = [None] * 8
    imag = [None] * 8
    even, odd = s04 + s26, s15 + s37
    real[0], real[4] = even + odd, even - odd
    real[2], imag[2] = s04 - s26, s37 - s15
    real[1], imag[1] = d04 + low, -d26 - high
    real[3], imag[3] = d04 - low, d26 - high
    for j in (1, 2, 3):
        real[8 - j], imag[8 - j] = real[j], -imag[j]
    groups = []
    for j in range(8):
        cos, sin = twiddle_ref[j : j + 1, :], twiddle_ref[8 + j : 9 + j, :]
        if imag[j] is None:
            pieces = [real[j] * cos, -real[j] * sin]
        else:
            pieces = [real[j] * cos + imag[j] * sin, imag[j] * cos - real[j] * sin]
        groups.append(jnp.concatenate(pieces, axis=1).astype(BF16))
    values = lax.dot_general(
        table_ref[...], jnp.concatenate(groups, axis=0), NT, preferred_element_type=F32
    )
    low, high = (values[:, at : at + 128].reshape(64, 8, 128) for at in (0, 128))
    sub = lax.broadcasted_iota(jnp.int32, (64, 8, 128), 1)
    return (
        jnp.where(sub < 4, low, pltpu.roll(high, 4, 1)),
        jnp.where(sub < 4, pltpu.roll(low, 4, 1), high),
    )


def regroup(even, odd):
    sub = lax.broadcasted_iota(jnp.int32, even.shape, 1)
    shape = (512, even.shape[2])
    first = jnp.where(sub < 4, even, pltpu.roll(odd, 4, 1))
    second = jnp.where(sub < 4, pltpu.roll(even, 4, 1), odd)
    return jnp.concatenate([first.reshape(shape), second.reshape(shape)], 1).astype(BF16)


def spaced(chunks):
    gap = jnp.zeros((chunks[0].shape[0], 2, 128), F32)
    pieces = []
    for value in chunks:
        pieces += [value, gap]
    return jnp.concatenate(pieces, 1)


def unspaced(rows):
    rows = rows.astype(F32).reshape(32, 40, 128)
    return [rows[:, 10 * j : 10 * j + 8] for j in range(4)]


def columns_back(rows_of, twiddle_ref):
    real = [None] * 8
    imag = [None] * 8
    for j in range(8):
        rows = rows_of(j)
        re, im = rows[:, :256], rows[:, 256:]
        cos, sin = twiddle_ref[j : j + 1, :], twiddle_ref[8 + j : 9 + j, :]
        real[j] = re * cos - im * sin
        imag[j] = re * sin + im * cos
    fold_re = [real[0]] + [real[j] + real[8 - j] for j in (1, 2, 3)] + [real[4]]
    fold_im = [None] + [imag[j] - imag[8 - j] for j in (1, 2, 3)]
    scale = 1.0 / IMAGE
    root = float(np.sqrt(0.5)) * scale
    base_even = (fold_re[0] + fold_re[4]) * scale
    base_odd = (fold_re[0] - fold_re[4]) * scale
    re2, im2 = fold_re[2] * scale, fold_im[2] * scale
    sum_re, dif_re = fold_re[1] + fold_re[3], fold_re[1] - fold_re[3]
    sum_im, dif_im = fold_im[1] + fold_im[3], fold_im[1] - fold_im[3]
    cross = root * (dif_re - sum_im), root * (dif_re + sum_im)
    return [
        base_even + re2 + sum_re * scale,
        base_odd - im2 + cross[0],
        base_even - re2 - dif_im * scale,
        base_odd + im2 - cross[1],
        base_even + re2 - sum_re * scale,
        base_odd - im2 - cross[0],
        base_even - re2 + dif_im * scale,
        base_odd + im2 + cross[1],
    ]


def swap_blocks(arrays, size):
    arrays = list(arrays)
    count = 128 // size
    lane = lax.broadcasted_iota(jnp.int32, arrays[0].shape, 1)
    step = count // 2
    while step:
        low = (lane & (step * size)) == 0
        for i in range(count):
            if not i & step:
                one, two = arrays[i], arrays[i + step]
                arrays[i] = jnp.where(low, one, pltpu.roll(two, step * size, 1))
                arrays[i + step] = jnp.where(low, pltpu.roll(one, 128 - step * size, 1), two)
        step //= 2
    return arrays


def halves(values):
    high = values.astype(BF16)
    return high, (values - high.astype(F32)).astype(BF16)


def ahead_body(strip_ref, twiddle_ref, table_ref, out_ref):
    z = [strip_ref[c, 0:2].astype(F32).reshape(32, 256) for c in range(8)]
    even, odd = columns_ahead(z, twiddle_ref, table_ref)
    out_ref[...] = jnp.stack([even, odd], 1).reshape(1024, 128).astype(BF16)


def middle_body(window, summing, *refs):
    in_ref, spectra_ref, ahead_ref, back_ref, row_ref, back_row_ref, tw_ref, back_tw_ref = refs[:8]
    out_ref = refs[-1]
    chunks = in_ref[...]
    if summing:
        fours = [part.reshape(16, 2, 8, 128) for part in unspaced(chunks)]
        rows = [fours[c % 4][:, c // 4].reshape(128, 128) for c in range(8)]
    else:
        rows = chunks.astype(F32).reshape(16, 8, 8, 128)
        rows = [rows[:, c].reshape(128, 128) for c in range(8)]
    rows = jnp.concatenate(rows, 1).astype(BF16)
    first = jnp.dot(ahead_ref[...], rows, preferred_element_type=F32)
    per_m = swap_blocks([first[:, 128 * c : 128 * c + 128] for c in range(8)], 16)
    cos, sin = tw_ref[0:16, :], tw_ref[16:32, :]
    rows = []
    for m in range(8):
        real = per_m[m][:64].reshape(4, 16, 128)
        imag = per_m[m][64:].reshape(4, 16, 128)
        rows.append((real * cos + imag * sin).astype(BF16).reshape(64, 128))
        rows.append((imag * cos - real * sin).astype(BF16).reshape(64, 128))
    second = jnp.dot(jnp.concatenate(rows, 0), row_ref[...], preferred_element_type=F32)
    rows = []
    for jlo in range(4):
        full_re, full_im = [], []
        for plane in range(2):
            m = 2 * jlo + plane
            part = second[128 * m : 128 * m + 128]
            full_re.append(part[:64, :128] + part[64:, 128:])
            full_im.append(part[64:, :128] - part[:64, 128:])
        weights = [
            spectra_ref[t].reshape(4, 4, 16, 128)[:, jlo].reshape(64, 128) for t in range(3)
        ]
        for plane in range(2):
            for part in (full_re, full_im):
                mixed = weights[plane] * part[0] + weights[plane + 1] * part[1]
                rows.append(mixed.astype(BF16))
    third = jnp.dot(jnp.concatenate(rows, 0), back_row_ref[...], preferred_element_type=F32)
    half = 8 * window
    cos, sin = back_tw_ref[0:16, :], back_tw_ref[16:32, :]
    per_m = []
    for m in range(8):
        part = third[128 * m : 128 * m + 128]
        real = (part[:64, :half] - part[64:, half:]).reshape(4, 16, half)
        imag = (part[64:, :half] + part[:64, half:]).reshape(4, 16, half)
        per_m.append(
            jnp.concatenate(
                [
                    (real * cos - imag * sin).reshape(64, half),
                    (real * sin + imag * cos).reshape(64, half),
                ],
                0,
            )
        )
    count = 128 // window
    tiles = 8 // count
    per_c = [[None] * tiles for _ in range(8)]
    for m_hi in range(tiles):
        for c_hi in range(tiles):
            cols = slice(128 * c_hi, 128 * c_hi + 128)
            group = [per_m[m_hi * count + i][:, cols] for i in range(count)]
            for i, value in enumerate(swap_blocks(group, window)):
                per_c[c_hi * count + i][m_hi] = value
    rows = jnp.concatenate([tile for v in per_c for tile in v], 1).astype(BF16)
    out = jnp.dot(back_ref[...], rows, preferred_element_type=F32)
    out = [out[:, half * c : half * c + half].reshape(16, 8, half) for c in range(8)]
    if summing:
        gather_ref, share_ref = refs[8:10]
        total = jnp.dot(gather_ref[...], chunks, preferred_element_type=F32)
        out = jnp.stack([spaced(out[:4]), spaced(out[4:])], 1).reshape(1280, 128)
        out = out + jnp.dot(
            share_ref[...], jnp.concatenate(halves(total), 0), preferred_element_type=F32
        )
    else:
        out = jnp.stack(out, 1).reshape(1024, half)
    out_ref[...] = out.astype(BF16)


def shifted(value, q):
    if q == 1:
        return value
    lane = lax.broadcasted_iota(jnp.int32, value.shape, 1)
    if q == 0:
        return jnp.where(lane == 0, 0.0, pltpu.roll(value, 1, 1))
    return jnp.where(lane == IMAGE - 1, 0.0, pltpu.roll(value, IMAGE - 1, 1))


def banded(weights, first_row, lowest):
    rows = []
    for r in range(GRAD_ROWS):
        total = jnp.zeros(weights[0].shape, F32)
        for p in range(3):
            total = total + jnp.where(first_row == r + p + lowest, weights[p], 0.0)
        rows.append(total)
    return jnp.concatenate(rows, 0)


def prepare_body(
    strip_ref,
    above_ref,
    below_ref,
    w_first_ref,
    w_second_ref,
    bias_ref,
    first_table_ref,
    second_table_ref,
    back_table_ref,
    rows_ref,
    estimate_ref,
    cot_ref,
    dirty_ref,
    first_ref,
    second_ref,
    back_ref,
    tall_ref,
    stack_ref,
):
    row = lax.broadcasted_iota(jnp.int32, (128, IMAGE), 0)
    tall_ref[...] = jnp.zeros_like(tall_ref)
    for i in range(6):
        for c in range(8):
            cols = slice(256 * c, 256 * c + 256)
            tall_ref[0:2, cols] = above_ref[c, i].astype(F32)
            tall_ref[2:18, cols] = strip_ref[c, i].astype(F32)
            tall_ref[18:20, cols] = below_ref[c, i].astype(F32)
        value = tall_ref[...]
        if i in (2, 3):
            dirty_ref[i - 2] = value
        else:
            for q in range(3):
                at = 20 * (3 * (i % 2) + q)
                stack_ref[at : at + 20, :] = shifted(value, q)[0:20]
            if i == 1:
                out = jnp.where(row < 120, stack_ref[...], jnp.where(row < 123, 1.0, 0.0))
                estimate_ref[...] = out.astype(BF16)
            if i == 5:
                cot_ref[...] = jnp.where(row < 120, stack_ref[...], 0.0).astype(BF16)
    w_first = w_first_ref[...]
    rows = rows_ref[0:1, :]
    parts = [jnp.dot(w_first, first_table_ref[p], preferred_element_type=F32) for p in range(3)]
    lanes = lax.broadcasted_iota(jnp.int32, (HIDDEN, 256), 1)
    bias = bias_ref[...]
    high = bias.astype(BF16).astype(F32)
    middle = (bias - high).astype(BF16).astype(F32)
    low = bias - high - middle
    offset = jnp.where(
        lanes == 120, high, jnp.where(lanes == 121, middle, jnp.where(lanes == 122, low, 0.0))
    )
    first = banded(parts, rows, 0) + jnp.concatenate([offset] * GRAD_ROWS, 0)
    first_ref[...] = first.astype(BF16)
    parts = [
        jnp.dot(w_second_ref[0], second_table_ref[0, e], preferred_element_type=F32)
        + jnp.dot(w_second_ref[1], second_table_ref[1, e], preferred_element_type=F32)
        for e in range(3)
    ]
    second_ref[...] = banded(parts, rows[:, :128], 0).astype(BF16)
    parts = [jnp.dot(w_first, back_table_ref[p], preferred_element_type=F32) for p in range(3)]
    rows = lax.broadcasted_iota(jnp.int32, (1, 192), 1) & 15
    parts = [parts[2 - p] for p in range(3)]
    back = banded_back(parts, rows)
    back_ref[...] = back.T.astype(BF16)


def banded_back(parts, rows):
    blocks = []
    for r in range(GRAD_ROWS):
        total = jnp.zeros(parts[0].shape, F32)
        for k in range(3):
            total = total + jnp.where(rows == r - k, parts[k], 0.0)
        blocks.append(total)
    return jnp.concatenate(blocks, 0)


def network_body(
    place_ref,
    in_ref,
    strip_ref,
    dirty_ref,
    estimate_ref,
    cot_ref,
    first_ref,
    second_ref,
    back_ref,
    twiddle_ref,
    inverse_ref,
    forward_ref,
    spread_ref,
    rows_ref,
    fold_ref,
    base_ref,
    out_ref,
    stack_ref,
    features_ref,
    spread_grad_ref,
    acc_first_ref,
    acc_second_ref,
):
    place = place_ref[0]
    chunks = in_ref[...].astype(F32).reshape(64, 2, 8, 256)
    values = lax.dot_general(
        regroup(chunks[:, 0], chunks[:, 1]), inverse_ref[...], TN, preferred_element_type=F32
    )
    row = lax.broadcasted_iota(jnp.int32, (HOLD, IMAGE), 0)
    inside = ((row >= 2) | (place > 0)) & ((row < 18) | (place < DEVS - 1))
    for plane in range(2):
        blocks = columns_back(
            lambda j: values[64 * j + 32 * plane : 64 * j + 32 * plane + HOLD], twiddle_ref
        )
        blurred = jnp.concatenate(blocks, 1).astype(BF16).astype(F32)
        residual = dirty_ref[plane] - jnp.where(inside, blurred, 0.0)
        residual = residual.astype(BF16).astype(F32)
        for q in range(3):
            at = 20 * (3 * plane + q)
            stack_ref[at : at + 20, :] = shifted(residual, q)[0:20]
    stack_ref[120:128, :] = jnp.zeros((8, IMAGE), F32)
    features_ref[0:128, :] = estimate_ref[...]
    features_ref[128:256, :] = stack_ref[...].astype(BF16)
    acc_first_ref[...] = jnp.zeros_like(acc_first_ref)
    acc_second_ref[...] = jnp.zeros_like(acc_second_ref)
    top = jnp.where(place > 0, 1.0, 0.0)
    bottom = jnp.where(place < DEVS - 1, 1.0, 0.0)

    def block(step, carry):
        cols = pl.ds(pl.multiple_of(step * 256, 256), 256)
        features = features_ref[:, cols]
        cots = cot_ref[:, cols]
        preact = jnp.dot(first_ref[...], features, preferred_element_type=F32)
        back = jnp.dot(second_ref[...], cots, preferred_element_type=F32)
        gate = 0.5 * jnp.tanh(0.5 * preact) + 0.5
        hidden = preact * gate
        grad_pre = back * (gate + hidden * (1.0 - gate))
        grad_pre = jnp.concatenate(
            [grad_pre[0:32] * top, grad_pre[32:544], grad_pre[544:576] * bottom], 0
        ).astype(BF16)
        spread_grad_ref[:, cols] = jnp.dot(back_ref[...], grad_pre, preferred_element_type=F32)
        acc_first_ref[...] += lax.dot_general(grad_pre, features, NT, preferred_element_type=F32)
        acc_second_ref[...] += lax.dot_general(
            hidden.astype(BF16), cots, NT, preferred_element_type=F32
        )
        return carry

    lax.fori_loop(0, 8, block, 0)

    cot_sums = []
    z = [[None, None] for _ in range(8)]
    for i in range(4):
        rows = [spread_grad_ref[64 * q + 16 * i : 64 * q + 16 * i + 16, :] for q in range(3)]
        total = shifted(rows[0], 2) + rows[1] + shifted(rows[2], 0)
        for c in range(8):
            part = total[:, 256 * c : 256 * c + 256]
            if i < 2:
                base_ref[c, i] = part + strip_ref[c, 4 + i].astype(F32)
            else:
                z[c][i - 2] = part.astype(BF16).astype(F32)
    for i in range(2):
        total = strip_ref[0, 4 + i].astype(F32)
        for c in range(1, 8):
            total = total + strip_ref[c, 4 + i].astype(F32)
        cot_sums.append(total.sum(axis=0, keepdims=True).sum(axis=1, keepdims=True))

    rows = rows_ref[0:1, :]
    parts = [jnp.zeros((HIDDEN, 384), F32) for _ in range(3)]
    for r in range(1, 17):
        of_first = acc_first_ref[32 * r : 32 * r + 32, :]
        of_second = acc_second_ref[32 * r : 32 * r + 32, :]
        for p in range(3):
            keep = (rows == r + p) | (rows == -1)
            parts[p] = parts[p] + jnp.concatenate(
                [
                    jnp.where(keep, of_first, 0.0),
                    jnp.where(rows[:, :128] == r + p, of_second, 0.0),
                ],
                1,
            )
    sums = jnp.zeros((HIDDEN, 128), F32)
    for p in range(3):
        sums = sums + jnp.dot(
            parts[p],
            fold_ref[p].astype(F32),
            precision=lax.Precision.HIGHEST,
            preferred_element_type=F32,
        )
    at = lax.broadcasted_iota(jnp.int32, (HIDDEN, 128), 1)
    of = lax.broadcasted_iota(jnp.int32, (HIDDEN, 128), 0)
    for i in range(2):
        sums = jnp.where((at == 55) & (of == i), cot_sums[i], sums)

    even, odd = columns_ahead([jnp.concatenate(v, 0) for v in z], twiddle_ref, forward_ref)
    even, odd = even.reshape(32, 2, 8, 128), odd.reshape(32, 2, 8, 128)
    out = spaced([even[:, 0], odd[:, 0], even[:, 1], odd[:, 1]]).reshape(1280, 128)
    out = out + jnp.dot(
        spread_ref[...], jnp.concatenate(halves(sums), 0), preferred_element_type=F32
    )
    out_ref[...] = out.astype(BF16)


def finish_body(in_ref, base_ref, twiddle_ref, inverse_ref, collect_ref, out_ref, sums_ref):
    chunks = in_ref[...]
    sums_ref[...] = jnp.dot(collect_ref[...], chunks, preferred_element_type=F32) * (1.0 / IMAGE)
    fours = unspaced(chunks)
    even = jnp.stack([fours[0], fours[2]], 1).reshape(64, 8, 128)
    odd = jnp.stack([fours[1], fours[3]], 1).reshape(64, 8, 128)
    values = lax.dot_general(
        regroup(even, odd), inverse_ref[...], TN, preferred_element_type=F32
    )
    blocks = columns_back(lambda j: values[32 * j : 32 * j + 32], twiddle_ref)
    for c in range(8):
        blurred = blocks[c].astype(BF16).astype(F32).reshape(2, STRIP, 256)
        out_ref[c] = base_ref[c] - blurred


def call(body, outs, *args, scratch=(), scalars=0, vmem=56):
    whole = pl.BlockSpec(memory_space=pltpu.VMEM)
    return pl.pallas_call(
        body,
        out_shape=outs,
        in_specs=[pl.BlockSpec(memory_space=pltpu.SMEM)] * scalars
        + [whole] * (len(args) - scalars),
        out_specs=jax.tree.map(lambda _: whole, outs),
        scratch_shapes=list(scratch),
        compiler_params=pltpu.CompilerParams(vmem_limit_bytes=vmem * 1024 * 1024),
    )(*args)


def like(*shape, dtype=BF16):
    return jax.ShapeDtypeStruct(shape, dtype)


def exchange(chunks, per):
    width = chunks.shape[-1]
    rows = 8 if per == 8 else 2
    moved = lax.all_to_all(chunks.reshape(DEVS * per // rows, rows, width), RC, 0, 0, tiled=True)
    return moved.reshape(DEVS * per, width)


def middle(chunks, spectra, window, lead, per):
    ahead, back = row_block_tables()
    twiddle, row_table = row_forward_tables()
    back_twiddle, back_row = row_inverse_tables(window, lead)
    extra = sum_tables()[1:3] if per == 10 else ()
    return call(
        functools.partial(middle_body, window, per == 10),
        like(DEVS * per, 8 * window),
        chunks,
        spectra,
        ahead,
        back,
        row_table,
        back_row,
        twiddle,
        back_twiddle,
        *extra,
    )


def shards(estimate, dirty_image, psf_spectra, w_first, b_first, w_second, cotangent):
    cells = jnp.stack([v.reshape(2, 8, STRIP, 256) for v in (estimate, dirty_image, cotangent)])
    cells = cells.transpose(2, 0, 1, 3, 4).reshape(8, 6, STRIP, 256)
    strip = lax.all_to_all(cells, "col", 0, 0, tiled=True)
    spec = call(
        ahead_body, like(1024, 128), strip, column_twiddle(), column_tables()[0]
    )
    spec = exchange(spec, 8)
    above = lax.ppermute(strip[:, :, -2:], RC, [(d, d + 1) for d in range(DEVS - 1)])
    below = lax.ppermute(strip[:, :, :2], RC, [(d + 1, d) for d in range(DEVS - 1)])
    first_table, second_table, back_table, row_of, fold = weight_tables()
    im_estimate, im_cot, dirty, first, second, back = call(
        prepare_body,
        (
            like(128, IMAGE),
            like(128, IMAGE),
            like(2, HOLD, IMAGE, dtype=F32),
            like(576, 256),
            like(576, 128),
            like(192, 576),
        ),
        strip,
        above,
        below,
        w_first.reshape(32, 36),
        w_second.reshape(2, 32, 9),
        b_first.reshape(32, 1),
        first_table,
        second_table,
        back_table,
        row_of,
        scratch=[pltpu.VMEM((HOLD, IMAGE), F32), pltpu.VMEM((128, IMAGE), F32)],
    )
    mixed = exchange(middle(spec, psf_spectra, 32, 2, 8), 8)
    place = (lax.axis_index("row") * 8 + lax.axis_index("col")).astype(jnp.int32).reshape(1)
    base, spec = call(
        network_body,
        (like(8, 2, STRIP, 256, dtype=F32), like(1280, 128)),
        place,
        mixed,
        strip,
        dirty,
        im_estimate,
        im_cot,
        first,
        second,
        back,
        column_twiddle(),
        column_tables()[1],
        column_tables()[0],
        sum_tables()[0],
        row_of,
        fold,
        scratch=[
            pltpu.VMEM((128, IMAGE), F32),
            pltpu.VMEM((256, IMAGE), BF16),
            pltpu.VMEM((192, IMAGE), F32),
            pltpu.VMEM((576, 256), F32),
            pltpu.VMEM((576, 128), F32),
        ],
        scalars=1,
    )
    mixed = exchange(middle(exchange(spec, 10), psf_spectra, 16, 0, 10), 10)
    image, sums = call(
        finish_body,
        (like(8, 2, STRIP, 256, dtype=F32), like(32, 128, dtype=F32)),
        mixed,
        base,
        column_twiddle(),
        column_tables()[1],
        sum_tables()[3],
    )
    image = lax.all_to_all(image, "col", 0, 0, tiled=True)
    grad_image = image.transpose(1, 0, 2, 3).reshape(2, 128, 256)
    grad_first = sums[:, :36].reshape(32, 3, 4, 3).transpose(0, 2, 1, 3)
    grad_second = jnp.flip(sums[:, 36:54].reshape(32, 3, 2, 3), (1, 3)).transpose(2, 0, 1, 3)
    return grad_image, grad_first, sums[:, 54], grad_second, sums[:2, 55]


def solution(mesh):
    return jax.shard_map(
        shards,
        mesh=mesh,
        in_specs=(
            P(None, "row", "col"),
            P(None, "row", "col"),
            P(None, ("row", "col"), None, None),
            P(),
            P(),
            P(),
            P(None, "row", "col"),
        ),
        out_specs=(P(None, "row", "col"), P(), P(), P(), P()),
        check_vma=False,
    )
```

```python
import functools

import jax
import jax.numpy as jnp
import numpy as np
from jax import lax
from jax.experimental import pallas as pl
from jax.experimental.pallas import tpu as pltpu
from jax.sharding import PartitionSpec as P

IMAGE = 2048
DEVS = 128
VM = 20
STRIP = 16
REACH = 20
HOLD = 24
GRAD_ROWS = 18
HIDDEN = 32
RC = ("row", "col")
F32 = jnp.float32
BF16 = jnp.bfloat16
NT = (((1,), (1,)), ((), ()))
TN = (((0,), (0,)), ((), ()))


def turn(product, period):
    angle = 2.0 * np.pi * (product % period) / period
    return np.cos(angle), np.sin(angle)


def bf16_table(values):
    return np.asarray(values, np.float32).astype(jnp.bfloat16)


@functools.lru_cache(None)
def column_twiddle():
    cos, sin = turn(np.arange(8)[:, None] * np.arange(256)[None, :], 2048)
    return np.concatenate([cos, sin]).astype(np.float32)


@functools.lru_cache(None)
def column_tables():
    freq = 2 * np.arange(128)[:, None] + np.arange(2)[None, :]
    cos, sin = turn(freq[:, :, None] * np.arange(256), 256)
    ahead = np.zeros((128, 2, 2, 2, 256))
    ahead[:, 0, :, 0] = cos
    ahead[:, 0, :, 1] = sin
    ahead[:, 1, :, 0] = -sin
    ahead[:, 1, :, 1] = cos
    back = np.zeros((128, 2, 2, 2, 256))
    back[:, 0, :, 0] = cos
    back[:, 1, :, 0] = -sin
    back[:, 0, :, 1] = sin
    back[:, 1, :, 1] = cos
    return bf16_table(ahead.reshape(512, 512)), bf16_table(back.reshape(512, 512))


@functools.lru_cache(None)
def row_block_tables():
    cos, sin = turn(np.arange(16)[:, None] * np.arange(16), 16)
    ahead = np.zeros((2, 2, 2, 16, 16, 2, 2, 2))
    for kappa in range(2):
        for jhi in range(2):
            ahead[0, kappa, jhi, :, :, jhi, 0, kappa] = cos
            ahead[0, kappa, jhi, :, :, jhi, 1, kappa] = sin
            ahead[1, kappa, jhi, :, :, jhi, 0, kappa] = -sin
            ahead[1, kappa, jhi, :, :, jhi, 1, kappa] = cos
    ahead = ahead.reshape(128, 128)
    return bf16_table(ahead), bf16_table(ahead.T / IMAGE)


@functools.lru_cache(None)
def row_forward_tables():
    pos = np.arange(128)
    cos, sin = turn(np.arange(16)[:, None] * pos, 2048)
    twiddle = np.concatenate([cos, sin]).astype(np.float32)
    cos, sin = turn(pos[:, None] * np.arange(128), 128)
    return twiddle, bf16_table(np.concatenate([cos, sin], 1))


@functools.lru_cache(None)
def row_inverse_tables(window, lead):
    pos = (16 * np.arange(8)[:, None] + np.arange(window)[None, :] - lead).reshape(-1)
    cos, sin = turn(np.arange(16)[:, None] * pos, 2048)
    twiddle = np.concatenate([cos, sin]).astype(np.float32)
    cos, sin = turn(np.arange(128)[:, None] * pos, 128)
    return twiddle, bf16_table(np.concatenate([cos, sin], 1))


@functools.lru_cache(None)
def sum_tables():
    spread = np.zeros((128, 10, 64))
    share = np.zeros((128, 10, 32))
    gather = np.zeros((16, 128, 10))
    collect = np.zeros((32, 128, 10))
    for d in range(128):
        spread[d, 8, d % 32] = 1.0
        spread[d, 9, 32 + d % 32] = 1.0
    share[:, 8, 0] = 1.0
    share[:, 9, 16] = 1.0
    gather[:, :, 8:] = 1.0
    for c in range(32):
        collect[c, c, 8:] = 1.0
    return (
        bf16_table(spread.reshape(1280, 64)),
        bf16_table(gather.reshape(16, 1280)),
        bf16_table(share.reshape(1280, 32)),
        bf16_table(collect.reshape(32, 1280)),
    )


@functools.lru_cache(None)
def weight_tables():
    first = np.zeros((4, 4, 256))
    second = np.zeros((3, 2, 128))
    back = np.zeros((3, 4, 192))
    rows = np.full((8, 256), 99)
    fold = np.zeros((3, 384, 128), np.float32)
    for q in range(3):
        for i in range(4):
            at = 128 * (i // 2) + 20 * (3 * (i % 2) + q)
            rows[:, at : at + 20] = np.arange(20)
            first[q, i, at : at + 20] = 1.0
            back[q, i, q * 64 + i * 16 : q * 64 + i * 16 + 16] = 1.0
            for p in range(3):
                fold[p, at : at + 20, (p * 3 + q) * 4 + i] = 1.0
        for o in range(2):
            at = 20 * (3 * o + q)
            second[q, o, at : at + 20] = 1.0
            for e in range(3):
                to = 36 + ((2 - e) * 3 + 2 - q) * 2 + o
                fold[e, 256 + at : 276 + at, to] = 1.0
    rows[:, 120] = -1
    for i in range(3):
        first[3, i, 120 + i] = 1.0
    fold[0, 120, 54] = 1.0
    return (
        first.astype(np.float32),
        second.astype(np.float32),
        back.astype(np.float32),
        rows.astype(np.int32),
        bf16_table(fold),
    )


def columns_ahead(z, twiddle_ref, table_ref):
    root = float(np.sqrt(0.5))
    s04, d04 = z[0] + z[4], z[0] - z[4]
    s26, d26 = z[2] + z[6], z[2] - z[6]
    s15, d15 = z[1] + z[5], z[1] - z[5]
    s37, d37 = z[3] + z[7], z[3] - z[7]
    low, high = root * (d15 - d37), root * (d15 + d37)
    real = [None] * 8
    imag = [None] * 8
    even, odd = s04 + s26, s15 + s37
    real[0], real[4] = even + odd, even - odd
    real[2], imag[2] = s04 - s26, s37 - s15
    real[1], imag[1] = d04 + low, -d26 - high
    real[3], imag[3] = d04 - low, d26 - high
    for j in (1, 2, 3):
        real[8 - j], imag[8 - j] = real[j], -imag[j]
    groups = []
    for j in range(8):
        cos, sin = twiddle_ref[j : j + 1, :], twiddle_ref[8 + j : 9 + j, :]
        if imag[j] is None:
            pieces = [real[j] * cos, -real[j] * sin]
        else:
            pieces = [real[j] * cos + imag[j] * sin, imag[j] * cos - real[j] * sin]
        groups.append(jnp.concatenate(pieces, axis=1).astype(BF16))
    values = lax.dot_general(
        table_ref[...], jnp.concatenate(groups, axis=0), NT, preferred_element_type=F32
    )
    low, high = (values[:, at : at + 128].reshape(64, 8, 128) for at in (0, 128))
    sub = lax.broadcasted_iota(jnp.int32, (64, 8, 128), 1)
    return (
        jnp.where(sub < 4, low, pltpu.roll(high, 4, 1)),
        jnp.where(sub < 4, pltpu.roll(low, 4, 1), high),
    )


def regroup(even, odd):
    sub = lax.broadcasted_iota(jnp.int32, even.shape, 1)
    shape = (512, even.shape[2])
    first = jnp.where(sub < 4, even, pltpu.roll(odd, 4, 1))
    second = jnp.where(sub < 4, pltpu.roll(even, 4, 1), odd)
    return jnp.concatenate([first.reshape(shape), second.reshape(shape)], 1).astype(BF16)


def spaced(chunks):
    gap = jnp.zeros((chunks[0].shape[0], 2, 128), F32)
    pieces = []
    for value in chunks:
        pieces += [value, gap]
    return jnp.concatenate(pieces, 1)


def unspaced(rows):
    rows = rows.astype(F32).reshape(32, 40, 128)
    return [rows[:, 10 * j : 10 * j + 8] for j in range(4)]


def columns_back(rows_of, twiddle_ref):
    real = [None] * 8
    imag = [None] * 8
    for j in range(8):
        rows = rows_of(j)
        re, im = rows[:, :256], rows[:, 256:]
        cos, sin = twiddle_ref[j : j + 1, :], twiddle_ref[8 + j : 9 + j, :]
        real[j] = re * cos - im * sin
        imag[j] = re * sin + im * cos
    fold_re = [real[0]] + [real[j] + real[8 - j] for j in (1, 2, 3)] + [real[4]]
    fold_im = [None] + [imag[j] - imag[8 - j] for j in (1, 2, 3)]
    scale = 1.0 / IMAGE
    root = float(np.sqrt(0.5)) * scale
    base_even = (fold_re[0] + fold_re[4]) * scale
    base_odd = (fold_re[0] - fold_re[4]) * scale
    re2, im2 = fold_re[2] * scale, fold_im[2] * scale
    sum_re, dif_re = fold_re[1] + fold_re[3], fold_re[1] - fold_re[3]
    sum_im, dif_im = fold_im[1] + fold_im[3], fold_im[1] - fold_im[3]
    cross = root * (dif_re - sum_im), root * (dif_re + sum_im)
    return [
        base_even + re2 + sum_re * scale,
        base_odd - im2 + cross[0],
        base_even - re2 - dif_im * scale,
        base_odd + im2 - cross[1],
        base_even + re2 - sum_re * scale,
        base_odd - im2 - cross[0],
        base_even - re2 + dif_im * scale,
        base_odd + im2 + cross[1],
    ]


def swap_blocks(arrays, size):
    arrays = list(arrays)
    count = 128 // size
    lane = lax.broadcasted_iota(jnp.int32, arrays[0].shape, 1)
    step = count // 2
    while step:
        low = (lane & (step * size)) == 0
        for i in range(count):
            if not i & step:
                one, two = arrays[i], arrays[i + step]
                arrays[i] = jnp.where(low, one, pltpu.roll(two, step * size, 1))
                arrays[i + step] = jnp.where(low, pltpu.roll(one, 128 - step * size, 1), two)
        step //= 2
    return arrays


def halves(values):
    high = values.astype(BF16)
    return high, (values - high.astype(F32)).astype(BF16)


def ahead_body(strip_ref, twiddle_ref, table_ref, out_ref):
    z = [strip_ref[c, 0:2].astype(F32).reshape(32, 256) for c in range(8)]
    even, odd = columns_ahead(z, twiddle_ref, table_ref)
    out_ref[...] = jnp.stack([even, odd], 1).reshape(1024, 128).astype(BF16)


def middle_body(window, summing, *refs):
    in_ref, spectra_ref, ahead_ref, back_ref, row_ref, back_row_ref, tw_ref, back_tw_ref = refs[:8]
    out_ref = refs[-1]
    chunks = in_ref[...]
    if summing:
        fours = [part.reshape(16, 2, 8, 128) for part in unspaced(chunks)]
        rows = [fours[c % 4][:, c // 4].reshape(128, 128) for c in range(8)]
    else:
        rows = chunks.astype(F32).reshape(16, 8, 8, 128)
        rows = [rows[:, c].reshape(128, 128) for c in range(8)]
    rows = jnp.concatenate(rows, 1).astype(BF16)
    first = jnp.dot(ahead_ref[...], rows, preferred_element_type=F32)
    per_m = swap_blocks([first[:, 128 * c : 128 * c + 128] for c in range(8)], 16)
    cos, sin = tw_ref[0:16, :], tw_ref[16:32, :]
    rows = []
    for m in range(8):
        real = per_m[m][:64].reshape(4, 16, 128)
        imag = per_m[m][64:].reshape(4, 16, 128)
        rows.append((real * cos + imag * sin).astype(BF16).reshape(64, 128))
        rows.append((imag * cos - real * sin).astype(BF16).reshape(64, 128))
    second = jnp.dot(jnp.concatenate(rows, 0), row_ref[...], preferred_element_type=F32)
    rows = []
    for jlo in range(4):
        full_re, full_im = [], []
        for plane in range(2):
            m = 2 * jlo + plane
            part = second[128 * m : 128 * m + 128]
            full_re.append(part[:64, :128] + part[64:, 128:])
            full_im.append(part[64:, :128] - part[:64, 128:])
        weights = [
            spectra_ref[t].reshape(4, 4, 16, 128)[:, jlo].reshape(64, 128) for t in range(3)
        ]
        for plane in range(2):
            for part in (full_re, full_im):
                mixed = weights[plane] * part[0] + weights[plane + 1] * part[1]
                rows.append(mixed.astype(BF16))
    third = jnp.dot(jnp.concatenate(rows, 0), back_row_ref[...], preferred_element_type=F32)
    half = 8 * window
    cos, sin = back_tw_ref[0:16, :], back_tw_ref[16:32, :]
    per_m = []
    for m in range(8):
        part = third[128 * m : 128 * m + 128]
        real = (part[:64, :half] - part[64:, half:]).reshape(4, 16, half)
        imag = (part[64:, :half] + part[:64, half:]).reshape(4, 16, half)
        per_m.append(
            jnp.concatenate(
                [
                    (real * cos - imag * sin).reshape(64, half),
                    (real * sin + imag * cos).reshape(64, half),
                ],
                0,
            )
        )
    count = 128 // window
    tiles = 8 // count
    per_c = [[None] * tiles for _ in range(8)]
    for m_hi in range(tiles):
        for c_hi in range(tiles):
            cols = slice(128 * c_hi, 128 * c_hi + 128)
            group = [per_m[m_hi * count + i][:, cols] for i in range(count)]
            for i, value in enumerate(swap_blocks(group, window)):
                per_c[c_hi * count + i][m_hi] = value
    rows = jnp.concatenate([tile for v in per_c for tile in v], 1).astype(BF16)
    out = jnp.dot(back_ref[...], rows, preferred_element_type=F32)
    out = [out[:, half * c : half * c + half].reshape(16, 8, half) for c in range(8)]
    if summing:
        gather_ref, share_ref = refs[8:10]
        total = jnp.dot(gather_ref[...], chunks, preferred_element_type=F32)
        out = jnp.stack([spaced(out[:4]), spaced(out[4:])], 1).reshape(1280, 128)
        out = out + jnp.dot(
            share_ref[...], jnp.concatenate(halves(total), 0), preferred_element_type=F32
        )
    else:
        out = jnp.stack(out, 1).reshape(1024, half)
    out_ref[...] = out.astype(BF16)


def shifted(value, q):
    if q == 1:
        return value
    lane = lax.broadcasted_iota(jnp.int32, value.shape, 1)
    if q == 0:
        return jnp.where(lane == 0, 0.0, pltpu.roll(value, 1, 1))
    return jnp.where(lane == IMAGE - 1, 0.0, pltpu.roll(value, IMAGE - 1, 1))


def banded(weights, window_row):
    rows = []
    for r in range(GRAD_ROWS):
        total = jnp.zeros(weights[0].shape, F32)
        for p in range(3):
            total = total + jnp.where(window_row == r + p, weights[p], 0.0)
        rows.append(total)
    return jnp.concatenate(rows, 0)


def prepare(
    strip_ref,
    above_ref,
    below_ref,
    w_first_ref,
    w_second_ref,
    bias_ref,
    first_table_ref,
    second_table_ref,
    back_table_ref,
    rows_ref,
    features_ref,
    cot_ref,
    dirty_ref,
    weights_ref,
    tall_ref,
    stack_ref,
):
    row = lax.broadcasted_iota(jnp.int32, (128, IMAGE), 0)
    tall_ref[...] = jnp.zeros_like(tall_ref)
    for i in range(6):
        for c in range(8):
            cols = slice(256 * c, 256 * c + 256)
            tall_ref[0:2, cols] = above_ref[c, i].astype(F32)
            tall_ref[2:18, cols] = strip_ref[c, i].astype(F32)
            tall_ref[18:20, cols] = below_ref[c, i].astype(F32)
        value = tall_ref[...]
        if i in (2, 3):
            dirty_ref[i - 2] = value
        else:
            for q in range(3):
                at = 20 * (3 * (i % 2) + q)
                stack_ref[at : at + 20, :] = shifted(value, q)[0:20]
            if i == 1:
                out = jnp.where(row < 120, stack_ref[...], jnp.where(row < 123, 1.0, 0.0))
                features_ref[0:128, :] = out.astype(BF16)
            if i == 5:
                cot_ref[...] = jnp.where(row < 120, stack_ref[...], 0.0).astype(BF16)
    rows = rows_ref[0:1, :]

    def spread(weights, table):
        return lax.dot_general(weights, table, TN, preferred_element_type=F32)

    def parts_of(source_ref, table_ref):
        return [
            sum(spread(source_ref[p, q].astype(F32), table_ref[q]) for q in range(3))
            for p in range(3)
        ]

    bias = bias_ref[...]
    high = bias.astype(BF16).astype(F32)
    middle = (bias - high).astype(BF16).astype(F32)
    pieces = jnp.concatenate([high, middle, bias - high - middle, jnp.zeros_like(bias)], 0)
    offset = spread(pieces, first_table_ref[3])
    first = banded(parts_of(w_first_ref, first_table_ref), rows)
    weights_ref[:, 0:256] = (first + jnp.concatenate([offset] * GRAD_ROWS, 0)).astype(BF16)
    parts = [
        sum(spread(w_second_ref[2 - e, 2 - q].astype(F32), second_table_ref[q]) for q in range(3))
        for e in range(3)
    ]
    weights_ref[:, 256:384] = banded(parts, rows[:, :128]).astype(BF16)
    parts = parts_of(w_first_ref, back_table_ref)
    rows = lax.broadcasted_iota(jnp.int32, (1, 192), 1) & 15
    parts = [parts[2 - p] for p in range(3)]
    weights_ref[:, 384:576] = banded_back(parts, rows).astype(BF16)


def banded_back(parts, rows):
    blocks = []
    for r in range(GRAD_ROWS):
        total = jnp.zeros(parts[0].shape, F32)
        for k in range(3):
            total = total + jnp.where(rows == r - k, parts[k], 0.0)
        blocks.append(total)
    return jnp.concatenate(blocks, 0)


def network_body(
    place_ref,
    in_ref,
    strip_ref,
    above_ref,
    below_ref,
    w_first_ref,
    w_second_ref,
    bias_ref,
    first_table_ref,
    second_table_ref,
    back_table_ref,
    twiddle_ref,
    inverse_ref,
    forward_ref,
    spread_ref,
    rows_ref,
    fold_ref,
    base_ref,
    out_ref,
    stack_ref,
    features_ref,
    spread_grad_ref,
    acc_first_ref,
    acc_second_ref,
    back_ref,
    cot_ref,
    dirty_ref,
    weights_ref,
    tall_ref,
):
    prepare(
        strip_ref,
        above_ref,
        below_ref,
        w_first_ref,
        w_second_ref,
        bias_ref,
        first_table_ref,
        second_table_ref,
        back_table_ref,
        rows_ref,
        features_ref,
        cot_ref,
        dirty_ref,
        weights_ref,
        tall_ref,
        stack_ref,
    )
    place = place_ref[0]
    chunks = in_ref[...].astype(F32).reshape(64, 2, 8, 256)
    values = lax.dot_general(
        regroup(chunks[:, 0], chunks[:, 1]), inverse_ref[...], TN, preferred_element_type=F32
    )
    row = lax.broadcasted_iota(jnp.int32, (HOLD, IMAGE), 0)
    inside = ((row >= 2) | (place > 0)) & ((row < 18) | (place < DEVS - 1))
    for plane in range(2):
        blocks = columns_back(
            lambda j: values[64 * j + 32 * plane : 64 * j + 32 * plane + HOLD], twiddle_ref
        )
        blurred = jnp.concatenate(blocks, 1).astype(BF16).astype(F32)
        residual = dirty_ref[plane] - jnp.where(inside, blurred, 0.0)
        residual = residual.astype(BF16).astype(F32)
        for q in range(3):
            at = 20 * (3 * plane + q)
            stack_ref[at : at + 20, :] = shifted(residual, q)[0:20]
    stack_ref[120:128, :] = jnp.zeros((8, IMAGE), F32)
    features_ref[128:256, :] = stack_ref[...].astype(BF16)
    back_ref[...] = weights_ref[:, 384:576].astype(F32).T.astype(BF16)
    acc_first_ref[...] = jnp.zeros_like(acc_first_ref)
    acc_second_ref[...] = jnp.zeros_like(acc_second_ref)
    top = jnp.where(place > 0, 1.0, 0.0)
    bottom = jnp.where(place < DEVS - 1, 1.0, 0.0)

    def block(step, carry):
        cols = pl.ds(pl.multiple_of(step * 256, 256), 256)
        features = features_ref[:, cols]
        cots = cot_ref[:, cols]
        preact = jnp.dot(weights_ref[:, 0:256], features, preferred_element_type=F32)
        back = jnp.dot(weights_ref[:, 256:384], cots, preferred_element_type=F32)
        gate = 0.5 * jnp.tanh(0.5 * preact) + 0.5
        hidden = preact * gate
        grad_pre = back * (gate + hidden * (1.0 - gate))
        grad_pre = jnp.concatenate(
            [grad_pre[0:32] * top, grad_pre[32:544], grad_pre[544:576] * bottom], 0
        ).astype(BF16)
        spread_grad_ref[:, cols] = jnp.dot(back_ref[...], grad_pre, preferred_element_type=F32)
        acc_first_ref[...] += lax.dot_general(grad_pre, features, NT, preferred_element_type=F32)
        acc_second_ref[...] += lax.dot_general(
            hidden.astype(BF16), cots, NT, preferred_element_type=F32
        )
        return carry

    lax.fori_loop(0, 8, block, 0)

    cot_sums = []
    z = [[None, None] for _ in range(8)]
    for i in range(4):
        rows = [spread_grad_ref[64 * q + 16 * i : 64 * q + 16 * i + 16, :] for q in range(3)]
        total = shifted(rows[0], 2) + rows[1] + shifted(rows[2], 0)
        for c in range(8):
            part = total[:, 256 * c : 256 * c + 256]
            if i < 2:
                base_ref[c, i] = part + strip_ref[c, 4 + i].astype(F32)
            else:
                z[c][i - 2] = part.astype(BF16).astype(F32)
    for i in range(2):
        total = strip_ref[0, 4 + i].astype(F32)
        for c in range(1, 8):
            total = total + strip_ref[c, 4 + i].astype(F32)
        cot_sums.append(total.sum(axis=0, keepdims=True).sum(axis=1, keepdims=True))

    rows = rows_ref[0:1, :]
    parts = [jnp.zeros((HIDDEN, 384), F32) for _ in range(3)]
    for r in range(1, 17):
        of_first = acc_first_ref[32 * r : 32 * r + 32, :]
        of_second = acc_second_ref[32 * r : 32 * r + 32, :]
        for p in range(3):
            keep = (rows == r + p) | (rows == -1)
            parts[p] = parts[p] + jnp.concatenate(
                [
                    jnp.where(keep, of_first, 0.0),
                    jnp.where(rows[:, :128] == r + p, of_second, 0.0),
                ],
                1,
            )
    sums = jnp.zeros((HIDDEN, 128), F32)
    for p in range(3):
        sums = sums + jnp.dot(
            parts[p],
            fold_ref[p].astype(F32),
            precision=lax.Precision.HIGHEST,
            preferred_element_type=F32,
        )
    at = lax.broadcasted_iota(jnp.int32, (HIDDEN, 128), 1)
    of = lax.broadcasted_iota(jnp.int32, (HIDDEN, 128), 0)
    for i in range(2):
        sums = jnp.where((at == 55) & (of == i), cot_sums[i], sums)

    even, odd = columns_ahead([jnp.concatenate(v, 0) for v in z], twiddle_ref, forward_ref)
    even, odd = even.reshape(32, 2, 8, 128), odd.reshape(32, 2, 8, 128)
    out = spaced([even[:, 0], odd[:, 0], even[:, 1], odd[:, 1]]).reshape(1280, 128)
    out = out + jnp.dot(
        spread_ref[...], jnp.concatenate(halves(sums), 0), preferred_element_type=F32
    )
    out_ref[...] = out.astype(BF16)


def finish_body(
    in_ref,
    base_ref,
    twiddle_ref,
    inverse_ref,
    collect_ref,
    out_ref,
    first_ref,
    first_bias_ref,
    second_ref,
    second_bias_ref,
):
    chunks = in_ref[...]
    sums = jnp.dot(collect_ref[...], chunks, preferred_element_type=F32) * (1.0 / IMAGE)
    sums = sums.T
    for p in range(3):
        for q in range(3):
            at = 3 * p + q
            first_ref[p, q] = sums[4 * at : 4 * at + 4]
            second_ref[p, q] = sums[36 + 2 * at : 38 + 2 * at]
    first_bias_ref[...] = sums[54:55]
    second_bias_ref[...] = sums[55:56, 0:2]
    fours = unspaced(chunks)
    even = jnp.stack([fours[0], fours[2]], 1).reshape(64, 8, 128)
    odd = jnp.stack([fours[1], fours[3]], 1).reshape(64, 8, 128)
    values = lax.dot_general(
        regroup(even, odd), inverse_ref[...], TN, preferred_element_type=F32
    )
    blocks = columns_back(lambda j: values[32 * j : 32 * j + 32], twiddle_ref)
    for c in range(8):
        blurred = blocks[c].astype(BF16).astype(F32).reshape(2, STRIP, 256)
        out_ref[c] = base_ref[c] - blurred


def call(body, outs, *args, scratch=(), scalars=0, after=(), cost=2):
    whole = pl.BlockSpec(memory_space=pltpu.VMEM)
    return pl.pallas_call(
        body,
        out_shape=outs,
        in_specs=[pl.BlockSpec(memory_space=pltpu.SMEM)] * scalars
        + [whole] * (len(args) - scalars)
        + [pl.BlockSpec(memory_space=pl.ANY)] * len(after),
        out_specs=jax.tree.map(lambda _: whole, outs),
        scratch_shapes=list(scratch),
        compiler_params=pltpu.CompilerParams(vmem_limit_bytes=VM * 1024 * 1024),
        cost_estimate=pl.CostEstimate(
            flops=cost * 10**9, bytes_accessed=cost * 10**6, transcendentals=0
        ),
    )(*args, *after)


def like(*shape, dtype=BF16):
    return jax.ShapeDtypeStruct(shape, dtype)


def exchange(chunks, per):
    width = chunks.shape[-1]
    rows = 8 if per == 8 else 2
    moved = lax.all_to_all(chunks.reshape(DEVS * per // rows, rows, width), RC, 0, 0, tiled=True)
    return moved.reshape(DEVS * per, width)


def middle(chunks, spectra, window, lead, per, after=()):
    ahead, back = row_block_tables()
    twiddle, row_table = row_forward_tables()
    back_twiddle, back_row = row_inverse_tables(window, lead)
    extra = sum_tables()[1:3] if per == 10 else ()
    return call(
        functools.partial(middle_body, window, per == 10),
        like(DEVS * per, 8 * window),
        chunks,
        spectra,
        ahead,
        back,
        row_table,
        back_row,
        twiddle,
        back_twiddle,
        *extra,
        after=after,
    )


def shards(estimate, dirty_image, psf_spectra, w_first, b_first, w_second, cotangent):
    cells = jnp.stack([v.reshape(2, 8, STRIP, 256) for v in (estimate, dirty_image, cotangent)])
    cells = cells.transpose(2, 0, 1, 3, 4).reshape(8, 6, STRIP, 256)
    strip = lax.all_to_all(cells, "col", 0, 0, tiled=True)
    spec = call(
        ahead_body, like(1024, 128), strip, column_twiddle(), column_tables()[0]
    )
    spec = exchange(spec, 8)
    above = lax.ppermute(strip[:, :, -2:], RC, [(d, d + 1) for d in range(DEVS - 1)])
    below = lax.ppermute(strip[:, :, :2], RC, [(d + 1, d) for d in range(DEVS - 1)])
    first_table, second_table, back_table, row_of, fold = weight_tables()
    mixed = exchange(middle(spec, psf_spectra, 32, 2, 8, ()), 8)
    place = (lax.axis_index("row") * 8 + lax.axis_index("col")).astype(jnp.int32).reshape(1)
    base, spec = call(
        network_body,
        (like(8, 2, STRIP, 256, dtype=F32), like(1280, 128)),
        place,
        mixed,
        strip,
        above,
        below,
        w_first.transpose(2, 3, 1, 0),
        w_second.transpose(2, 3, 0, 1),
        b_first.reshape(1, 32),
        first_table,
        second_table,
        back_table,
        column_twiddle(),
        column_tables()[1],
        column_tables()[0],
        sum_tables()[0],
        row_of,
        fold,
        scratch=[
            pltpu.VMEM((128, IMAGE), F32),
            pltpu.VMEM((256, IMAGE), BF16),
            pltpu.VMEM((192, IMAGE), F32),
            pltpu.VMEM((576, 256), F32),
            pltpu.VMEM((576, 128), F32),
            pltpu.VMEM((192, 576), BF16),
            pltpu.VMEM((128, IMAGE), BF16),
            pltpu.VMEM((2, HOLD, IMAGE), F32),
            pltpu.VMEM((576, 576), BF16),
            pltpu.VMEM((HOLD, IMAGE), F32),
        ],
        scalars=1,
        cost=8,
    )
    mixed = exchange(middle(exchange(spec, 10), psf_spectra, 16, 0, 10), 10)
    image, grad_first, first_bias, grad_second, second_bias = call(
        finish_body,
        (
            like(8, 2, STRIP, 256, dtype=F32),
            like(3, 3, 4, 32, dtype=F32),
            like(1, 32, dtype=F32),
            like(3, 3, 2, 32, dtype=F32),
            like(1, 2, dtype=F32),
        ),
        mixed,
        base,
        column_twiddle(),
        column_tables()[1],
        sum_tables()[3],
    )
    image = lax.all_to_all(image, "col", 0, 0, tiled=True)
    grad_image = image.transpose(1, 0, 2, 3).reshape(2, 128, 256)
    return (
        grad_image,
        grad_first.transpose(3, 2, 0, 1),
        first_bias.reshape(32),
        grad_second.transpose(2, 3, 0, 1),
        second_bias.reshape(2),
    )


def solution(mesh):
    return jax.shard_map(
        shards,
        mesh=mesh,
        in_specs=(
            P(None, "row", "col"),
            P(None, "row", "col"),
            P(None, ("row", "col"), None, None),
            P(),
            P(),
            P(),
            P(None, "row", "col"),
        ),
        out_specs=(P(None, "row", "col"), P(), P(), P(), P()),
        check_vma=False,
    )
```

```python
import functools

import jax
import jax.numpy as jnp
import numpy as np
from jax import lax
from jax.experimental import pallas as pl
from jax.experimental.pallas import tpu as pltpu
from jax.sharding import PartitionSpec as P

IMAGE = 2048
DEVS = 128
VM = 20
STRIP = 16
REACH = 20
HOLD = 24
GRAD_ROWS = 18
HIDDEN = 32
RC = ("row", "col")
F32 = jnp.float32
BF16 = jnp.bfloat16
NT = (((1,), (1,)), ((), ()))
TN = (((0,), (0,)), ((), ()))


def turn(product, period):
    angle = 2.0 * np.pi * (product % period) / period
    return np.cos(angle), np.sin(angle)


def bf16_table(values):
    return np.asarray(values, np.float32).astype(jnp.bfloat16)


@functools.lru_cache(None)
def column_twiddle():
    cos, sin = turn(np.arange(8)[:, None] * np.arange(256)[None, :], 2048)
    return np.concatenate([cos, sin]).astype(np.float32)


@functools.lru_cache(None)
def column_tables():
    freq = 2 * np.arange(128)[:, None] + np.arange(2)[None, :]
    cos, sin = turn(freq[:, :, None] * np.arange(256), 256)
    ahead = np.zeros((128, 2, 2, 2, 256))
    ahead[:, 0, :, 0] = cos
    ahead[:, 0, :, 1] = sin
    ahead[:, 1, :, 0] = -sin
    ahead[:, 1, :, 1] = cos
    back = np.zeros((128, 2, 2, 2, 256))
    back[:, 0, :, 0] = cos
    back[:, 1, :, 0] = -sin
    back[:, 0, :, 1] = sin
    back[:, 1, :, 1] = cos
    return bf16_table(ahead.reshape(512, 512)), bf16_table(back.reshape(512, 512))


@functools.lru_cache(None)
def row_block_tables():
    cos, sin = turn(np.arange(16)[:, None] * np.arange(16), 16)
    ahead = np.zeros((2, 2, 2, 16, 16, 2, 2, 2))
    for kappa in range(2):
        for jhi in range(2):
            ahead[0, kappa, jhi, :, :, jhi, 0, kappa] = cos
            ahead[0, kappa, jhi, :, :, jhi, 1, kappa] = sin
            ahead[1, kappa, jhi, :, :, jhi, 0, kappa] = -sin
            ahead[1, kappa, jhi, :, :, jhi, 1, kappa] = cos
    ahead = ahead.reshape(128, 128)
    return bf16_table(ahead), bf16_table(ahead.T / IMAGE)


@functools.lru_cache(None)
def row_forward_tables():
    pos = np.arange(128)
    cos, sin = turn(np.arange(16)[:, None] * pos, 2048)
    twiddle = np.concatenate([cos, sin]).astype(np.float32)
    cos, sin = turn(pos[:, None] * np.arange(128), 128)
    return twiddle, bf16_table(np.concatenate([cos, sin], 1))


@functools.lru_cache(None)
def row_inverse_tables(window, lead):
    pos = (16 * np.arange(8)[:, None] + np.arange(window)[None, :] - lead).reshape(-1)
    cos, sin = turn(np.arange(16)[:, None] * pos, 2048)
    twiddle = np.concatenate([cos, sin]).astype(np.float32)
    cos, sin = turn(np.arange(128)[:, None] * pos, 128)
    return twiddle, bf16_table(np.concatenate([cos, sin], 1))


@functools.lru_cache(None)
def sum_tables():
    spread = np.zeros((128, 10, 64))
    share = np.zeros((128, 10, 32))
    gather = np.zeros((16, 128, 10))
    collect = np.zeros((32, 128, 10))
    for d in range(128):
        spread[d, 8, d % 32] = 1.0
        spread[d, 9, 32 + d % 32] = 1.0
    share[:, 8, 0] = 1.0
    share[:, 9, 16] = 1.0
    gather[:, :, 8:] = 1.0
    for c in range(32):
        collect[c, c, 8:] = 1.0
    return (
        bf16_table(spread.reshape(1280, 64)),
        bf16_table(gather.reshape(16, 1280)),
        bf16_table(share.reshape(1280, 32)),
        bf16_table(collect.reshape(32, 1280)),
    )


@functools.lru_cache(None)
def weight_tables():
    first = np.zeros((4, 4, 256))
    second = np.zeros((3, 2, 128))
    back = np.zeros((3, 4, 192))
    rows = np.full((8, 256), 99)
    fold = np.zeros((3, 384, 128), np.float32)
    for q in range(3):
        for i in range(4):
            at = 128 * (i // 2) + 20 * (3 * (i % 2) + q)
            rows[:, at : at + 20] = np.arange(20)
            first[q, i, at : at + 20] = 1.0
            back[q, i, q * 64 + i * 16 : q * 64 + i * 16 + 16] = 1.0
            for p in range(3):
                fold[p, at : at + 20, (p * 3 + q) * 4 + i] = 1.0
        for o in range(2):
            at = 20 * (3 * o + q)
            second[q, o, at : at + 20] = 1.0
            for e in range(3):
                to = 36 + ((2 - e) * 3 + 2 - q) * 2 + o
                fold[e, 256 + at : 276 + at, to] = 1.0
    rows[:, 120] = -1
    for i in range(3):
        first[3, i, 120 + i] = 1.0
    fold[0, 120, 54] = 1.0
    return (
        first.astype(np.float32),
        second.astype(np.float32),
        back.astype(np.float32),
        rows.astype(np.int32),
        bf16_table(fold),
    )


def columns_ahead(z, twiddle_ref, table_ref):
    root = float(np.sqrt(0.5))
    s04, d04 = z[0] + z[4], z[0] - z[4]
    s26, d26 = z[2] + z[6], z[2] - z[6]
    s15, d15 = z[1] + z[5], z[1] - z[5]
    s37, d37 = z[3] + z[7], z[3] - z[7]
    low, high = root * (d15 - d37), root * (d15 + d37)
    real = [None] * 8
    imag = [None] * 8
    even, odd = s04 + s26, s15 + s37
    real[0], real[4] = even + odd, even - odd
    real[2], imag[2] = s04 - s26, s37 - s15
    real[1], imag[1] = d04 + low, -d26 - high
    real[3], imag[3] = d04 - low, d26 - high
    for j in (1, 2, 3):
        real[8 - j], imag[8 - j] = real[j], -imag[j]
    groups = []
    for j in range(8):
        cos, sin = twiddle_ref[j : j + 1, :], twiddle_ref[8 + j : 9 + j, :]
        if imag[j] is None:
            pieces = [real[j] * cos, -real[j] * sin]
        else:
            pieces = [real[j] * cos + imag[j] * sin, imag[j] * cos - real[j] * sin]
        groups.append(jnp.concatenate(pieces, axis=1).astype(BF16))
    values = lax.dot_general(
        table_ref[...], jnp.concatenate(groups, axis=0), NT, preferred_element_type=F32
    )
    low, high = (values[:, at : at + 128].reshape(64, 8, 128) for at in (0, 128))
    sub = lax.broadcasted_iota(jnp.int32, (64, 8, 128), 1)
    return (
        jnp.where(sub < 4, low, pltpu.roll(high, 4, 1)),
        jnp.where(sub < 4, pltpu.roll(low, 4, 1), high),
    )


def regroup(even, odd):
    sub = lax.broadcasted_iota(jnp.int32, even.shape, 1)
    shape = (512, even.shape[2])
    first = jnp.where(sub < 4, even, pltpu.roll(odd, 4, 1))
    second = jnp.where(sub < 4, pltpu.roll(even, 4, 1), odd)
    return jnp.concatenate([first.reshape(shape), second.reshape(shape)], 1).astype(BF16)


def spaced(chunks):
    gap = jnp.zeros((chunks[0].shape[0], 2, 128), F32)
    pieces = []
    for value in chunks:
        pieces += [value, gap]
    return jnp.concatenate(pieces, 1)


def unspaced(rows):
    rows = rows.astype(F32).reshape(32, 40, 128)
    return [rows[:, 10 * j : 10 * j + 8] for j in range(4)]


def columns_back(rows_of, twiddle_ref):
    real = [None] * 8
    imag = [None] * 8
    for j in range(8):
        rows = rows_of(j)
        re, im = rows[:, :256], rows[:, 256:]
        cos, sin = twiddle_ref[j : j + 1, :], twiddle_ref[8 + j : 9 + j, :]
        real[j] = re * cos - im * sin
        imag[j] = re * sin + im * cos
    fold_re = [real[0]] + [real[j] + real[8 - j] for j in (1, 2, 3)] + [real[4]]
    fold_im = [None] + [imag[j] - imag[8 - j] for j in (1, 2, 3)]
    scale = 1.0 / IMAGE
    root = float(np.sqrt(0.5)) * scale
    base_even = (fold_re[0] + fold_re[4]) * scale
    base_odd = (fold_re[0] - fold_re[4]) * scale
    re2, im2 = fold_re[2] * scale, fold_im[2] * scale
    sum_re, dif_re = fold_re[1] + fold_re[3], fold_re[1] - fold_re[3]
    sum_im, dif_im = fold_im[1] + fold_im[3], fold_im[1] - fold_im[3]
    cross = root * (dif_re - sum_im), root * (dif_re + sum_im)
    return [
        base_even + re2 + sum_re * scale,
        base_odd - im2 + cross[0],
        base_even - re2 - dif_im * scale,
        base_odd + im2 - cross[1],
        base_even + re2 - sum_re * scale,
        base_odd - im2 - cross[0],
        base_even - re2 + dif_im * scale,
        base_odd + im2 + cross[1],
    ]


def swap_blocks(arrays, size):
    arrays = list(arrays)
    count = 128 // size
    lane = lax.broadcasted_iota(jnp.int32, arrays[0].shape, 1)
    step = count // 2
    while step:
        low = (lane & (step * size)) == 0
        for i in range(count):
            if not i & step:
                one, two = arrays[i], arrays[i + step]
                arrays[i] = jnp.where(low, one, pltpu.roll(two, step * size, 1))
                arrays[i + step] = jnp.where(low, pltpu.roll(one, 128 - step * size, 1), two)
        step //= 2
    return arrays


def halves(values):
    high = values.astype(BF16)
    return high, (values - high.astype(F32)).astype(BF16)


def ahead_body(strip_ref, twiddle_ref, table_ref, out_ref):
    z = [strip_ref[c, 0:2].astype(F32).reshape(32, 256) for c in range(8)]
    even, odd = columns_ahead(z, twiddle_ref, table_ref)
    out_ref[...] = jnp.stack([even, odd], 1).reshape(1024, 128).astype(BF16)


def middle_body(window, summing, *refs):
    in_ref, spectra_ref, ahead_ref, back_ref, row_ref, back_row_ref, tw_ref, back_tw_ref = refs[:8]
    out_ref = refs[-1]
    chunks = in_ref[...]
    if summing:
        fours = [part.reshape(16, 2, 8, 128) for part in unspaced(chunks)]
        rows = [fours[c % 4][:, c // 4].reshape(128, 128) for c in range(8)]
    else:
        rows = chunks.astype(F32).reshape(16, 8, 8, 128)
        rows = [rows[:, c].reshape(128, 128) for c in range(8)]
    rows = jnp.concatenate(rows, 1).astype(BF16)
    first = jnp.dot(ahead_ref[...], rows, preferred_element_type=F32)
    per_m = swap_blocks([first[:, 128 * c : 128 * c + 128] for c in range(8)], 16)
    cos, sin = tw_ref[0:16, :], tw_ref[16:32, :]
    rows = []
    for m in range(8):
        real = per_m[m][:64].reshape(4, 16, 128)
        imag = per_m[m][64:].reshape(4, 16, 128)
        rows.append((real * cos + imag * sin).astype(BF16).reshape(64, 128))
        rows.append((imag * cos - real * sin).astype(BF16).reshape(64, 128))
    second = jnp.dot(jnp.concatenate(rows, 0), row_ref[...], preferred_element_type=F32)
    rows = []
    for jlo in range(4):
        full_re, full_im = [], []
        for plane in range(2):
            m = 2 * jlo + plane
            part = second[128 * m : 128 * m + 128]
            full_re.append(part[:64, :128] + part[64:, 128:])
            full_im.append(part[64:, :128] - part[:64, 128:])
        weights = [
            spectra_ref[t].reshape(4, 4, 16, 128)[:, jlo].reshape(64, 128) for t in range(3)
        ]
        for plane in range(2):
            for part in (full_re, full_im):
                mixed = weights[plane] * part[0] + weights[plane + 1] * part[1]
                rows.append(mixed.astype(BF16))
    third = jnp.dot(jnp.concatenate(rows, 0), back_row_ref[...], preferred_element_type=F32)
    half = 8 * window
    cos, sin = back_tw_ref[0:16, :], back_tw_ref[16:32, :]
    per_m = []
    for m in range(8):
        part = third[128 * m : 128 * m + 128]
        real = (part[:64, :half] - part[64:, half:]).reshape(4, 16, half)
        imag = (part[64:, :half] + part[:64, half:]).reshape(4, 16, half)
        per_m.append(
            jnp.concatenate(
                [
                    (real * cos - imag * sin).reshape(64, half),
                    (real * sin + imag * cos).reshape(64, half),
                ],
                0,
            )
        )
    count = 128 // window
    tiles = 8 // count
    per_c = [[None] * tiles for _ in range(8)]
    for m_hi in range(tiles):
        for c_hi in range(tiles):
            cols = slice(128 * c_hi, 128 * c_hi + 128)
            group = [per_m[m_hi * count + i][:, cols] for i in range(count)]
            for i, value in enumerate(swap_blocks(group, window)):
                per_c[c_hi * count + i][m_hi] = value
    rows = jnp.concatenate([tile for v in per_c for tile in v], 1).astype(BF16)
    out = jnp.dot(back_ref[...], rows, preferred_element_type=F32)
    out = [out[:, half * c : half * c + half].reshape(16, 8, half) for c in range(8)]
    if summing:
        gather_ref, share_ref = refs[8:10]
        total = jnp.dot(gather_ref[...], chunks, preferred_element_type=F32)
        out = jnp.stack([spaced(out[:4]), spaced(out[4:])], 1).reshape(1280, 128)
        out = out + jnp.dot(
            share_ref[...], jnp.concatenate(halves(total), 0), preferred_element_type=F32
        )
    else:
        out = jnp.stack(out, 1).reshape(1024, half)
    out_ref[...] = out.astype(BF16)


def shifted(value, q):
    if q == 1:
        return value
    lane = lax.broadcasted_iota(jnp.int32, value.shape, 1)
    if q == 0:
        return jnp.where(lane == 0, 0.0, pltpu.roll(value, 1, 1))
    return jnp.where(lane == IMAGE - 1, 0.0, pltpu.roll(value, IMAGE - 1, 1))


def banded(weights, window_row):
    rows = []
    for r in range(GRAD_ROWS):
        total = jnp.zeros(weights[0].shape, F32)
        for p in range(3):
            total = total + jnp.where(window_row == r + p, weights[p], 0.0)
        rows.append(total)
    return jnp.concatenate(rows, 0)


def prepare(
    strip_ref,
    above_ref,
    below_ref,
    w_first_ref,
    w_second_ref,
    bias_ref,
    first_table_ref,
    second_table_ref,
    back_table_ref,
    rows_ref,
    features_ref,
    cot_ref,
    dirty_ref,
    weights_ref,
    tall_ref,
    stack_ref,
):
    row = lax.broadcasted_iota(jnp.int32, (128, IMAGE), 0)
    tall_ref[...] = jnp.zeros_like(tall_ref)
    for i in range(6):
        for c in range(8):
            cols = slice(256 * c, 256 * c + 256)
            tall_ref[0:2, cols] = above_ref[c, i].astype(F32)
            tall_ref[2:18, cols] = strip_ref[c, i].astype(F32)
            tall_ref[18:20, cols] = below_ref[c, i].astype(F32)
        value = tall_ref[...]
        if i in (2, 3):
            dirty_ref[i - 2] = value
        else:
            for q in range(3):
                at = 20 * (3 * (i % 2) + q)
                stack_ref[at : at + 20, :] = shifted(value, q)[0:20]
            if i == 1:
                out = jnp.where(row < 120, stack_ref[...], jnp.where(row < 123, 1.0, 0.0))
                features_ref[0:128, :] = out.astype(BF16)
            if i == 5:
                cot_ref[...] = jnp.where(row < 120, stack_ref[...], 0.0).astype(BF16)
    rows = rows_ref[0:1, :]

    def spread(weights, table):
        return lax.dot_general(weights, table, TN, preferred_element_type=F32)

    def parts_of(source_ref, table_ref):
        return [
            sum(spread(source_ref[p, q].astype(F32), table_ref[q]) for q in range(3))
            for p in range(3)
        ]

    bias = bias_ref[...]
    high = bias.astype(BF16).astype(F32)
    middle = (bias - high).astype(BF16).astype(F32)
    pieces = jnp.concatenate([high, middle, bias - high - middle, jnp.zeros_like(bias)], 0)
    offset = spread(pieces, first_table_ref[3])
    first = banded(parts_of(w_first_ref, first_table_ref), rows)
    first = first + jnp.concatenate([offset] * GRAD_ROWS, 0)
    weights_ref[:, 0:256] = (0.5 * first).astype(BF16)
    parts = [
        sum(spread(w_second_ref[2 - e, 2 - q].astype(F32), second_table_ref[q]) for q in range(3))
        for e in range(3)
    ]
    weights_ref[:, 256:384] = (0.5 * banded(parts, rows[:, :128])).astype(BF16)
    parts = parts_of(w_first_ref, back_table_ref)
    rows = lax.broadcasted_iota(jnp.int32, (1, 192), 1) & 15
    parts = [parts[2 - p] for p in range(3)]
    weights_ref[:, 384:576] = banded_back(parts, rows).astype(BF16)


def banded_back(parts, rows):
    blocks = []
    for r in range(GRAD_ROWS):
        total = jnp.zeros(parts[0].shape, F32)
        for k in range(3):
            total = total + jnp.where(rows == r - k, parts[k], 0.0)
        blocks.append(total)
    return jnp.concatenate(blocks, 0)


def network_body(
    place_ref,
    in_ref,
    strip_ref,
    above_ref,
    below_ref,
    w_first_ref,
    w_second_ref,
    bias_ref,
    first_table_ref,
    second_table_ref,
    back_table_ref,
    twiddle_ref,
    inverse_ref,
    forward_ref,
    spread_ref,
    rows_ref,
    fold_ref,
    base_ref,
    out_ref,
    stack_ref,
    features_ref,
    spread_grad_ref,
    acc_first_ref,
    acc_second_ref,
    back_ref,
    cot_ref,
    dirty_ref,
    weights_ref,
    tall_ref,
):
    prepare(
        strip_ref,
        above_ref,
        below_ref,
        w_first_ref,
        w_second_ref,
        bias_ref,
        first_table_ref,
        second_table_ref,
        back_table_ref,
        rows_ref,
        features_ref,
        cot_ref,
        dirty_ref,
        weights_ref,
        tall_ref,
        stack_ref,
    )
    place = place_ref[0]
    chunks = in_ref[...].astype(F32).reshape(64, 2, 8, 256)
    values = lax.dot_general(
        regroup(chunks[:, 0], chunks[:, 1]), inverse_ref[...], TN, preferred_element_type=F32
    )
    row = lax.broadcasted_iota(jnp.int32, (HOLD, IMAGE), 0)
    inside = ((row >= 2) | (place > 0)) & ((row < 18) | (place < DEVS - 1))
    for plane in range(2):
        blocks = columns_back(
            lambda j: values[64 * j + 32 * plane : 64 * j + 32 * plane + HOLD], twiddle_ref
        )
        blurred = jnp.concatenate(blocks, 1).astype(BF16).astype(F32)
        residual = dirty_ref[plane] - jnp.where(inside, blurred, 0.0)
        residual = residual.astype(BF16).astype(F32)
        for q in range(3):
            at = 20 * (3 * plane + q)
            stack_ref[at : at + 20, :] = shifted(residual, q)[0:20]
    stack_ref[120:128, :] = jnp.zeros((8, IMAGE), F32)
    features_ref[128:256, :] = stack_ref[...].astype(BF16)
    back_ref[...] = weights_ref[:, 384:576].astype(F32).T.astype(BF16)
    acc_first_ref[...] = jnp.zeros_like(acc_first_ref)
    acc_second_ref[...] = jnp.zeros_like(acc_second_ref)
    top = jnp.where(place > 0, 1.0, 0.0)
    bottom = jnp.where(place < DEVS - 1, 1.0, 0.0)

    def block(step, carry):
        cols = pl.ds(pl.multiple_of(step * 512, 512), 512)
        features = features_ref[:, cols]
        cots = cot_ref[:, cols]
        preact = jnp.dot(weights_ref[:, 0:256], features, preferred_element_type=F32)
        back = jnp.dot(weights_ref[:, 256:384], cots, preferred_element_type=F32)
        bend = jnp.tanh(preact)
        gate = 1.0 + bend
        hidden = preact * gate
        grad_pre = back * gate * (1.0 + preact * (1.0 - bend))
        grad_pre = jnp.concatenate(
            [grad_pre[0:32] * top, grad_pre[32:544], grad_pre[544:576] * bottom], 0
        ).astype(BF16)
        spread_grad_ref[:, cols] = jnp.dot(back_ref[...], grad_pre, preferred_element_type=F32)
        acc_first_ref[...] += lax.dot_general(grad_pre, features, NT, preferred_element_type=F32)
        acc_second_ref[...] += lax.dot_general(
            hidden.astype(BF16), cots, NT, preferred_element_type=F32
        )
        return carry

    lax.fori_loop(0, 4, block, 0, unroll=True)

    cot_sums = []
    z = [[None, None] for _ in range(8)]
    for i in range(4):
        rows = [spread_grad_ref[64 * q + 16 * i : 64 * q + 16 * i + 16, :] for q in range(3)]
        total = shifted(rows[0], 2) + rows[1] + shifted(rows[2], 0)
        for c in range(8):
            part = total[:, 256 * c : 256 * c + 256]
            if i < 2:
                base_ref[c, i] = part + strip_ref[c, 4 + i].astype(F32)
            else:
                z[c][i - 2] = part.astype(BF16).astype(F32)
    for i in range(2):
        total = strip_ref[0, 4 + i].astype(F32)
        for c in range(1, 8):
            total = total + strip_ref[c, 4 + i].astype(F32)
        cot_sums.append(total.sum(axis=0, keepdims=True).sum(axis=1, keepdims=True))

    rows = rows_ref[0:1, :]
    parts = [jnp.zeros((HIDDEN, 384), F32) for _ in range(3)]
    for r in range(1, 17):
        of_first = acc_first_ref[32 * r : 32 * r + 32, :]
        of_second = acc_second_ref[32 * r : 32 * r + 32, :]
        for p in range(3):
            keep = (rows == r + p) | (rows == -1)
            parts[p] = parts[p] + jnp.concatenate(
                [
                    jnp.where(keep, of_first, 0.0),
                    jnp.where(rows[:, :128] == r + p, of_second, 0.0),
                ],
                1,
            )
    sums = jnp.zeros((HIDDEN, 128), F32)
    for p in range(3):
        sums = sums + jnp.dot(
            parts[p],
            fold_ref[p].astype(F32),
            precision=lax.Precision.HIGHEST,
            preferred_element_type=F32,
        )
    at = lax.broadcasted_iota(jnp.int32, (HIDDEN, 128), 1)
    of = lax.broadcasted_iota(jnp.int32, (HIDDEN, 128), 0)
    for i in range(2):
        sums = jnp.where((at == 55) & (of == i), cot_sums[i], sums)

    even, odd = columns_ahead([jnp.concatenate(v, 0) for v in z], twiddle_ref, forward_ref)
    even, odd = even.reshape(32, 2, 8, 128), odd.reshape(32, 2, 8, 128)
    out = spaced([even[:, 0], odd[:, 0], even[:, 1], odd[:, 1]]).reshape(1280, 128)
    out = out + jnp.dot(
        spread_ref[...], jnp.concatenate(halves(sums), 0), preferred_element_type=F32
    )
    out_ref[...] = out.astype(BF16)


def finish_body(
    in_ref,
    base_ref,
    twiddle_ref,
    inverse_ref,
    collect_ref,
    out_ref,
    first_ref,
    first_bias_ref,
    second_ref,
    second_bias_ref,
):
    chunks = in_ref[...]
    sums = jnp.dot(collect_ref[...], chunks, preferred_element_type=F32) * (1.0 / IMAGE)
    sums = sums.T
    for p in range(3):
        for q in range(3):
            at = 3 * p + q
            first_ref[p, q] = sums[4 * at : 4 * at + 4]
            second_ref[p, q] = sums[36 + 2 * at : 38 + 2 * at]
    first_bias_ref[...] = sums[54:55]
    second_bias_ref[...] = sums[55:56, 0:2]
    fours = unspaced(chunks)
    even = jnp.stack([fours[0], fours[2]], 1).reshape(64, 8, 128)
    odd = jnp.stack([fours[1], fours[3]], 1).reshape(64, 8, 128)
    values = lax.dot_general(
        regroup(even, odd), inverse_ref[...], TN, preferred_element_type=F32
    )
    blocks = columns_back(lambda j: values[32 * j : 32 * j + 32], twiddle_ref)
    for c in range(8):
        blurred = blocks[c].astype(BF16).astype(F32).reshape(2, STRIP, 256)
        out_ref[c] = base_ref[c] - blurred


def call(body, outs, *args, scratch=(), scalars=0, after=(), cost=2):
    whole = pl.BlockSpec(memory_space=pltpu.VMEM)
    return pl.pallas_call(
        body,
        out_shape=outs,
        in_specs=[pl.BlockSpec(memory_space=pltpu.SMEM)] * scalars
        + [whole] * (len(args) - scalars)
        + [pl.BlockSpec(memory_space=pl.ANY)] * len(after),
        out_specs=jax.tree.map(lambda _: whole, outs),
        scratch_shapes=list(scratch),
        compiler_params=pltpu.CompilerParams(vmem_limit_bytes=VM * 1024 * 1024),
        cost_estimate=pl.CostEstimate(
            flops=cost * 10**9, bytes_accessed=cost * 10**6, transcendentals=0
        ),
    )(*args, *after)


def like(*shape, dtype=BF16):
    return jax.ShapeDtypeStruct(shape, dtype)


def exchange(chunks, per):
    width = chunks.shape[-1]
    rows = 8 if per == 8 else 2
    moved = lax.all_to_all(chunks.reshape(DEVS * per // rows, rows, width), RC, 0, 0, tiled=True)
    return moved.reshape(DEVS * per, width)


def middle(chunks, spectra, window, lead, per, after=()):
    ahead, back = row_block_tables()
    twiddle, row_table = row_forward_tables()
    back_twiddle, back_row = row_inverse_tables(window, lead)
    extra = sum_tables()[1:3] if per == 10 else ()
    return call(
        functools.partial(middle_body, window, per == 10),
        like(DEVS * per, 8 * window),
        chunks,
        spectra,
        ahead,
        back,
        row_table,
        back_row,
        twiddle,
        back_twiddle,
        *extra,
        after=after,
    )


def shards(estimate, dirty_image, psf_spectra, w_first, b_first, w_second, cotangent):
    cells = jnp.stack([v.reshape(2, 8, STRIP, 256) for v in (estimate, dirty_image, cotangent)])
    cells = cells.transpose(2, 0, 1, 3, 4).reshape(8, 6, STRIP, 256)
    strip = lax.all_to_all(cells, "col", 0, 0, tiled=True)
    spec = call(
        ahead_body, like(1024, 128), strip, column_twiddle(), column_tables()[0]
    )
    spec = exchange(spec, 8)
    above = lax.ppermute(strip[:, :, -2:], RC, [(d, d + 1) for d in range(DEVS - 1)])
    below = lax.ppermute(strip[:, :, :2], RC, [(d + 1, d) for d in range(DEVS - 1)])
    first_table, second_table, back_table, row_of, fold = weight_tables()
    mixed = exchange(middle(spec, psf_spectra, 32, 2, 8, ()), 8)
    place = (lax.axis_index("row") * 8 + lax.axis_index("col")).astype(jnp.int32).reshape(1)
    base, spec = call(
        network_body,
        (like(8, 2, STRIP, 256, dtype=F32), like(1280, 128)),
        place,
        mixed,
        strip,
        above,
        below,
        w_first.transpose(2, 3, 1, 0),
        w_second.transpose(2, 3, 0, 1),
        b_first.reshape(1, 32),
        first_table,
        second_table,
        back_table,
        column_twiddle(),
        column_tables()[1],
        column_tables()[0],
        sum_tables()[0],
        row_of,
        fold,
        scratch=[
            pltpu.VMEM((128, IMAGE), F32),
            pltpu.VMEM((256, IMAGE), BF16),
            pltpu.VMEM((192, IMAGE), F32),
            pltpu.VMEM((576, 256), F32),
            pltpu.VMEM((576, 128), F32),
            pltpu.VMEM((192, 576), BF16),
            pltpu.VMEM((128, IMAGE), BF16),
            pltpu.VMEM((2, HOLD, IMAGE), F32),
            pltpu.VMEM((576, 576), BF16),
            pltpu.VMEM((HOLD, IMAGE), F32),
        ],
        scalars=1,
        cost=8,
    )
    mixed = exchange(middle(exchange(spec, 10), psf_spectra, 16, 0, 10), 10)
    image, grad_first, first_bias, grad_second, second_bias = call(
        finish_body,
        (
            like(8, 2, STRIP, 256, dtype=F32),
            like(3, 3, 4, 32, dtype=F32),
            like(1, 32, dtype=F32),
            like(3, 3, 2, 32, dtype=F32),
            like(1, 2, dtype=F32),
        ),
        mixed,
        base,
        column_twiddle(),
        column_tables()[1],
        sum_tables()[3],
    )
    image = lax.all_to_all(image, "col", 0, 0, tiled=True)
    grad_image = image.transpose(1, 0, 2, 3).reshape(2, 128, 256)
    return (
        grad_image,
        grad_first.transpose(3, 2, 0, 1),
        first_bias.reshape(32),
        grad_second.transpose(2, 3, 0, 1),
        second_bias.reshape(2),
    )


def solution(mesh):
    return jax.shard_map(
        shards,
        mesh=mesh,
        in_specs=(
            P(None, "row", "col"),
            P(None, "row", "col"),
            P(None, ("row", "col"), None, None),
            P(),
            P(),
            P(),
            P(None, "row", "col"),
        ),
        out_specs=(P(None, "row", "col"), P(), P(), P(), P()),
        check_vma=False,
    )
```

```python
import functools

import jax
import jax.numpy as jnp
import numpy as np
from jax import lax
from jax.experimental import pallas as pl
from jax.experimental.pallas import tpu as pltpu
from jax.sharding import PartitionSpec as P

IMAGE = 2048
DEVS = 128
VM = 20
STRIP = 16
REACH = 20
HOLD = 24
GRAD_ROWS = 18
HIDDEN = 32
RC = ("row", "col")
F32 = jnp.float32
BF16 = jnp.bfloat16
NT = (((1,), (1,)), ((), ()))
TN = (((0,), (0,)), ((), ()))


def turn(product, period):
    angle = 2.0 * np.pi * (product % period) / period
    return np.cos(angle), np.sin(angle)


def bf16_table(values):
    return np.asarray(values, np.float32).astype(jnp.bfloat16)


@functools.lru_cache(None)
def column_twiddle():
    cos, sin = turn(np.arange(8)[:, None] * np.arange(256)[None, :], 2048)
    return np.concatenate([cos, sin]).astype(np.float32)


@functools.lru_cache(None)
def column_tables():
    freq = 2 * np.arange(128)[:, None] + np.arange(2)[None, :]
    cos, sin = turn(freq[:, :, None] * np.arange(256), 256)
    ahead = np.zeros((128, 2, 2, 2, 256))
    ahead[:, 0, :, 0] = cos
    ahead[:, 0, :, 1] = sin
    ahead[:, 1, :, 0] = -sin
    ahead[:, 1, :, 1] = cos
    back = np.zeros((128, 2, 2, 2, 256))
    back[:, 0, :, 0] = cos
    back[:, 1, :, 0] = -sin
    back[:, 0, :, 1] = sin
    back[:, 1, :, 1] = cos
    return bf16_table(ahead.reshape(512, 512)), bf16_table(back.reshape(512, 512))


@functools.lru_cache(None)
def row_block_tables():
    cos, sin = turn(np.arange(16)[:, None] * np.arange(16), 16)
    ahead = np.zeros((2, 2, 2, 16, 16, 2, 2, 2))
    for kappa in range(2):
        for jhi in range(2):
            ahead[0, kappa, jhi, :, :, jhi, 0, kappa] = cos
            ahead[0, kappa, jhi, :, :, jhi, 1, kappa] = sin
            ahead[1, kappa, jhi, :, :, jhi, 0, kappa] = -sin
            ahead[1, kappa, jhi, :, :, jhi, 1, kappa] = cos
    ahead = ahead.reshape(128, 128)
    return bf16_table(ahead), bf16_table(ahead.T / IMAGE)


@functools.lru_cache(None)
def row_forward_tables():
    pos = np.arange(128)
    cos, sin = turn(np.arange(16)[:, None] * pos, 2048)
    twiddle = np.concatenate([cos, sin]).astype(np.float32)
    cos, sin = turn(pos[:, None] * np.arange(128), 128)
    return twiddle, bf16_table(np.concatenate([cos, sin], 1))


@functools.lru_cache(None)
def row_inverse_tables(window, lead):
    pos = (16 * np.arange(8)[:, None] + np.arange(window)[None, :] - lead).reshape(-1)
    cos, sin = turn(np.arange(16)[:, None] * pos, 2048)
    twiddle = np.concatenate([cos, sin]).astype(np.float32)
    cos, sin = turn(np.arange(128)[:, None] * pos, 128)
    return twiddle, bf16_table(np.concatenate([cos, sin], 1))


@functools.lru_cache(None)
def sum_tables():
    spread = np.zeros((128, 10, 64))
    share = np.zeros((128, 10, 32))
    gather = np.zeros((16, 128, 10))
    collect = np.zeros((32, 128, 10))
    for d in range(128):
        spread[d, 8, d % 32] = 1.0
        spread[d, 9, 32 + d % 32] = 1.0
    share[:, 8, 0] = 1.0
    share[:, 9, 16] = 1.0
    gather[:, :, 8:] = 1.0
    for c in range(32):
        collect[c, c, 8:] = 1.0
    return (
        bf16_table(spread.reshape(1280, 64)),
        bf16_table(gather.reshape(16, 1280)),
        bf16_table(share.reshape(1280, 32)),
        bf16_table(collect.reshape(32, 1280)),
    )


@functools.lru_cache(None)
def weight_tables():
    first = np.zeros((4, 4, 256))
    second = np.zeros((3, 2, 128))
    back = np.zeros((3, 4, 192))
    rows = np.full((8, 256), 99)
    fold = np.zeros((3, 384, 128), np.float32)
    for q in range(3):
        for i in range(4):
            at = 128 * (i // 2) + 20 * (3 * (i % 2) + q)
            rows[:, at : at + 20] = np.arange(20)
            first[q, i, at : at + 20] = 1.0
            back[q, i, q * 64 + i * 16 : q * 64 + i * 16 + 16] = 1.0
            for p in range(3):
                fold[p, at : at + 20, (p * 3 + q) * 4 + i] = 1.0
        for o in range(2):
            at = 20 * (3 * o + q)
            second[q, o, at : at + 20] = 1.0
            for e in range(3):
                to = 36 + ((2 - e) * 3 + 2 - q) * 2 + o
                fold[e, 256 + at : 276 + at, to] = 1.0
    rows[:, 120] = -1
    for i in range(3):
        first[3, i, 120 + i] = 1.0
    fold[0, 120, 54] = 1.0
    return (
        first.astype(np.float32),
        second.astype(np.float32),
        back.astype(np.float32),
        rows.astype(np.int32),
        bf16_table(fold),
    )


def columns_ahead(z, twiddle_ref, table_ref):
    root = float(np.sqrt(0.5))
    s04, d04 = z[0] + z[4], z[0] - z[4]
    s26, d26 = z[2] + z[6], z[2] - z[6]
    s15, d15 = z[1] + z[5], z[1] - z[5]
    s37, d37 = z[3] + z[7], z[3] - z[7]
    low, high = root * (d15 - d37), root * (d15 + d37)
    real = [None] * 8
    imag = [None] * 8
    even, odd = s04 + s26, s15 + s37
    real[0], real[4] = even + odd, even - odd
    real[2], imag[2] = s04 - s26, s37 - s15
    real[1], imag[1] = d04 + low, -d26 - high
    real[3], imag[3] = d04 - low, d26 - high
    for j in (1, 2, 3):
        real[8 - j], imag[8 - j] = real[j], -imag[j]
    groups = []
    for j in range(8):
        cos, sin = twiddle_ref[j : j + 1, :], twiddle_ref[8 + j : 9 + j, :]
        if imag[j] is None:
            pieces = [real[j] * cos, -real[j] * sin]
        else:
            pieces = [real[j] * cos + imag[j] * sin, imag[j] * cos - real[j] * sin]
        groups.append(jnp.concatenate(pieces, axis=1).astype(BF16))
    values = lax.dot_general(
        table_ref[...], jnp.concatenate(groups, axis=0), NT, preferred_element_type=F32
    )
    low, high = (values[:, at : at + 128].reshape(64, 8, 128) for at in (0, 128))
    sub = lax.broadcasted_iota(jnp.int32, (64, 8, 128), 1)
    return (
        jnp.where(sub < 4, low, pltpu.roll(high, 4, 1)),
        jnp.where(sub < 4, pltpu.roll(low, 4, 1), high),
    )


def regroup(even, odd):
    sub = lax.broadcasted_iota(jnp.int32, even.shape, 1)
    shape = (512, even.shape[2])
    first = jnp.where(sub < 4, even, pltpu.roll(odd, 4, 1))
    second = jnp.where(sub < 4, pltpu.roll(even, 4, 1), odd)
    return jnp.concatenate([first.reshape(shape), second.reshape(shape)], 1).astype(BF16)


def spaced(chunks):
    gap = jnp.zeros((chunks[0].shape[0], 2, 128), F32)
    pieces = []
    for value in chunks:
        pieces += [value, gap]
    return jnp.concatenate(pieces, 1)


def unspaced(rows):
    rows = rows.astype(F32).reshape(32, 40, 128)
    return [rows[:, 10 * j : 10 * j + 8] for j in range(4)]


def columns_back(rows_of, twiddle_ref):
    real = [None] * 8
    imag = [None] * 8
    for j in range(8):
        rows = rows_of(j)
        re, im = rows[:, :256], rows[:, 256:]
        cos, sin = twiddle_ref[j : j + 1, :], twiddle_ref[8 + j : 9 + j, :]
        real[j] = re * cos - im * sin
        imag[j] = re * sin + im * cos
    fold_re = [real[0]] + [real[j] + real[8 - j] for j in (1, 2, 3)] + [real[4]]
    fold_im = [None] + [imag[j] - imag[8 - j] for j in (1, 2, 3)]
    scale = 1.0 / IMAGE
    root = float(np.sqrt(0.5)) * scale
    base_even = (fold_re[0] + fold_re[4]) * scale
    base_odd = (fold_re[0] - fold_re[4]) * scale
    re2, im2 = fold_re[2] * scale, fold_im[2] * scale
    sum_re, dif_re = fold_re[1] + fold_re[3], fold_re[1] - fold_re[3]
    sum_im, dif_im = fold_im[1] + fold_im[3], fold_im[1] - fold_im[3]
    cross = root * (dif_re - sum_im), root * (dif_re + sum_im)
    return [
        base_even + re2 + sum_re * scale,
        base_odd - im2 + cross[0],
        base_even - re2 - dif_im * scale,
        base_odd + im2 - cross[1],
        base_even + re2 - sum_re * scale,
        base_odd - im2 - cross[0],
        base_even - re2 + dif_im * scale,
        base_odd + im2 + cross[1],
    ]


def swap_blocks(arrays, size):
    arrays = list(arrays)
    count = 128 // size
    lane = lax.broadcasted_iota(jnp.int32, arrays[0].shape, 1)
    step = count // 2
    while step:
        low = (lane & (step * size)) == 0
        for i in range(count):
            if not i & step:
                one, two = arrays[i], arrays[i + step]
                arrays[i] = jnp.where(low, one, pltpu.roll(two, step * size, 1))
                arrays[i + step] = jnp.where(low, pltpu.roll(one, 128 - step * size, 1), two)
        step //= 2
    return arrays


def halves(values):
    high = values.astype(BF16)
    return high, (values - high.astype(F32)).astype(BF16)


def cells_body(estimate_ref, dirty_ref, cot_ref, out_ref):
    sources = (estimate_ref, dirty_ref, cot_ref)
    planes = [sources[i // 2][i % 2].astype(F32) for i in range(6)]
    gap = jnp.zeros((2, 256), F32)
    for c in range(8):
        pieces = []
        for i in range(6):
            out_ref[c, 16 * i : 16 * i + 16] = sources[i // 2][i % 2, 16 * c : 16 * c + 16]
            pieces.append(planes[i][16 * c - 2 : 16 * c] if c > 0 else gap)
            pieces.append(planes[i][16 * c + 16 : 16 * c + 18] if c < 7 else gap)
        pieces.append(jnp.zeros((8, 256), F32))
        out_ref[c, 96:128] = jnp.concatenate(pieces, 0).astype(BF16)


def ahead_body(strip_ref, twiddle_ref, table_ref, out_ref):
    z = [strip_ref[c, 0:32].astype(F32) for c in range(8)]
    even, odd = columns_ahead(z, twiddle_ref, table_ref)
    out_ref[...] = jnp.stack([even, odd], 1).reshape(1024, 128).astype(BF16)


def middle_body(window, summing, *refs):
    in_ref, spectra_ref, ahead_ref, back_ref, row_ref, back_row_ref, tw_ref, back_tw_ref = refs[:8]
    out_ref = refs[-1]
    chunks = in_ref[...]
    if summing:
        fours = [part.reshape(16, 2, 8, 128) for part in unspaced(chunks)]
        rows = [fours[c % 4][:, c // 4].reshape(128, 128) for c in range(8)]
    else:
        rows = chunks.astype(F32).reshape(16, 8, 8, 128)
        rows = [rows[:, c].reshape(128, 128) for c in range(8)]
    rows = jnp.concatenate(rows, 1).astype(BF16)
    first = jnp.dot(ahead_ref[...], rows, preferred_element_type=F32)
    per_m = swap_blocks([first[:, 128 * c : 128 * c + 128] for c in range(8)], 16)
    cos, sin = tw_ref[0:16, :], tw_ref[16:32, :]
    rows = []
    for m in range(8):
        real = per_m[m][:64].reshape(4, 16, 128)
        imag = per_m[m][64:].reshape(4, 16, 128)
        rows.append((real * cos + imag * sin).astype(BF16).reshape(64, 128))
        rows.append((imag * cos - real * sin).astype(BF16).reshape(64, 128))
    second = jnp.dot(jnp.concatenate(rows, 0), row_ref[...], preferred_element_type=F32)
    rows = []
    for jlo in range(4):
        full_re, full_im = [], []
        for plane in range(2):
            m = 2 * jlo + plane
            part = second[128 * m : 128 * m + 128]
            full_re.append(part[:64, :128] + part[64:, 128:])
            full_im.append(part[64:, :128] - part[:64, 128:])
        weights = [
            spectra_ref[t].reshape(4, 4, 16, 128)[:, jlo].reshape(64, 128) for t in range(3)
        ]
        for plane in range(2):
            for part in (full_re, full_im):
                mixed = weights[plane] * part[0] + weights[plane + 1] * part[1]
                rows.append(mixed.astype(BF16))
    third = jnp.dot(jnp.concatenate(rows, 0), back_row_ref[...], preferred_element_type=F32)
    half = 8 * window
    cos, sin = back_tw_ref[0:16, :], back_tw_ref[16:32, :]
    per_m = []
    for m in range(8):
        part = third[128 * m : 128 * m + 128]
        real = (part[:64, :half] - part[64:, half:]).reshape(4, 16, half)
        imag = (part[64:, :half] + part[:64, half:]).reshape(4, 16, half)
        per_m.append(
            jnp.concatenate(
                [
                    (real * cos - imag * sin).reshape(64, half),
                    (real * sin + imag * cos).reshape(64, half),
                ],
                0,
            )
        )
    count = 128 // window
    tiles = 8 // count
    per_c = [[None] * tiles for _ in range(8)]
    for m_hi in range(tiles):
        for c_hi in range(tiles):
            cols = slice(128 * c_hi, 128 * c_hi + 128)
            group = [per_m[m_hi * count + i][:, cols] for i in range(count)]
            for i, value in enumerate(swap_blocks(group, window)):
                per_c[c_hi * count + i][m_hi] = value
    rows = jnp.concatenate([tile for v in per_c for tile in v], 1).astype(BF16)
    out = jnp.dot(back_ref[...], rows, preferred_element_type=F32)
    out = [out[:, half * c : half * c + half].reshape(16, 8, half) for c in range(8)]
    if summing:
        gather_ref, share_ref = refs[8:10]
        total = jnp.dot(gather_ref[...], chunks, preferred_element_type=F32)
        out = jnp.stack([spaced(out[:4]), spaced(out[4:])], 1).reshape(1280, 128)
        out = out + jnp.dot(
            share_ref[...], jnp.concatenate(halves(total), 0), preferred_element_type=F32
        )
    else:
        out = jnp.stack(out, 1).reshape(1024, half)
    out_ref[...] = out.astype(BF16)


def shifted(value, q):
    if q == 1:
        return value
    lane = lax.broadcasted_iota(jnp.int32, value.shape, 1)
    if q == 0:
        return jnp.where(lane == 0, 0.0, pltpu.roll(value, 1, 1))
    return jnp.where(lane == IMAGE - 1, 0.0, pltpu.roll(value, IMAGE - 1, 1))


def banded(weights, window_row):
    rows = []
    for r in range(GRAD_ROWS):
        total = jnp.zeros(weights[0].shape, F32)
        for p in range(3):
            total = total + jnp.where(window_row == r + p, weights[p], 0.0)
        rows.append(total)
    return jnp.concatenate(rows, 0)


def prepare(
    place,
    strip_ref,
    beyond_ref,
    w_first_ref,
    w_second_ref,
    bias_ref,
    first_table_ref,
    second_table_ref,
    back_table_ref,
    rows_ref,
    features_ref,
    cot_ref,
    dirty_ref,
    weights_ref,
    tall_ref,
    stack_ref,
):
    row = lax.broadcasted_iota(jnp.int32, (128, IMAGE), 0)
    tall_ref[...] = jnp.zeros_like(tall_ref)
    rims = [strip_ref[c, 96:128].astype(F32) for c in range(8)]
    opens = (place & 7) == 0
    closes = (place & 7) == 7
    for i in range(6):
        for c in range(8):
            cols = slice(256 * c, 256 * c + 256)
            beyond = beyond_ref[c, i].astype(F32)
            tall_ref[0:2, cols] = jnp.where(opens, beyond, rims[c][4 * i : 4 * i + 2])
            tall_ref[2:18, cols] = strip_ref[c, 16 * i : 16 * i + 16].astype(F32)
            tall_ref[18:20, cols] = jnp.where(closes, beyond, rims[c][4 * i + 2 : 4 * i + 4])
        value = tall_ref[...]
        if i in (2, 3):
            dirty_ref[i - 2] = value
        else:
            for q in range(3):
                at = 20 * (3 * (i % 2) + q)
                stack_ref[at : at + 20, :] = shifted(value, q)[0:20]
            if i == 1:
                out = jnp.where(row < 120, stack_ref[...], jnp.where(row < 123, 1.0, 0.0))
                features_ref[0:128, :] = out.astype(BF16)
            if i == 5:
                cot_ref[...] = jnp.where(row < 120, stack_ref[...], 0.0).astype(BF16)
    rows = rows_ref[0:1, :]

    def spread(weights, table):
        return lax.dot_general(weights, table, TN, preferred_element_type=F32)

    def parts_of(source_ref, table_ref):
        return [
            sum(spread(source_ref[p, q].astype(F32), table_ref[q]) for q in range(3))
            for p in range(3)
        ]

    bias = bias_ref[...]
    high = bias.astype(BF16).astype(F32)
    middle = (bias - high).astype(BF16).astype(F32)
    pieces = jnp.concatenate([high, middle, bias - high - middle, jnp.zeros_like(bias)], 0)
    offset = spread(pieces, first_table_ref[3])
    first = banded(parts_of(w_first_ref, first_table_ref), rows)
    first = first + jnp.concatenate([offset] * GRAD_ROWS, 0)
    weights_ref[:, 0:256] = (0.5 * first).astype(BF16)
    parts = [
        sum(spread(w_second_ref[2 - e, 2 - q].astype(F32), second_table_ref[q]) for q in range(3))
        for e in range(3)
    ]
    weights_ref[:, 256:384] = (0.5 * banded(parts, rows[:, :128])).astype(BF16)
    parts = parts_of(w_first_ref, back_table_ref)
    rows = lax.broadcasted_iota(jnp.int32, (1, 192), 1) & 15
    parts = [parts[2 - p] for p in range(3)]
    weights_ref[:, 384:576] = banded_back(parts, rows).astype(BF16)


def banded_back(parts, rows):
    blocks = []
    for r in range(GRAD_ROWS):
        total = jnp.zeros(parts[0].shape, F32)
        for k in range(3):
            total = total + jnp.where(rows == r - k, parts[k], 0.0)
        blocks.append(total)
    return jnp.concatenate(blocks, 0)


def network_body(
    place_ref,
    in_ref,
    strip_ref,
    beyond_ref,
    w_first_ref,
    w_second_ref,
    bias_ref,
    first_table_ref,
    second_table_ref,
    back_table_ref,
    twiddle_ref,
    inverse_ref,
    forward_ref,
    spread_ref,
    rows_ref,
    fold_ref,
    base_ref,
    out_ref,
    stack_ref,
    features_ref,
    spread_grad_ref,
    acc_first_ref,
    acc_second_ref,
    back_ref,
    cot_ref,
    dirty_ref,
    weights_ref,
    tall_ref,
):
    place = place_ref[0]
    prepare(
        place,
        strip_ref,
        beyond_ref,
        w_first_ref,
        w_second_ref,
        bias_ref,
        first_table_ref,
        second_table_ref,
        back_table_ref,
        rows_ref,
        features_ref,
        cot_ref,
        dirty_ref,
        weights_ref,
        tall_ref,
        stack_ref,
    )
    chunks = in_ref[...].astype(F32).reshape(64, 2, 8, 256)
    values = lax.dot_general(
        regroup(chunks[:, 0], chunks[:, 1]), inverse_ref[...], TN, preferred_element_type=F32
    )
    row = lax.broadcasted_iota(jnp.int32, (HOLD, IMAGE), 0)
    inside = ((row >= 2) | (place > 0)) & ((row < 18) | (place < DEVS - 1))
    for plane in range(2):
        blocks = columns_back(
            lambda j: values[64 * j + 32 * plane : 64 * j + 32 * plane + HOLD], twiddle_ref
        )
        blurred = jnp.concatenate(blocks, 1).astype(BF16).astype(F32)
        residual = dirty_ref[plane] - jnp.where(inside, blurred, 0.0)
        residual = residual.astype(BF16).astype(F32)
        for q in range(3):
            at = 20 * (3 * plane + q)
            stack_ref[at : at + 20, :] = shifted(residual, q)[0:20]
    stack_ref[120:128, :] = jnp.zeros((8, IMAGE), F32)
    features_ref[128:256, :] = stack_ref[...].astype(BF16)
    back_ref[...] = weights_ref[:, 384:576].astype(F32).T.astype(BF16)
    acc_first_ref[...] = jnp.zeros_like(acc_first_ref)
    acc_second_ref[...] = jnp.zeros_like(acc_second_ref)
    top = jnp.where(place > 0, 1.0, 0.0)
    bottom = jnp.where(place < DEVS - 1, 1.0, 0.0)

    def block(step, carry):
        cols = pl.ds(pl.multiple_of(step * 512, 512), 512)
        features = features_ref[:, cols]
        cots = cot_ref[:, cols]
        preact = jnp.dot(weights_ref[:, 0:256], features, preferred_element_type=F32)
        back = jnp.dot(weights_ref[:, 256:384], cots, preferred_element_type=F32)
        bend = jnp.tanh(preact)
        gate = 1.0 + bend
        hidden = preact * gate
        grad_pre = back * gate * (1.0 + preact * (1.0 - bend))
        grad_pre = jnp.concatenate(
            [grad_pre[0:32] * top, grad_pre[32:544], grad_pre[544:576] * bottom], 0
        ).astype(BF16)
        spread_grad_ref[:, cols] = jnp.dot(back_ref[...], grad_pre, preferred_element_type=F32)
        acc_first_ref[...] += lax.dot_general(
            grad_pre[32:544], features, NT, preferred_element_type=F32
        )
        acc_second_ref[...] += lax.dot_general(
            hidden[32:544].astype(BF16), cots, NT, preferred_element_type=F32
        )
        return carry

    lax.fori_loop(0, 4, block, 0, unroll=True)

    cot_sums = []
    z = [[None, None] for _ in range(8)]
    for i in range(4):
        rows = [spread_grad_ref[64 * q + 16 * i : 64 * q + 16 * i + 16, :] for q in range(3)]
        total = shifted(rows[0], 2) + rows[1] + shifted(rows[2], 0)
        for c in range(8):
            part = total[:, 256 * c : 256 * c + 256]
            if i < 2:
                base_ref[c, i] = part + strip_ref[c, 64 + 16 * i : 80 + 16 * i].astype(F32)
            else:
                z[c][i - 2] = part.astype(BF16).astype(F32)
    for i in range(2):
        total = strip_ref[0, 64 + 16 * i : 80 + 16 * i].astype(F32)
        for c in range(1, 8):
            total = total + strip_ref[c, 64 + 16 * i : 80 + 16 * i].astype(F32)
        cot_sums.append(total.sum(axis=0, keepdims=True).sum(axis=1, keepdims=True))

    rows = rows_ref[0:1, :]
    parts = [jnp.zeros((HIDDEN, 384), F32) for _ in range(3)]
    for r in range(1, 17):
        of_first = acc_first_ref[32 * r - 32 : 32 * r, :]
        of_second = acc_second_ref[32 * r - 32 : 32 * r, :]
        for p in range(3):
            keep = (rows == r + p) | (rows == -1)
            parts[p] = parts[p] + jnp.concatenate(
                [
                    jnp.where(keep, of_first, 0.0),
                    jnp.where(rows[:, :128] == r + p, of_second, 0.0),
                ],
                1,
            )
    sums = jnp.zeros((HIDDEN, 128), F32)
    for p in range(3):
        sums = sums + jnp.dot(
            parts[p],
            fold_ref[p].astype(F32),
            precision=lax.Precision.HIGHEST,
            preferred_element_type=F32,
        )
    at = lax.broadcasted_iota(jnp.int32, (HIDDEN, 128), 1)
    of = lax.broadcasted_iota(jnp.int32, (HIDDEN, 128), 0)
    for i in range(2):
        sums = jnp.where((at == 55) & (of == i), cot_sums[i], sums)

    even, odd = columns_ahead([jnp.concatenate(v, 0) for v in z], twiddle_ref, forward_ref)
    even, odd = even.reshape(32, 2, 8, 128), odd.reshape(32, 2, 8, 128)
    out = spaced([even[:, 0], odd[:, 0], even[:, 1], odd[:, 1]]).reshape(1280, 128)
    out = out + jnp.dot(
        spread_ref[...], jnp.concatenate(halves(sums), 0), preferred_element_type=F32
    )
    out_ref[...] = out.astype(BF16)


def finish_body(
    in_ref,
    base_ref,
    twiddle_ref,
    inverse_ref,
    collect_ref,
    out_ref,
    first_ref,
    first_bias_ref,
    second_ref,
    second_bias_ref,
):
    chunks = in_ref[...]
    sums = jnp.dot(collect_ref[...], chunks, preferred_element_type=F32) * (1.0 / IMAGE)
    sums = sums.T
    for p in range(3):
        for q in range(3):
            at = 3 * p + q
            first_ref[p, q] = sums[4 * at : 4 * at + 4]
            second_ref[p, q] = sums[36 + 2 * at : 38 + 2 * at]
    first_bias_ref[...] = sums[54:55]
    second_bias_ref[...] = sums[55:56, 0:2]
    fours = unspaced(chunks)
    even = jnp.stack([fours[0], fours[2]], 1).reshape(64, 8, 128)
    odd = jnp.stack([fours[1], fours[3]], 1).reshape(64, 8, 128)
    values = lax.dot_general(
        regroup(even, odd), inverse_ref[...], TN, preferred_element_type=F32
    )
    blocks = columns_back(lambda j: values[32 * j : 32 * j + 32], twiddle_ref)
    for c in range(8):
        blurred = blocks[c].astype(BF16).astype(F32).reshape(2, STRIP, 256)
        out_ref[c] = base_ref[c] - blurred


def call(body, outs, *args, scratch=(), scalars=0, after=(), cost=2, vmem=VM):
    whole = pl.BlockSpec(memory_space=pltpu.VMEM)
    return pl.pallas_call(
        body,
        out_shape=outs,
        in_specs=[pl.BlockSpec(memory_space=pltpu.SMEM)] * scalars
        + [whole] * (len(args) - scalars)
        + [pl.BlockSpec(memory_space=pl.ANY)] * len(after),
        out_specs=jax.tree.map(lambda _: whole, outs),
        scratch_shapes=list(scratch),
        compiler_params=pltpu.CompilerParams(vmem_limit_bytes=vmem * 1024 * 1024),
        cost_estimate=pl.CostEstimate(
            flops=cost * 10**9, bytes_accessed=cost * 10**6, transcendentals=0
        ),
    )(*args, *after)


def like(*shape, dtype=BF16):
    return jax.ShapeDtypeStruct(shape, dtype)


def exchange(chunks, per):
    width = chunks.shape[-1]
    rows = 8 if per == 8 else 2
    moved = lax.all_to_all(chunks.reshape(DEVS * per // rows, rows, width), RC, 0, 0, tiled=True)
    return moved.reshape(DEVS * per, width)


def middle(chunks, spectra, window, lead, per, after=()):
    ahead, back = row_block_tables()
    twiddle, row_table = row_forward_tables()
    back_twiddle, back_row = row_inverse_tables(window, lead)
    extra = sum_tables()[1:3] if per == 10 else ()
    return call(
        functools.partial(middle_body, window, per == 10),
        like(DEVS * per, 8 * window),
        chunks,
        spectra,
        ahead,
        back,
        row_table,
        back_row,
        twiddle,
        back_twiddle,
        *extra,
        after=after,
    )


def shards(estimate, dirty_image, psf_spectra, w_first, b_first, w_second, cotangent):
    cells = call(
        cells_body, like(8, 128, 256), estimate, dirty_image, cotangent, vmem=60
    )
    strip = lax.all_to_all(cells, "col", 0, 0, tiled=True)
    spec = call(
        ahead_body, like(1024, 128), strip, column_twiddle(), column_tables()[0]
    )
    spec = exchange(spec, 8)
    rows = strip[:, :96].reshape(8, 6, STRIP, 256)
    edge = jnp.where(lax.axis_index("col") == 7, rows[:, :, -2:], rows[:, :, :2])
    seams = [(8 * r + 7, 8 * r + 8) for r in range(15)]
    beyond = lax.ppermute(edge, RC, seams + [(b, a) for a, b in seams])
    first_table, second_table, back_table, row_of, fold = weight_tables()
    mixed = exchange(middle(spec, psf_spectra, 32, 2, 8, ()), 8)
    place = (lax.axis_index("row") * 8 + lax.axis_index("col")).astype(jnp.int32).reshape(1)
    base, spec = call(
        network_body,
        (like(8, 2, STRIP, 256, dtype=F32), like(1280, 128)),
        place,
        mixed,
        strip,
        beyond,
        w_first.transpose(2, 3, 1, 0),
        w_second.transpose(2, 3, 0, 1),
        b_first.reshape(1, 32),
        first_table,
        second_table,
        back_table,
        column_twiddle(),
        column_tables()[1],
        column_tables()[0],
        sum_tables()[0],
        row_of,
        fold,
        scratch=[
            pltpu.VMEM((128, IMAGE), F32),
            pltpu.VMEM((256, IMAGE), BF16),
            pltpu.VMEM((192, IMAGE), F32),
            pltpu.VMEM((512, 256), F32),
            pltpu.VMEM((512, 128), F32),
            pltpu.VMEM((192, 576), BF16),
            pltpu.VMEM((128, IMAGE), BF16),
            pltpu.VMEM((2, HOLD, IMAGE), F32),
            pltpu.VMEM((576, 576), BF16),
            pltpu.VMEM((HOLD, IMAGE), F32),
        ],
        scalars=1,
        cost=8,
    )
    mixed = exchange(middle(exchange(spec, 10), psf_spectra, 16, 0, 10), 10)
    image, grad_first, first_bias, grad_second, second_bias = call(
        finish_body,
        (
            like(8, 2, STRIP, 256, dtype=F32),
            like(3, 3, 4, 32, dtype=F32),
            like(1, 32, dtype=F32),
            like(3, 3, 2, 32, dtype=F32),
            like(1, 2, dtype=F32),
        ),
        mixed,
        base,
        column_twiddle(),
        column_tables()[1],
        sum_tables()[3],
    )
    image = lax.all_to_all(image, "col", 0, 0, tiled=True)
    grad_image = image.transpose(1, 0, 2, 3).reshape(2, 128, 256)
    return (
        grad_image,
        grad_first.transpose(3, 2, 0, 1),
        first_bias.reshape(32),
        grad_second.transpose(2, 3, 0, 1),
        second_bias.reshape(2),
    )


def solution(mesh):
    return jax.shard_map(
        shards,
        mesh=mesh,
        in_specs=(
            P(None, "row", "col"),
            P(None, "row", "col"),
            P(None, ("row", "col"), None, None),
            P(),
            P(),
            P(),
            P(None, "row", "col"),
        ),
        out_specs=(P(None, "row", "col"), P(), P(), P(), P()),
        check_vma=False,
    )
```

```python
import functools

import jax
import jax.numpy as jnp
import numpy as np
from jax import lax
from jax.experimental import pallas as pl
from jax.experimental.pallas import tpu as pltpu
from jax.sharding import PartitionSpec as P

IMAGE = 2048
DEVS = 128
VM = 28
STRIP = 16
REACH = 20
HOLD = 24
GRAD_ROWS = 18
HIDDEN = 32
RC = ("row", "col")
F32 = jnp.float32
BF16 = jnp.bfloat16
NT = (((1,), (1,)), ((), ()))
TN = (((0,), (0,)), ((), ()))


def turn(product, period):
    angle = 2.0 * np.pi * (product % period) / period
    return np.cos(angle), np.sin(angle)


def bf16_table(values):
    return np.asarray(values, np.float32).astype(jnp.bfloat16)


@functools.lru_cache(None)
def column_twiddle():
    cos, sin = turn(np.arange(8)[:, None] * np.arange(256)[None, :], 2048)
    return np.concatenate([cos, sin]).astype(np.float32)


@functools.lru_cache(None)
def column_tables():
    freq = 2 * np.arange(128)[:, None] + np.arange(2)[None, :]
    cos, sin = turn(freq[:, :, None] * np.arange(256), 256)
    ahead = np.zeros((128, 2, 2, 2, 256))
    ahead[:, 0, :, 0] = cos
    ahead[:, 0, :, 1] = sin
    ahead[:, 1, :, 0] = -sin
    ahead[:, 1, :, 1] = cos
    back = np.zeros((128, 2, 2, 2, 256))
    back[:, 0, :, 0] = cos
    back[:, 1, :, 0] = -sin
    back[:, 0, :, 1] = sin
    back[:, 1, :, 1] = cos
    return bf16_table(ahead.reshape(512, 512)), bf16_table(back.reshape(512, 512))


@functools.lru_cache(None)
def row_block_tables():
    cos, sin = turn(np.arange(16)[:, None] * np.arange(16), 16)
    ahead = np.zeros((2, 2, 2, 16, 16, 2, 2, 2))
    for kappa in range(2):
        for jhi in range(2):
            ahead[0, kappa, jhi, :, :, jhi, 0, kappa] = cos
            ahead[0, kappa, jhi, :, :, jhi, 1, kappa] = sin
            ahead[1, kappa, jhi, :, :, jhi, 0, kappa] = -sin
            ahead[1, kappa, jhi, :, :, jhi, 1, kappa] = cos
    ahead = ahead.reshape(128, 128)
    return bf16_table(ahead), bf16_table(ahead.T / IMAGE)


@functools.lru_cache(None)
def row_forward_tables():
    pos = np.arange(128)
    cos, sin = turn(np.arange(16)[:, None] * pos, 2048)
    twiddle = np.concatenate([cos, sin]).astype(np.float32)
    cos, sin = turn(pos[:, None] * np.arange(128), 128)
    return twiddle, bf16_table(np.concatenate([cos, sin], 1))


@functools.lru_cache(None)
def row_inverse_tables(window, lead):
    pos = (16 * np.arange(8)[:, None] + np.arange(window)[None, :] - lead).reshape(-1)
    cos, sin = turn(np.arange(16)[:, None] * pos, 2048)
    twiddle = np.concatenate([cos, sin]).astype(np.float32)
    cos, sin = turn(np.arange(128)[:, None] * pos, 128)
    return twiddle, bf16_table(np.concatenate([cos, sin], 1))


@functools.lru_cache(None)
def sum_tables():
    spread = np.zeros((128, 10, 64))
    share = np.zeros((128, 10, 32))
    gather = np.zeros((16, 128, 10))
    collect = np.zeros((32, 128, 10))
    for d in range(128):
        spread[d, 8, d % 32] = 1.0
        spread[d, 9, 32 + d % 32] = 1.0
    share[:, 8, 0] = 1.0
    share[:, 9, 16] = 1.0
    gather[:, :, 8:] = 1.0
    for c in range(32):
        collect[c, c, 8:] = 1.0
    return (
        bf16_table(spread.reshape(1280, 64)),
        bf16_table(gather.reshape(16, 1280)),
        bf16_table(share.reshape(1280, 32)),
        bf16_table(collect.reshape(32, 1280)),
    )


@functools.lru_cache(None)
def weight_tables():
    first = np.zeros((4, 4, 256))
    second = np.zeros((3, 2, 128))
    back = np.zeros((3, 4, 192))
    rows = np.full((8, 256), 99)
    fold = np.zeros((3, 384, 128), np.float32)
    for q in range(3):
        for i in range(4):
            at = 128 * (i // 2) + 20 * (3 * (i % 2) + q)
            rows[:, at : at + 20] = np.arange(20)
            first[q, i, at : at + 20] = 1.0
            back[q, i, q * 64 + i * 16 : q * 64 + i * 16 + 16] = 1.0
            for p in range(3):
                fold[p, at : at + 20, (p * 3 + q) * 4 + i] = 1.0
        for o in range(2):
            at = 20 * (3 * o + q)
            second[q, o, at : at + 20] = 1.0
            for e in range(3):
                to = 36 + ((2 - e) * 3 + 2 - q) * 2 + o
                fold[e, 256 + at : 276 + at, to] = 1.0
    rows[:, 120] = -1
    for i in range(3):
        first[3, i, 120 + i] = 1.0
    fold[0, 120, 54] = 1.0
    band = np.zeros((4, 4, 640), np.float32)
    band[:, :, 0:256] = first
    band[:3, :2, 256:384] = second
    band[:3, :, 384:576] = back
    return (
        band,
        rows.astype(np.int32),
        bf16_table(fold),
    )


def columns_ahead(z, twiddle_ref, table_ref):
    root = float(np.sqrt(0.5))
    s04, d04 = z[0] + z[4], z[0] - z[4]
    s26, d26 = z[2] + z[6], z[2] - z[6]
    s15, d15 = z[1] + z[5], z[1] - z[5]
    s37, d37 = z[3] + z[7], z[3] - z[7]
    low, high = root * (d15 - d37), root * (d15 + d37)
    real = [None] * 8
    imag = [None] * 8
    even, odd = s04 + s26, s15 + s37
    real[0], real[4] = even + odd, even - odd
    real[2], imag[2] = s04 - s26, s37 - s15
    real[1], imag[1] = d04 + low, -d26 - high
    real[3], imag[3] = d04 - low, d26 - high
    for j in (1, 2, 3):
        real[8 - j], imag[8 - j] = real[j], -imag[j]
    groups = []
    for j in range(8):
        cos, sin = twiddle_ref[j : j + 1, :], twiddle_ref[8 + j : 9 + j, :]
        if imag[j] is None:
            pieces = [real[j] * cos, -real[j] * sin]
        else:
            pieces = [real[j] * cos + imag[j] * sin, imag[j] * cos - real[j] * sin]
        groups.append(jnp.concatenate(pieces, axis=1).astype(BF16))
    values = lax.dot_general(
        table_ref[...], jnp.concatenate(groups, axis=0), NT, preferred_element_type=F32
    )
    low, high = (values[:, at : at + 128].reshape(64, 8, 128) for at in (0, 128))
    sub = lax.broadcasted_iota(jnp.int32, (64, 8, 128), 1)
    return (
        jnp.where(sub < 4, low, pltpu.roll(high, 4, 1)),
        jnp.where(sub < 4, pltpu.roll(low, 4, 1), high),
    )


def regroup(even, odd):
    sub = lax.broadcasted_iota(jnp.int32, even.shape, 1)
    shape = (512, even.shape[2])
    first = jnp.where(sub < 4, even, pltpu.roll(odd, 4, 1))
    second = jnp.where(sub < 4, pltpu.roll(even, 4, 1), odd)
    return jnp.concatenate([first.reshape(shape), second.reshape(shape)], 1).astype(BF16)


def spaced(chunks):
    gap = jnp.zeros((chunks[0].shape[0], 2, 128), F32)
    pieces = []
    for value in chunks:
        pieces += [value, gap]
    return jnp.concatenate(pieces, 1)


def unspaced(rows):
    rows = rows.astype(F32).reshape(32, 40, 128)
    return [rows[:, 10 * j : 10 * j + 8] for j in range(4)]


def columns_back(rows_of, twiddle_ref):
    real = [None] * 8
    imag = [None] * 8
    for j in range(8):
        rows = rows_of(j)
        re, im = rows[:, :256], rows[:, 256:]
        cos, sin = twiddle_ref[j : j + 1, :], twiddle_ref[8 + j : 9 + j, :]
        real[j] = re * cos - im * sin
        imag[j] = re * sin + im * cos
    fold_re = [real[0]] + [real[j] + real[8 - j] for j in (1, 2, 3)] + [real[4]]
    fold_im = [None] + [imag[j] - imag[8 - j] for j in (1, 2, 3)]
    scale = 1.0 / IMAGE
    root = float(np.sqrt(0.5)) * scale
    base_even = (fold_re[0] + fold_re[4]) * scale
    base_odd = (fold_re[0] - fold_re[4]) * scale
    re2, im2 = fold_re[2] * scale, fold_im[2] * scale
    sum_re, dif_re = fold_re[1] + fold_re[3], fold_re[1] - fold_re[3]
    sum_im, dif_im = fold_im[1] + fold_im[3], fold_im[1] - fold_im[3]
    cross = root * (dif_re - sum_im), root * (dif_re + sum_im)
    return [
        base_even + re2 + sum_re * scale,
        base_odd - im2 + cross[0],
        base_even - re2 - dif_im * scale,
        base_odd + im2 - cross[1],
        base_even + re2 - sum_re * scale,
        base_odd - im2 - cross[0],
        base_even - re2 + dif_im * scale,
        base_odd + im2 + cross[1],
    ]


def swap_blocks(arrays, size):
    arrays = list(arrays)
    count = 128 // size
    lane = lax.broadcasted_iota(jnp.int32, arrays[0].shape, 1)
    step = count // 2
    while step:
        low = (lane & (step * size)) == 0
        for i in range(count):
            if not i & step:
                one, two = arrays[i], arrays[i + step]
                arrays[i] = jnp.where(low, one, pltpu.roll(two, step * size, 1))
                arrays[i + step] = jnp.where(low, pltpu.roll(one, 128 - step * size, 1), two)
        step //= 2
    return arrays


def halves(values):
    high = values.astype(BF16)
    return high, (values - high.astype(F32)).astype(BF16)


def cells_body(estimate_ref, dirty_ref, cot_ref, out_ref):
    sources = (estimate_ref, dirty_ref, cot_ref)
    planes = [sources[i // 2][i % 2].astype(F32) for i in range(6)]
    gap = jnp.zeros((2, 256), F32)
    for c in range(8):
        pieces = []
        for i in range(6):
            out_ref[c, 16 * i : 16 * i + 16] = sources[i // 2][i % 2, 16 * c : 16 * c + 16]
            pieces.append(planes[i][16 * c - 2 : 16 * c] if c > 0 else gap)
            pieces.append(planes[i][16 * c + 16 : 16 * c + 18] if c < 7 else gap)
        pieces.append(jnp.zeros((8, 256), F32))
        out_ref[c, 96:128] = jnp.concatenate(pieces, 0).astype(BF16)


def ahead_body(strip_ref, twiddle_ref, table_ref, out_ref):
    z = [strip_ref[c, 0:32].astype(F32) for c in range(8)]
    even, odd = columns_ahead(z, twiddle_ref, table_ref)
    out_ref[...] = jnp.stack([even, odd], 1).reshape(1024, 128).astype(BF16)


def middle_body(window, summing, *refs):
    in_ref, spectra_ref, ahead_ref, back_ref, row_ref, back_row_ref, tw_ref, back_tw_ref = refs[:8]
    out_ref = refs[-1]
    chunks = in_ref[...]
    if summing:
        fours = [part.reshape(16, 2, 8, 128) for part in unspaced(chunks)]
        rows = [fours[c % 4][:, c // 4].reshape(128, 128) for c in range(8)]
    else:
        rows = chunks.astype(F32).reshape(16, 8, 8, 128)
        rows = [rows[:, c].reshape(128, 128) for c in range(8)]
    rows = jnp.concatenate(rows, 1).astype(BF16)
    first = jnp.dot(ahead_ref[...], rows, preferred_element_type=F32)
    per_m = swap_blocks([first[:, 128 * c : 128 * c + 128] for c in range(8)], 16)
    cos, sin = tw_ref[0:16, :], tw_ref[16:32, :]
    rows = []
    for m in range(8):
        real = per_m[m][:64].reshape(4, 16, 128)
        imag = per_m[m][64:].reshape(4, 16, 128)
        rows.append((real * cos + imag * sin).astype(BF16).reshape(64, 128))
        rows.append((imag * cos - real * sin).astype(BF16).reshape(64, 128))
    second = jnp.dot(jnp.concatenate(rows, 0), row_ref[...], preferred_element_type=F32)
    rows = []
    for jlo in range(4):
        full_re, full_im = [], []
        for plane in range(2):
            m = 2 * jlo + plane
            part = second[128 * m : 128 * m + 128]
            full_re.append(part[:64, :128] + part[64:, 128:])
            full_im.append(part[64:, :128] - part[:64, 128:])
        weights = [
            spectra_ref[t].reshape(4, 4, 16, 128)[:, jlo].reshape(64, 128) for t in range(3)
        ]
        for plane in range(2):
            for part in (full_re, full_im):
                mixed = weights[plane] * part[0] + weights[plane + 1] * part[1]
                rows.append(mixed.astype(BF16))
    third = jnp.dot(jnp.concatenate(rows, 0), back_row_ref[...], preferred_element_type=F32)
    half = 8 * window
    cos, sin = back_tw_ref[0:16, :], back_tw_ref[16:32, :]
    per_m = []
    for m in range(8):
        part = third[128 * m : 128 * m + 128]
        real = (part[:64, :half] - part[64:, half:]).reshape(4, 16, half)
        imag = (part[64:, :half] + part[:64, half:]).reshape(4, 16, half)
        per_m.append(
            jnp.concatenate(
                [
                    (real * cos - imag * sin).reshape(64, half),
                    (real * sin + imag * cos).reshape(64, half),
                ],
                0,
            )
        )
    count = 128 // window
    tiles = 8 // count
    per_c = [[None] * tiles for _ in range(8)]
    for m_hi in range(tiles):
        for c_hi in range(tiles):
            cols = slice(128 * c_hi, 128 * c_hi + 128)
            group = [per_m[m_hi * count + i][:, cols] for i in range(count)]
            for i, value in enumerate(swap_blocks(group, window)):
                per_c[c_hi * count + i][m_hi] = value
    rows = jnp.concatenate([tile for v in per_c for tile in v], 1).astype(BF16)
    out = jnp.dot(back_ref[...], rows, preferred_element_type=F32)
    out = [out[:, half * c : half * c + half].reshape(16, 8, half) for c in range(8)]
    if summing:
        gather_ref, share_ref = refs[8:10]
        total = jnp.dot(gather_ref[...], chunks, preferred_element_type=F32)
        out = jnp.stack([spaced(out[:4]), spaced(out[4:])], 1).reshape(1280, 128)
        out = out + jnp.dot(
            share_ref[...], jnp.concatenate(halves(total), 0), preferred_element_type=F32
        )
    else:
        out = jnp.stack(out, 1).reshape(1024, half)
    out_ref[...] = out.astype(BF16)


def shifted(value, q):
    if q == 1:
        return value
    lane = lax.broadcasted_iota(jnp.int32, value.shape, 1)
    if q == 0:
        return jnp.where(lane == 0, 0.0, pltpu.roll(value, 1, 1))
    return jnp.where(lane == IMAGE - 1, 0.0, pltpu.roll(value, IMAGE - 1, 1))


def banded(weights, window_row):
    rows = []
    for r in range(GRAD_ROWS):
        total = jnp.zeros(weights[0].shape, F32)
        for p in range(3):
            total = total + jnp.where(window_row == r + p, weights[p], 0.0)
        rows.append(total)
    return jnp.concatenate(rows, 0)


def prepare(
    place,
    strip_ref,
    beyond_ref,
    w_first_ref,
    w_second_ref,
    bias_ref,
    band_ref,
    rows_ref,
    features_ref,
    cot_ref,
    dirty_ref,
    weights_ref,
    tall_ref,
    stack_ref,
):
    row = lax.broadcasted_iota(jnp.int32, (128, IMAGE), 0)
    tall_ref[...] = jnp.zeros_like(tall_ref)
    rims = [strip_ref[c, 96:128].astype(F32) for c in range(8)]
    opens = (place & 7) == 0
    closes = (place & 7) == 7
    for i in range(6):
        for c in range(8):
            cols = slice(256 * c, 256 * c + 256)
            beyond = beyond_ref[c, i].astype(F32)
            tall_ref[0:2, cols] = jnp.where(opens, beyond, rims[c][4 * i : 4 * i + 2])
            tall_ref[2:18, cols] = strip_ref[c, 16 * i : 16 * i + 16].astype(F32)
            tall_ref[18:20, cols] = jnp.where(closes, beyond, rims[c][4 * i + 2 : 4 * i + 4])
        value = tall_ref[...]
        if i in (2, 3):
            dirty_ref[i - 2] = value
        else:
            for q in range(3):
                at = 20 * (3 * (i % 2) + q)
                stack_ref[at : at + 20, :] = shifted(value, q)[0:20]
            if i == 1:
                out = jnp.where(row < 120, stack_ref[...], jnp.where(row < 123, 1.0, 0.0))
                features_ref[0:128, :] = out.astype(BF16)
            if i == 5:
                cot_ref[...] = jnp.where(row < 120, stack_ref[...], 0.0).astype(BF16)
    rows = rows_ref[0:1, :]

    def spread(weights, table):
        return lax.dot_general(weights, table, TN, preferred_element_type=F32)

    def parts_of(source_ref, lanes):
        return [
            sum(spread(source_ref[p, q].astype(F32), band_ref[q][:, lanes]) for q in range(3))
            for p in range(3)
        ]

    bias = bias_ref[...]
    high = bias.astype(BF16).astype(F32)
    middle = (bias - high).astype(BF16).astype(F32)
    pieces = jnp.concatenate([high, middle, bias - high - middle, jnp.zeros_like(bias)], 0)
    offset = spread(pieces, band_ref[3][:, 0:256])
    first = banded(parts_of(w_first_ref, slice(0, 256)), rows)
    first = first + jnp.concatenate([offset] * GRAD_ROWS, 0)
    weights_ref[:, 0:256] = (0.5 * first).astype(BF16)
    parts = [
        sum(
            spread(w_second_ref[2 - e, 2 - q].astype(F32), band_ref[q][0:2, 256:384])
            for q in range(3)
        )
        for e in range(3)
    ]
    weights_ref[:, 256:384] = (0.5 * banded(parts, rows[:, :128])).astype(BF16)
    parts = parts_of(w_first_ref, slice(384, 576))
    rows = lax.broadcasted_iota(jnp.int32, (1, 192), 1) & 15
    parts = [parts[2 - p] for p in range(3)]
    weights_ref[:, 384:576] = banded_back(parts, rows).astype(BF16)


def banded_back(parts, rows):
    blocks = []
    for r in range(GRAD_ROWS):
        total = jnp.zeros(parts[0].shape, F32)
        for k in range(3):
            total = total + jnp.where(rows == r - k, parts[k], 0.0)
        blocks.append(total)
    return jnp.concatenate(blocks, 0)


def network_body(
    place_ref,
    in_ref,
    strip_ref,
    beyond_ref,
    w_first_ref,
    w_second_ref,
    bias_ref,
    band_ref,
    twiddle_ref,
    inverse_ref,
    forward_ref,
    spread_ref,
    rows_ref,
    fold_ref,
    base_ref,
    out_ref,
    stack_ref,
    features_ref,
    spread_grad_ref,
    acc_first_ref,
    acc_second_ref,
    back_ref,
    cot_ref,
    dirty_ref,
    weights_ref,
    tall_ref,
):
    place = place_ref[0]
    prepare(
        place,
        strip_ref,
        beyond_ref,
        w_first_ref,
        w_second_ref,
        bias_ref,
        band_ref,
        rows_ref,
        features_ref,
        cot_ref,
        dirty_ref,
        weights_ref,
        tall_ref,
        stack_ref,
    )
    chunks = in_ref[...].astype(F32).reshape(64, 2, 8, 256)
    values = lax.dot_general(
        regroup(chunks[:, 0], chunks[:, 1]), inverse_ref[...], TN, preferred_element_type=F32
    )
    row = lax.broadcasted_iota(jnp.int32, (HOLD, IMAGE), 0)
    inside = ((row >= 2) | (place > 0)) & ((row < 18) | (place < DEVS - 1))
    for plane in range(2):
        blocks = columns_back(
            lambda j: values[64 * j + 32 * plane : 64 * j + 32 * plane + HOLD], twiddle_ref
        )
        blurred = jnp.concatenate(blocks, 1).astype(BF16).astype(F32)
        residual = dirty_ref[plane] - jnp.where(inside, blurred, 0.0)
        residual = residual.astype(BF16).astype(F32)
        for q in range(3):
            at = 20 * (3 * plane + q)
            stack_ref[at : at + 20, :] = shifted(residual, q)[0:20]
    stack_ref[120:128, :] = jnp.zeros((8, IMAGE), F32)
    features_ref[128:256, :] = stack_ref[...].astype(BF16)
    back_ref[...] = weights_ref[:, 384:576].astype(F32).T.astype(BF16)
    acc_first_ref[...] = jnp.zeros_like(acc_first_ref)
    acc_second_ref[...] = jnp.zeros_like(acc_second_ref)
    top = jnp.where(place > 0, 1.0, 0.0)
    bottom = jnp.where(place < DEVS - 1, 1.0, 0.0)

    def block(step, carry):
        cols = pl.ds(pl.multiple_of(step * 1024, 1024), 1024)
        features = features_ref[:, cols]
        cots = cot_ref[:, cols]
        preact = jnp.dot(weights_ref[:, 0:256], features, preferred_element_type=F32)
        back = jnp.dot(weights_ref[:, 256:384], cots, preferred_element_type=F32)
        bend = jnp.tanh(preact)
        gate = 1.0 + bend
        hidden = preact * gate
        grad_pre = back * gate * (1.0 + preact * (1.0 - bend))
        grad_pre = jnp.concatenate(
            [grad_pre[0:32] * top, grad_pre[32:544], grad_pre[544:576] * bottom], 0
        ).astype(BF16)
        spread_grad_ref[:, cols] = jnp.dot(back_ref[...], grad_pre, preferred_element_type=F32)
        acc_first_ref[...] += lax.dot_general(
            grad_pre[32:544], features, NT, preferred_element_type=F32
        )
        acc_second_ref[...] += lax.dot_general(
            hidden[32:544].astype(BF16), cots, NT, preferred_element_type=F32
        )
        return carry

    lax.fori_loop(0, 2, block, 0, unroll=True)

    cot_sums = []
    z = [[None, None] for _ in range(8)]
    for i in range(4):
        rows = [spread_grad_ref[64 * q + 16 * i : 64 * q + 16 * i + 16, :] for q in range(3)]
        total = shifted(rows[0], 2) + rows[1] + shifted(rows[2], 0)
        for c in range(8):
            part = total[:, 256 * c : 256 * c + 256]
            if i < 2:
                base_ref[c, i] = part + strip_ref[c, 64 + 16 * i : 80 + 16 * i].astype(F32)
            else:
                z[c][i - 2] = part.astype(BF16).astype(F32)
    for i in range(2):
        total = strip_ref[0, 64 + 16 * i : 80 + 16 * i].astype(F32)
        for c in range(1, 8):
            total = total + strip_ref[c, 64 + 16 * i : 80 + 16 * i].astype(F32)
        cot_sums.append(total.sum(axis=0, keepdims=True).sum(axis=1, keepdims=True))

    rows = rows_ref[0:1, :]
    parts = [jnp.zeros((HIDDEN, 384), F32) for _ in range(3)]
    for r in range(1, 17):
        of_first = acc_first_ref[32 * r - 32 : 32 * r, :]
        of_second = acc_second_ref[32 * r - 32 : 32 * r, :]
        for p in range(3):
            keep = (rows == r + p) | (rows == -1)
            parts[p] = parts[p] + jnp.concatenate(
                [
                    jnp.where(keep, of_first, 0.0),
                    jnp.where(rows[:, :128] == r + p, of_second, 0.0),
                ],
                1,
            )
    sums = jnp.zeros((HIDDEN, 128), F32)
    for p in range(3):
        sums = sums + jnp.dot(
            parts[p],
            fold_ref[p].astype(F32),
            precision=lax.Precision.HIGHEST,
            preferred_element_type=F32,
        )
    at = lax.broadcasted_iota(jnp.int32, (HIDDEN, 128), 1)
    of = lax.broadcasted_iota(jnp.int32, (HIDDEN, 128), 0)
    for i in range(2):
        sums = jnp.where((at == 55) & (of == i), cot_sums[i], sums)

    even, odd = columns_ahead([jnp.concatenate(v, 0) for v in z], twiddle_ref, forward_ref)
    even, odd = even.reshape(32, 2, 8, 128), odd.reshape(32, 2, 8, 128)
    out = spaced([even[:, 0], odd[:, 0], even[:, 1], odd[:, 1]]).reshape(1280, 128)
    out = out + jnp.dot(
        spread_ref[...], jnp.concatenate(halves(sums), 0), preferred_element_type=F32
    )
    out_ref[...] = out.astype(BF16)


def finish_body(
    in_ref,
    base_ref,
    twiddle_ref,
    inverse_ref,
    collect_ref,
    out_ref,
    first_ref,
    first_bias_ref,
    second_ref,
    second_bias_ref,
):
    chunks = in_ref[...]
    sums = jnp.dot(collect_ref[...], chunks, preferred_element_type=F32) * (1.0 / IMAGE)
    sums = sums.T
    for p in range(3):
        for q in range(3):
            at = 3 * p + q
            first_ref[p, q] = sums[4 * at : 4 * at + 4]
            second_ref[p, q] = sums[36 + 2 * at : 38 + 2 * at]
    first_bias_ref[...] = sums[54:55]
    second_bias_ref[...] = sums[55:56, 0:2]
    fours = unspaced(chunks)
    even = jnp.stack([fours[0], fours[2]], 1).reshape(64, 8, 128)
    odd = jnp.stack([fours[1], fours[3]], 1).reshape(64, 8, 128)
    values = lax.dot_general(
        regroup(even, odd), inverse_ref[...], TN, preferred_element_type=F32
    )
    blocks = columns_back(lambda j: values[32 * j : 32 * j + 32], twiddle_ref)
    for c in range(8):
        blurred = blocks[c].astype(BF16).astype(F32).reshape(2, STRIP, 256)
        out_ref[c] = base_ref[c] - blurred


def call(body, outs, *args, scratch=(), scalars=0, after=(), cost=2, vmem=VM):
    whole = pl.BlockSpec(memory_space=pltpu.VMEM)
    return pl.pallas_call(
        body,
        out_shape=outs,
        in_specs=[pl.BlockSpec(memory_space=pltpu.SMEM)] * scalars
        + [whole] * (len(args) - scalars)
        + [pl.BlockSpec(memory_space=pl.ANY)] * len(after),
        out_specs=jax.tree.map(lambda _: whole, outs),
        scratch_shapes=list(scratch),
        compiler_params=pltpu.CompilerParams(vmem_limit_bytes=vmem * 1024 * 1024),
        cost_estimate=pl.CostEstimate(
            flops=cost * 10**9, bytes_accessed=cost * 10**6, transcendentals=0
        ),
    )(*args, *after)


def like(*shape, dtype=BF16):
    return jax.ShapeDtypeStruct(shape, dtype)


def exchange(chunks, per):
    width = chunks.shape[-1]
    rows = 8 if per == 8 else 2
    moved = lax.all_to_all(chunks.reshape(DEVS * per // rows, rows, width), RC, 0, 0, tiled=True)
    return moved.reshape(DEVS * per, width)


def middle(chunks, spectra, window, lead, per, after=()):
    ahead, back = row_block_tables()
    twiddle, row_table = row_forward_tables()
    back_twiddle, back_row = row_inverse_tables(window, lead)
    extra = sum_tables()[1:3] if per == 10 else ()
    return call(
        functools.partial(middle_body, window, per == 10),
        like(DEVS * per, 8 * window),
        chunks,
        spectra,
        ahead,
        back,
        row_table,
        back_row,
        twiddle,
        back_twiddle,
        *extra,
        after=after,
    )


def shards(estimate, dirty_image, psf_spectra, w_first, b_first, w_second, cotangent):
    cells = call(
        cells_body, like(8, 128, 256), estimate, dirty_image, cotangent, vmem=60
    )
    strip = lax.all_to_all(cells, "col", 0, 0, tiled=True)
    spec = call(
        ahead_body, like(1024, 128), strip, column_twiddle(), column_tables()[0]
    )
    spec = exchange(spec, 8)
    rows = strip[:, :96].reshape(8, 6, STRIP, 256)
    edge = jnp.where(lax.axis_index("col") == 7, rows[:, :, -2:], rows[:, :, :2])
    seams = [(8 * r + 7, 8 * r + 8) for r in range(15)]
    beyond = lax.ppermute(edge, RC, seams + [(b, a) for a, b in seams])
    band, row_of, fold = weight_tables()
    mixed = exchange(middle(spec, psf_spectra, 32, 2, 8, ()), 8)
    place = (lax.axis_index("row") * 8 + lax.axis_index("col")).astype(jnp.int32).reshape(1)
    base, spec = call(
        network_body,
        (like(8, 2, STRIP, 256, dtype=F32), like(1280, 128)),
        place,
        mixed,
        strip,
        beyond,
        w_first.transpose(2, 3, 1, 0),
        w_second.transpose(2, 3, 0, 1),
        b_first.reshape(1, 32),
        band,
        column_twiddle(),
        column_tables()[1],
        column_tables()[0],
        sum_tables()[0],
        row_of,
        fold,
        scratch=[
            pltpu.VMEM((128, IMAGE), F32),
            pltpu.VMEM((256, IMAGE), BF16),
            pltpu.VMEM((192, IMAGE), F32),
            pltpu.VMEM((512, 256), F32),
            pltpu.VMEM((512, 128), F32),
            pltpu.VMEM((192, 576), BF16),
            pltpu.VMEM((128, IMAGE), BF16),
            pltpu.VMEM((2, HOLD, IMAGE), F32),
            pltpu.VMEM((576, 576), BF16),
            pltpu.VMEM((HOLD, IMAGE), F32),
        ],
        scalars=1,
        cost=8,
    )
    mixed = exchange(middle(exchange(spec, 10), psf_spectra, 16, 0, 10), 10)
    image, grad_first, first_bias, grad_second, second_bias = call(
        finish_body,
        (
            like(8, 2, STRIP, 256, dtype=F32),
            like(3, 3, 4, 32, dtype=F32),
            like(1, 32, dtype=F32),
            like(3, 3, 2, 32, dtype=F32),
            like(1, 2, dtype=F32),
        ),
        mixed,
        base,
        column_twiddle(),
        column_tables()[1],
        sum_tables()[3],
    )
    image = lax.all_to_all(image, "col", 0, 0, tiled=True)
    grad_image = image.transpose(1, 0, 2, 3).reshape(2, 128, 256)
    return (
        grad_image,
        grad_first.transpose(3, 2, 0, 1),
        first_bias.reshape(32),
        grad_second.transpose(2, 3, 0, 1),
        second_bias.reshape(2),
    )


def solution(mesh):
    return jax.shard_map(
        shards,
        mesh=mesh,
        in_specs=(
            P(None, "row", "col"),
            P(None, "row", "col"),
            P(None, ("row", "col"), None, None),
            P(),
            P(),
            P(),
            P(None, "row", "col"),
        ),
        out_specs=(P(None, "row", "col"), P(), P(), P(), P()),
        check_vma=False,
    )
```

```python
import functools

import jax
import jax.numpy as jnp
import numpy as np
from jax import lax
from jax.experimental import pallas as pl
from jax.experimental.pallas import tpu as pltpu
from jax.sharding import PartitionSpec as P

IMAGE = 2048
DEVS = 128
VM = 28
STRIP = 16
REACH = 20
HOLD = 24
GRAD_ROWS = 18
HIDDEN = 32
RC = ("row", "col")
F32 = jnp.float32
BF16 = jnp.bfloat16
NT = (((1,), (1,)), ((), ()))
TN = (((0,), (0,)), ((), ()))


def turn(product, period):
    angle = 2.0 * np.pi * (product % period) / period
    return np.cos(angle), np.sin(angle)


def bf16_table(values):
    return np.asarray(values, np.float32).astype(jnp.bfloat16)


@functools.lru_cache(None)
def column_twiddle():
    cos, sin = turn(np.arange(8)[:, None] * np.arange(256)[None, :], 2048)
    return np.concatenate([cos, sin]).astype(np.float32)


@functools.lru_cache(None)
def column_tables():
    freq = 2 * np.arange(128)[:, None] + np.arange(2)[None, :]
    cos, sin = turn(freq[:, :, None] * np.arange(256), 256)
    ahead = np.zeros((128, 2, 2, 2, 256))
    ahead[:, 0, :, 0] = cos
    ahead[:, 0, :, 1] = sin
    ahead[:, 1, :, 0] = -sin
    ahead[:, 1, :, 1] = cos
    back = np.zeros((128, 2, 2, 2, 256))
    back[:, 0, :, 0] = cos
    back[:, 1, :, 0] = -sin
    back[:, 0, :, 1] = sin
    back[:, 1, :, 1] = cos
    return bf16_table(ahead.reshape(512, 512)), bf16_table(back.reshape(512, 512))


@functools.lru_cache(None)
def row_block_tables():
    cos, sin = turn(np.arange(16)[:, None] * np.arange(16), 16)
    ahead = np.zeros((2, 2, 2, 16, 16, 2, 2, 2))
    for kappa in range(2):
        for jhi in range(2):
            ahead[0, kappa, jhi, :, :, jhi, 0, kappa] = cos
            ahead[0, kappa, jhi, :, :, jhi, 1, kappa] = sin
            ahead[1, kappa, jhi, :, :, jhi, 0, kappa] = -sin
            ahead[1, kappa, jhi, :, :, jhi, 1, kappa] = cos
    ahead = ahead.reshape(128, 128)
    return bf16_table(ahead), bf16_table(ahead.T / IMAGE)


@functools.lru_cache(None)
def row_forward_tables():
    pos = np.arange(128)
    cos, sin = turn(np.arange(16)[:, None] * pos, 2048)
    twiddle = np.concatenate([cos, sin]).astype(np.float32)
    cos, sin = turn(pos[:, None] * np.arange(128), 128)
    return twiddle, bf16_table(np.concatenate([cos, sin], 1))


@functools.lru_cache(None)
def row_inverse_tables(window, lead):
    pos = (16 * np.arange(8)[:, None] + np.arange(window)[None, :] - lead).reshape(-1)
    cos, sin = turn(np.arange(16)[:, None] * pos, 2048)
    twiddle = np.concatenate([cos, sin]).astype(np.float32)
    cos, sin = turn(np.arange(128)[:, None] * pos, 128)
    return twiddle, bf16_table(np.concatenate([cos, sin], 1))


@functools.lru_cache(None)
def sum_tables():
    spread = np.zeros((128, 10, 64))
    share = np.zeros((128, 10, 32))
    gather = np.zeros((16, 128, 10))
    collect = np.zeros((32, 128, 10))
    for d in range(128):
        spread[d, 8, d % 32] = 1.0
        spread[d, 9, 32 + d % 32] = 1.0
    share[:, 8, 0] = 1.0
    share[:, 9, 16] = 1.0
    gather[:, :, 8:] = 1.0
    for c in range(32):
        collect[c, c, 8:] = 1.0
    return (
        bf16_table(spread.reshape(1280, 64)),
        bf16_table(gather.reshape(16, 1280)),
        bf16_table(share.reshape(1280, 32)),
        bf16_table(collect.reshape(32, 1280)),
    )


@functools.lru_cache(None)
def weight_tables():
    first = np.zeros((4, 4, 256))
    second = np.zeros((3, 2, 128))
    back = np.zeros((3, 4, 192))
    rows = np.full((8, 256), 99)
    fold = np.zeros((3, 384, 128), np.float32)
    for q in range(3):
        for i in range(4):
            at = 128 * (i // 2) + 20 * (3 * (i % 2) + q)
            rows[:, at : at + 20] = np.arange(20)
            first[q, i, at : at + 20] = 1.0
            back[q, i, q * 64 + i * 16 : q * 64 + i * 16 + 16] = 1.0
            for p in range(3):
                fold[p, at : at + 20, (p * 3 + q) * 4 + i] = 1.0
        for o in range(2):
            at = 20 * (3 * o + q)
            second[q, o, at : at + 20] = 1.0
            for e in range(3):
                to = 36 + ((2 - e) * 3 + 2 - q) * 2 + o
                fold[e, 256 + at : 276 + at, to] = 1.0
    rows[:, 120] = -1
    for i in range(3):
        first[3, i, 120 + i] = 1.0
    fold[0, 120, 54] = 1.0
    band = np.zeros((4, 4, 640), np.float32)
    band[:, :, 0:256] = first
    band[:3, :2, 256:384] = second
    band[:3, :, 384:576] = back
    return (
        band,
        rows.astype(np.int32),
        bf16_table(fold),
    )


def columns_ahead(z, twiddle_ref, table_ref):
    root = float(np.sqrt(0.5))
    s04, d04 = z[0] + z[4], z[0] - z[4]
    s26, d26 = z[2] + z[6], z[2] - z[6]
    s15, d15 = z[1] + z[5], z[1] - z[5]
    s37, d37 = z[3] + z[7], z[3] - z[7]
    low, high = root * (d15 - d37), root * (d15 + d37)
    real = [None] * 8
    imag = [None] * 8
    even, odd = s04 + s26, s15 + s37
    real[0], real[4] = even + odd, even - odd
    real[2], imag[2] = s04 - s26, s37 - s15
    real[1], imag[1] = d04 + low, -d26 - high
    real[3], imag[3] = d04 - low, d26 - high
    for j in (1, 2, 3):
        real[8 - j], imag[8 - j] = real[j], -imag[j]
    groups = []
    for j in range(8):
        cos, sin = twiddle_ref[j : j + 1, :], twiddle_ref[8 + j : 9 + j, :]
        if imag[j] is None:
            pieces = [real[j] * cos, -real[j] * sin]
        else:
            pieces = [real[j] * cos + imag[j] * sin, imag[j] * cos - real[j] * sin]
        groups.append(jnp.concatenate(pieces, axis=1).astype(BF16))
    values = lax.dot_general(
        table_ref[...], jnp.concatenate(groups, axis=0), NT, preferred_element_type=F32
    )
    low, high = (values[:, at : at + 128].reshape(64, 8, 128) for at in (0, 128))
    sub = lax.broadcasted_iota(jnp.int32, (64, 8, 128), 1)
    return (
        jnp.where(sub < 4, low, pltpu.roll(high, 4, 1)),
        jnp.where(sub < 4, pltpu.roll(low, 4, 1), high),
    )


def regroup(even, odd):
    sub = lax.broadcasted_iota(jnp.int32, even.shape, 1)
    shape = (512, even.shape[2])
    first = jnp.where(sub < 4, even, pltpu.roll(odd, 4, 1))
    second = jnp.where(sub < 4, pltpu.roll(even, 4, 1), odd)
    return jnp.concatenate([first.reshape(shape), second.reshape(shape)], 1).astype(BF16)


def spaced(chunks):
    gap = jnp.zeros((chunks[0].shape[0], 2, 128), F32)
    pieces = []
    for value in chunks:
        pieces += [value, gap]
    return jnp.concatenate(pieces, 1)


def unspaced(rows):
    rows = rows.astype(F32).reshape(32, 40, 128)
    return [rows[:, 10 * j : 10 * j + 8] for j in range(4)]


def columns_back(rows_of, twiddle_ref):
    real = [None] * 8
    imag = [None] * 8
    for j in range(8):
        rows = rows_of(j)
        re, im = rows[:, :256], rows[:, 256:]
        cos, sin = twiddle_ref[j : j + 1, :], twiddle_ref[8 + j : 9 + j, :]
        real[j] = re * cos - im * sin
        imag[j] = re * sin + im * cos
    fold_re = [real[0]] + [real[j] + real[8 - j] for j in (1, 2, 3)] + [real[4]]
    fold_im = [None] + [imag[j] - imag[8 - j] for j in (1, 2, 3)]
    scale = 1.0 / IMAGE
    root = float(np.sqrt(0.5)) * scale
    base_even = (fold_re[0] + fold_re[4]) * scale
    base_odd = (fold_re[0] - fold_re[4]) * scale
    re2, im2 = fold_re[2] * scale, fold_im[2] * scale
    sum_re, dif_re = fold_re[1] + fold_re[3], fold_re[1] - fold_re[3]
    sum_im, dif_im = fold_im[1] + fold_im[3], fold_im[1] - fold_im[3]
    cross = root * (dif_re - sum_im), root * (dif_re + sum_im)
    return [
        base_even + re2 + sum_re * scale,
        base_odd - im2 + cross[0],
        base_even - re2 - dif_im * scale,
        base_odd + im2 - cross[1],
        base_even + re2 - sum_re * scale,
        base_odd - im2 - cross[0],
        base_even - re2 + dif_im * scale,
        base_odd + im2 + cross[1],
    ]


def swap_blocks(arrays, size):
    arrays = list(arrays)
    count = 128 // size
    lane = lax.broadcasted_iota(jnp.int32, arrays[0].shape, 1)
    step = count // 2
    while step:
        low = (lane & (step * size)) == 0
        for i in range(count):
            if not i & step:
                one, two = arrays[i], arrays[i + step]
                arrays[i] = jnp.where(low, one, pltpu.roll(two, step * size, 1))
                arrays[i + step] = jnp.where(low, pltpu.roll(one, 128 - step * size, 1), two)
        step //= 2
    return arrays


def halves(values):
    high = values.astype(BF16)
    return high, (values - high.astype(F32)).astype(BF16)


def cells_body(estimate_ref, dirty_ref, cot_ref, out_ref):
    sources = (estimate_ref, dirty_ref, cot_ref)
    planes = [sources[i // 2][i % 2].astype(F32) for i in range(6)]
    gap = jnp.zeros((2, 256), F32)
    for c in range(8):
        pieces = []
        for i in range(6):
            out_ref[c, 16 * i : 16 * i + 16] = sources[i // 2][i % 2, 16 * c : 16 * c + 16]
            pieces.append(planes[i][16 * c - 2 : 16 * c] if c > 0 else gap)
            pieces.append(planes[i][16 * c + 16 : 16 * c + 18] if c < 7 else gap)
        pieces.append(jnp.zeros((8, 256), F32))
        out_ref[c, 96:128] = jnp.concatenate(pieces, 0).astype(BF16)


def ahead_body(strip_ref, twiddle_ref, table_ref, out_ref):
    z = [strip_ref[c, 0:32].astype(F32) for c in range(8)]
    even, odd = columns_ahead(z, twiddle_ref, table_ref)
    out_ref[...] = jnp.stack([even, odd], 1).reshape(1024, 128).astype(BF16)


def middle_body(window, summing, *refs):
    in_ref, spectra_ref, ahead_ref, back_ref, row_ref, back_row_ref, tw_ref, back_tw_ref = refs[:8]
    out_ref = refs[-1]
    chunks = in_ref[...]
    if summing:
        fours = [part.reshape(16, 2, 8, 128) for part in unspaced(chunks)]
        rows = [fours[c % 4][:, c // 4].reshape(128, 128) for c in range(8)]
    else:
        rows = chunks.astype(F32).reshape(16, 8, 8, 128)
        rows = [rows[:, c].reshape(128, 128) for c in range(8)]
    rows = jnp.concatenate(rows, 1).astype(BF16)
    first = jnp.dot(ahead_ref[...], rows, preferred_element_type=F32)
    per_m = swap_blocks([first[:, 128 * c : 128 * c + 128] for c in range(8)], 16)
    cos, sin = tw_ref[0:16, :], tw_ref[16:32, :]
    rows = []
    for m in range(8):
        real = per_m[m][:64].reshape(4, 16, 128)
        imag = per_m[m][64:].reshape(4, 16, 128)
        rows.append((real * cos + imag * sin).astype(BF16).reshape(64, 128))
        rows.append((imag * cos - real * sin).astype(BF16).reshape(64, 128))
    second = jnp.dot(jnp.concatenate(rows, 0), row_ref[...], preferred_element_type=F32)
    rows = []
    for jlo in range(4):
        full_re, full_im = [], []
        for plane in range(2):
            m = 2 * jlo + plane
            part = second[128 * m : 128 * m + 128]
            full_re.append(part[:64, :128] + part[64:, 128:])
            full_im.append(part[64:, :128] - part[:64, 128:])
        weights = [
            spectra_ref[t].reshape(4, 4, 16, 128)[:, jlo].reshape(64, 128) for t in range(3)
        ]
        for plane in range(2):
            for part in (full_re, full_im):
                mixed = weights[plane] * part[0] + weights[plane + 1] * part[1]
                rows.append(mixed.astype(BF16))
    third = jnp.dot(jnp.concatenate(rows, 0), back_row_ref[...], preferred_element_type=F32)
    half = 8 * window
    cos, sin = back_tw_ref[0:16, :], back_tw_ref[16:32, :]
    per_m = []
    for m in range(8):
        part = third[128 * m : 128 * m + 128]
        real = (part[:64, :half] - part[64:, half:]).reshape(4, 16, half)
        imag = (part[64:, :half] + part[:64, half:]).reshape(4, 16, half)
        per_m.append(
            jnp.concatenate(
                [
                    (real * cos - imag * sin).reshape(64, half),
                    (real * sin + imag * cos).reshape(64, half),
                ],
                0,
            )
        )
    count = 128 // window
    tiles = 8 // count
    per_c = [[None] * tiles for _ in range(8)]
    for m_hi in range(tiles):
        for c_hi in range(tiles):
            cols = slice(128 * c_hi, 128 * c_hi + 128)
            group = [per_m[m_hi * count + i][:, cols] for i in range(count)]
            for i, value in enumerate(swap_blocks(group, window)):
                per_c[c_hi * count + i][m_hi] = value
    rows = jnp.concatenate([tile for v in per_c for tile in v], 1).astype(BF16)
    out = jnp.dot(back_ref[...], rows, preferred_element_type=F32)
    out = [out[:, half * c : half * c + half].reshape(16, 8, half) for c in range(8)]
    if summing:
        gather_ref, share_ref = refs[8:10]
        total = jnp.dot(gather_ref[...], chunks, preferred_element_type=F32)
        out = jnp.stack([spaced(out[:4]), spaced(out[4:])], 1).reshape(1280, 128)
        out = out + jnp.dot(
            share_ref[...], jnp.concatenate(halves(total), 0), preferred_element_type=F32
        )
    else:
        out = jnp.stack(out, 1).reshape(1024, half)
    out_ref[...] = out.astype(BF16)


def shifted(value, q):
    if q == 1:
        return value
    lane = lax.broadcasted_iota(jnp.int32, value.shape, 1)
    if q == 0:
        return jnp.where(lane == 0, 0.0, pltpu.roll(value, 1, 1))
    return jnp.where(lane == IMAGE - 1, 0.0, pltpu.roll(value, IMAGE - 1, 1))


def banded(weights, window_row):
    rows = []
    for r in range(GRAD_ROWS):
        total = jnp.zeros(weights[0].shape, F32)
        for p in range(3):
            total = total + jnp.where(window_row == r + p, weights[p], 0.0)
        rows.append(total)
    return jnp.concatenate(rows, 0)


def prepare(
    place,
    strip_ref,
    beyond_ref,
    w_first_ref,
    w_second_ref,
    bias_ref,
    band_ref,
    rows_ref,
    features_ref,
    cot_ref,
    dirty_ref,
    weights_ref,
    tall_ref,
    stack_ref,
):
    row = lax.broadcasted_iota(jnp.int32, (128, IMAGE), 0)
    tall_ref[...] = jnp.zeros_like(tall_ref)
    rims = [strip_ref[c, 96:128].astype(F32) for c in range(8)]
    opens = (place & 7) == 0
    closes = (place & 7) == 7
    for i in range(6):
        for c in range(8):
            cols = slice(256 * c, 256 * c + 256)
            beyond = beyond_ref[c, i].astype(F32)
            tall_ref[0:2, cols] = jnp.where(opens, beyond, rims[c][4 * i : 4 * i + 2])
            tall_ref[2:18, cols] = strip_ref[c, 16 * i : 16 * i + 16].astype(F32)
            tall_ref[18:20, cols] = jnp.where(closes, beyond, rims[c][4 * i + 2 : 4 * i + 4])
        value = tall_ref[...]
        if i in (2, 3):
            dirty_ref[i - 2] = value
        else:
            for q in range(3):
                at = 20 * (3 * (i % 2) + q)
                stack_ref[at : at + 20, :] = shifted(value, q)[0:20]
            if i == 1:
                out = jnp.where(row < 120, stack_ref[...], jnp.where(row < 123, 1.0, 0.0))
                features_ref[0:128, :] = out.astype(BF16)
            if i == 5:
                cot_ref[...] = jnp.where(row < 120, stack_ref[...], 0.0).astype(BF16)
    rows = rows_ref[0:1, :]

    def spread(weights, table):
        return lax.dot_general(weights, table, TN, preferred_element_type=F32)

    def parts_of(source_ref, lanes):
        return [
            sum(spread(source_ref[p, q].astype(F32), band_ref[q][:, lanes]) for q in range(3))
            for p in range(3)
        ]

    bias = bias_ref[...]
    high = bias.astype(BF16).astype(F32)
    middle = (bias - high).astype(BF16).astype(F32)
    pieces = jnp.concatenate([high, middle, bias - high - middle, jnp.zeros_like(bias)], 0)
    offset = spread(pieces, band_ref[3][:, 0:256])
    first = banded(parts_of(w_first_ref, slice(0, 256)), rows)
    first = first + jnp.concatenate([offset] * GRAD_ROWS, 0)
    weights_ref[:, 0:256] = (0.5 * first).astype(BF16)
    parts = [
        sum(
            spread(w_second_ref[2 - e, 2 - q].astype(F32), band_ref[q][0:2, 256:384])
            for q in range(3)
        )
        for e in range(3)
    ]
    weights_ref[:, 256:384] = (0.5 * banded(parts, rows[:, :128])).astype(BF16)
    parts = parts_of(w_first_ref, slice(384, 576))
    rows = lax.broadcasted_iota(jnp.int32, (1, 192), 1) & 15
    parts = [parts[2 - p] for p in range(3)]
    weights_ref[:, 384:576] = banded_back(parts, rows).astype(BF16)


def banded_back(parts, rows):
    blocks = []
    for r in range(GRAD_ROWS):
        total = jnp.zeros(parts[0].shape, F32)
        for k in range(3):
            total = total + jnp.where(rows == r - k, parts[k], 0.0)
        blocks.append(total)
    return jnp.concatenate(blocks, 0)


def network_body(
    place_ref,
    in_ref,
    strip_ref,
    beyond_ref,
    w_first_ref,
    w_second_ref,
    bias_ref,
    band_ref,
    twiddle_ref,
    inverse_ref,
    forward_ref,
    spread_ref,
    rows_ref,
    fold_ref,
    base_ref,
    out_ref,
    stack_ref,
    features_ref,
    spread_grad_ref,
    acc_first_ref,
    acc_second_ref,
    back_ref,
    cot_ref,
    dirty_ref,
    weights_ref,
    tall_ref,
):
    place = place_ref[0]
    prepare(
        place,
        strip_ref,
        beyond_ref,
        w_first_ref,
        w_second_ref,
        bias_ref,
        band_ref,
        rows_ref,
        features_ref,
        cot_ref,
        dirty_ref,
        weights_ref,
        tall_ref,
        stack_ref,
    )
    chunks = in_ref[...].astype(F32).reshape(64, 2, 8, 256)
    values = lax.dot_general(
        regroup(chunks[:, 0], chunks[:, 1]), inverse_ref[...], TN, preferred_element_type=F32
    )
    row = lax.broadcasted_iota(jnp.int32, (HOLD, IMAGE), 0)
    inside = ((row >= 2) | (place > 0)) & ((row < 18) | (place < DEVS - 1))
    for plane in range(2):
        blocks = columns_back(
            lambda j: values[64 * j + 32 * plane : 64 * j + 32 * plane + HOLD], twiddle_ref
        )
        blurred = jnp.concatenate(blocks, 1).astype(BF16).astype(F32)
        residual = dirty_ref[plane] - jnp.where(inside, blurred, 0.0)
        residual = residual.astype(BF16).astype(F32)
        for q in range(3):
            at = 20 * (3 * plane + q)
            stack_ref[at : at + 20, :] = shifted(residual, q)[0:20]
    stack_ref[120:128, :] = jnp.zeros((8, IMAGE), F32)
    features_ref[128:256, :] = stack_ref[...].astype(BF16)
    back_ref[...] = weights_ref[:, 384:576].astype(F32).T.astype(BF16)
    acc_first_ref[...] = jnp.zeros_like(acc_first_ref)
    acc_second_ref[...] = jnp.zeros_like(acc_second_ref)
    top = jnp.where(place > 0, 1.0, 0.0)
    bottom = jnp.where(place < DEVS - 1, 1.0, 0.0)

    def block(step, carry):
        cols = pl.ds(pl.multiple_of(step * 1024, 1024), 1024)
        features = features_ref[:, cols]
        cots = cot_ref[:, cols]
        preact = jnp.dot(weights_ref[:, 0:256], features, preferred_element_type=F32)
        back = jnp.dot(weights_ref[:, 256:384], cots, preferred_element_type=F32)
        bend = jnp.tanh(preact)
        gate = 1.0 + bend
        hidden = preact * gate
        grad_pre = back * gate * (1.0 + preact * (1.0 - bend))
        grad_pre = jnp.concatenate(
            [grad_pre[0:32] * top, grad_pre[32:544], grad_pre[544:576] * bottom], 0
        ).astype(BF16)
        spread_grad_ref[:, cols] = jnp.dot(back_ref[...], grad_pre, preferred_element_type=F32)
        acc_first_ref[...] += lax.dot_general(
            grad_pre[32:544], features, NT, preferred_element_type=F32
        )
        acc_second_ref[...] += lax.dot_general(
            hidden[32:544].astype(BF16), cots, NT, preferred_element_type=F32
        )
        return carry

    lax.fori_loop(0, 2, block, 0, unroll=True)

    cot_sums = []
    z = [[None, None] for _ in range(8)]
    for i in range(4):
        rows = [spread_grad_ref[64 * q + 16 * i : 64 * q + 16 * i + 16, :] for q in range(3)]
        total = shifted(rows[0], 2) + rows[1] + shifted(rows[2], 0)
        for c in range(8):
            part = total[:, 256 * c : 256 * c + 256]
            if i < 2:
                base_ref[c, i] = part + strip_ref[c, 64 + 16 * i : 80 + 16 * i].astype(F32)
            else:
                z[c][i - 2] = part.astype(BF16).astype(F32)
    for i in range(2):
        total = strip_ref[0, 64 + 16 * i : 80 + 16 * i].astype(F32)
        for c in range(1, 8):
            total = total + strip_ref[c, 64 + 16 * i : 80 + 16 * i].astype(F32)
        cot_sums.append(total.sum(axis=0, keepdims=True).sum(axis=1, keepdims=True))

    rows = rows_ref[0:1, :]
    parts = [jnp.zeros((HIDDEN, 384), F32) for _ in range(3)]
    for r in range(1, 17):
        of_first = acc_first_ref[32 * r - 32 : 32 * r, :]
        of_second = acc_second_ref[32 * r - 32 : 32 * r, :]
        for p in range(3):
            keep = (rows == r + p) | (rows == -1)
            parts[p] = parts[p] + jnp.concatenate(
                [
                    jnp.where(keep, of_first, 0.0),
                    jnp.where(rows[:, :128] == r + p, of_second, 0.0),
                ],
                1,
            )
    sums = jnp.zeros((HIDDEN, 128), F32)
    for p in range(3):
        sums = sums + jnp.dot(
            parts[p],
            fold_ref[p].astype(F32),
            precision=lax.Precision.HIGHEST,
            preferred_element_type=F32,
        )
    at = lax.broadcasted_iota(jnp.int32, (HIDDEN, 128), 1)
    of = lax.broadcasted_iota(jnp.int32, (HIDDEN, 128), 0)
    for i in range(2):
        sums = jnp.where((at == 55) & (of == i), cot_sums[i], sums)

    even, odd = columns_ahead([jnp.concatenate(v, 0) for v in z], twiddle_ref, forward_ref)
    even, odd = even.reshape(32, 2, 8, 128), odd.reshape(32, 2, 8, 128)
    out = spaced([even[:, 0], odd[:, 0], even[:, 1], odd[:, 1]]).reshape(1280, 128)
    out = out + jnp.dot(
        spread_ref[...], jnp.concatenate(halves(sums), 0), preferred_element_type=F32
    )
    out_ref[...] = out.astype(BF16)


def finish_body(
    in_ref,
    base_ref,
    twiddle_ref,
    inverse_ref,
    collect_ref,
    out_ref,
    first_ref,
    first_bias_ref,
    second_ref,
    second_bias_ref,
):
    chunks = in_ref[...]
    sums = jnp.dot(collect_ref[...], chunks, preferred_element_type=F32) * (1.0 / IMAGE)
    sums = sums.T
    for p in range(3):
        for q in range(3):
            at = 3 * p + q
            first_ref[p, q] = sums[4 * at : 4 * at + 4]
            second_ref[p, q] = sums[36 + 2 * at : 38 + 2 * at]
    first_bias_ref[...] = sums[54:55]
    second_bias_ref[...] = sums[55:56, 0:2]
    fours = unspaced(chunks)
    even = jnp.stack([fours[0], fours[2]], 1).reshape(64, 8, 128)
    odd = jnp.stack([fours[1], fours[3]], 1).reshape(64, 8, 128)
    values = lax.dot_general(
        regroup(even, odd), inverse_ref[...], TN, preferred_element_type=F32
    )
    blocks = columns_back(lambda j: values[32 * j : 32 * j + 32], twiddle_ref)
    for c in range(8):
        blurred = blocks[c].astype(BF16).astype(F32).reshape(2, STRIP, 256)
        out_ref[c] = base_ref[c] - blurred


def call(body, outs, *args, scratch=(), scalars=0, after=(), cost=2, vmem=VM):
    whole = pl.BlockSpec(memory_space=pltpu.VMEM)
    return pl.pallas_call(
        body,
        out_shape=outs,
        in_specs=[pl.BlockSpec(memory_space=pltpu.SMEM)] * scalars
        + [whole] * (len(args) - scalars)
        + [pl.BlockSpec(memory_space=pl.ANY)] * len(after),
        out_specs=jax.tree.map(lambda _: whole, outs),
        scratch_shapes=list(scratch),
        compiler_params=pltpu.CompilerParams(vmem_limit_bytes=vmem * 1024 * 1024),
        cost_estimate=pl.CostEstimate(
            flops=cost * 10**9, bytes_accessed=cost * 10**6, transcendentals=0
        ),
    )(*args, *after)


def like(*shape, dtype=BF16):
    return jax.ShapeDtypeStruct(shape, dtype)


def exchange(chunks, per):
    width = chunks.shape[-1]
    rows = 8 if per == 8 else 2
    moved = lax.all_to_all(chunks.reshape(DEVS * per // rows, rows, width), RC, 0, 0, tiled=True)
    return moved.reshape(DEVS * per, width)


def middle(chunks, spectra, window, lead, per, early=()):
    ahead, back = row_block_tables()
    twiddle, row_table = row_forward_tables()
    back_twiddle, back_row = row_inverse_tables(window, lead)
    extra = sum_tables()[1:3] if per == 10 else early
    return call(
        functools.partial(middle_body, window, per == 10),
        like(DEVS * per, 8 * window),
        chunks,
        spectra,
        ahead,
        back,
        row_table,
        back_row,
        twiddle,
        back_twiddle,
        *extra,
    )


def shards(estimate, dirty_image, psf_spectra, w_first, b_first, w_second, cotangent):
    cells = call(
        cells_body, like(8, 128, 256), estimate, dirty_image, cotangent, vmem=60
    )
    strip = lax.all_to_all(cells, "col", 0, 0, tiled=True)
    spec = call(
        ahead_body, like(1024, 128), strip, column_twiddle(), column_tables()[0]
    )
    spec = exchange(spec, 8)
    bias = b_first.reshape(1, 32)
    rows = strip[:, :96].reshape(8, 6, STRIP, 256)
    edge = jnp.where(lax.axis_index("col") == 7, rows[:, :, -2:], rows[:, :, :2])
    seams = [(8 * r + 7, 8 * r + 8) for r in range(15)]
    beyond = lax.ppermute(edge, RC, seams + [(b, a) for a, b in seams])
    band, row_of, fold = weight_tables()
    mixed = exchange(middle(spec, psf_spectra, 32, 2, 8, (bias,)), 8)
    place = (lax.axis_index("row") * 8 + lax.axis_index("col")).astype(jnp.int32).reshape(1)
    base, spec = call(
        network_body,
        (like(8, 2, STRIP, 256, dtype=F32), like(1280, 128)),
        place,
        mixed,
        strip,
        beyond,
        w_first.transpose(2, 3, 1, 0),
        w_second.transpose(2, 3, 0, 1),
        bias,
        band,
        column_twiddle(),
        column_tables()[1],
        column_tables()[0],
        sum_tables()[0],
        row_of,
        fold,
        scratch=[
            pltpu.VMEM((128, IMAGE), F32),
            pltpu.VMEM((256, IMAGE), BF16),
            pltpu.VMEM((192, IMAGE), F32),
            pltpu.VMEM((512, 256), F32),
            pltpu.VMEM((512, 128), F32),
            pltpu.VMEM((192, 576), BF16),
            pltpu.VMEM((128, IMAGE), BF16),
            pltpu.VMEM((2, HOLD, IMAGE), F32),
            pltpu.VMEM((576, 576), BF16),
            pltpu.VMEM((HOLD, IMAGE), F32),
        ],
        scalars=1,
        cost=8,
    )
    mixed = exchange(middle(exchange(spec, 10), psf_spectra, 16, 0, 10), 10)
    image, grad_first, first_bias, grad_second, second_bias = call(
        finish_body,
        (
            like(8, 2, STRIP, 256, dtype=F32),
            like(3, 3, 4, 32, dtype=F32),
            like(1, 32, dtype=F32),
            like(3, 3, 2, 32, dtype=F32),
            like(1, 2, dtype=F32),
        ),
        mixed,
        base,
        column_twiddle(),
        column_tables()[1],
        sum_tables()[3],
    )
    image = lax.all_to_all(image, "col", 0, 0, tiled=True)
    grad_image = image.transpose(1, 0, 2, 3).reshape(2, 128, 256)
    return (
        grad_image,
        grad_first.transpose(3, 2, 0, 1),
        first_bias.reshape(32),
        grad_second.transpose(2, 3, 0, 1),
        second_bias.reshape(2),
    )


def solution(mesh):
    return jax.shard_map(
        shards,
        mesh=mesh,
        in_specs=(
            P(None, "row", "col"),
            P(None, "row", "col"),
            P(None, ("row", "col"), None, None),
            P(),
            P(),
            P(),
            P(None, "row", "col"),
        ),
        out_specs=(P(None, "row", "col"), P(), P(), P(), P()),
        check_vma=False,
    )
```
